128 devices in a mesh: dp: 16 (over x, y_hi, core), tensor: 8 (over z, y_lo).
Axes of the slice: x: 4, y: 4 (y_hi: 2, y_lo: 2; y = y_hi * 2 + y_lo), z: 4, core: 2. Of those that a mesh axis runs over, the one named last changes fastest.
Arguments:
- tokens: bfloat16 [16, 2, 512, 2048], P('dp', None, 'tensor'), may hold values from -6 to 6
- lengths: int32 [16, 2], P('dp'), may hold values from 128 to 512, as said below
- cotangent: bfloat16 [16, 2, 512, 2048], P('dp', None, 'tensor'), may hold values from -6 to 6
- attn_gain: float32 [2048], replicated, may hold values from 0.1 to 1.9
- mixer_in: bfloat16 [2048, 4, 2048], P(None, None, 'tensor'), may hold values from -0.125 to 0.125
- rate_proj: bfloat16 [2048, 2, 16], P(None, None, 'tensor'), may hold values from -0.125 to 0.125
- conv_weight: float32 [3, 4, 2048], P(None, None, 'tensor'), may hold values from -2.5 to 2.5
- decay_rate: float32 [16], P('tensor'), may hold values from 0.05 to 4
- decay_bias: float32 [16], P('tensor'), may hold values from -5 to -2
- out_gain: float32 [128], replicated, may hold values from 0.25 to 1.75
- out_proj: bfloat16 [2048, 2048], P('tensor'), may hold values from -0.25 to 0.25
- ffn_gain: float32 [2048], replicated, may hold values from 0.1 to 1.9
- gate_up: bfloat16 [2048, 2, 5632], P(None, None, 'tensor'), may hold values from -0.125 to 0.125
- down_proj: bfloat16 [5632, 2048], P('tensor'), may hold values from -0.109375 to 0.109375
Outputs:
- layer_out: bfloat16 [16, 2, 512, 2048], P('dp', None, 'tensor')
- d_tokens: bfloat16 [16, 2, 512, 2048], P('dp', None, 'tensor')
- d_attn_gain: float32 [2048], replicated
- d_mixer_in: float32 [2048, 4, 2048], P(None, None, 'tensor')
- d_rate_proj: float32 [2048, 2, 16], P(None, None, 'tensor')
- d_conv_weight: float32 [3, 4, 2048], P(None, None, 'tensor')
- d_decay_rate: float32 [16], P('tensor')
- d_decay_bias: float32 [16], P('tensor')
- d_out_gain: float32 [128], replicated
- d_out_proj: float32 [2048, 2048], P('tensor')
- d_ffn_gain: float32 [2048], replicated
- d_gate_up: float32 [2048, 2, 5632], P(None, None, 'tensor')
- d_down_proj: float32 [5632, 2048], P('tensor')
The draws below stay inside these ranges and needn't reach their ends.
Inputs may be any that keep to these rules, and one draw needn't show every extreme that they name: `lengths`: in each group at least one microbatch has all 512 tokens live; positions at or past a microbatch's length are padding.
All inputs are finite; a program needn't handle non-finite values.
Results may differ from the reference program's by a relative error of at most 0.04.
Values may be sent and summed in bfloat16 or wider, within the bound.
No kernel may reach another device: no remote copies, remote signals or barrier semaphores. Data moves between devices by JAX's collectives and lax.ppermute only.
A program may use at most 320 MiB of HBM per device.

```python
import math
import jax
import jax.numpy as jnp
from jax import lax

D = 2048
H = 16
DK = 128
FF = 5632
CONV = 4
BLOCK = 64
MICRO = 2
CAP = 512
HK = 2048
GROUPS = 16


def draw_lengths(key, part):
    key = jax.random.fold_in(key, 11)
    first, second = jax.random.split(key)
    drawn = jax.random.randint(first, (GROUPS, MICRO), CAP // 4, CAP + 1)
    full_slot = jax.random.randint(second, (GROUPS, 1), 0, MICRO)
    slots = jnp.arange(MICRO)[None, :]
    return jnp.where(slots == full_slot, CAP, drawn).astype(jnp.int32)


def block_levels(own_key, dims, cuts, smallest, largest):
    level, own = 1.0, jax.random.fold_in(own_key, 6)
    for dim, parts in cuts:
        steps = jnp.exp(jax.random.uniform(jax.random.fold_in(own, dim), (parts,), jnp.float32, smallest / len(cuts), largest / len(cuts)))
        level = level * jnp.repeat(steps, dims[dim] // parts).reshape([-1 if axis == dim else 1 for axis in range(len(dims))])
    return level


def centred(rng, shape, width, bound, cuts=(), held_as=jnp.bfloat16):
    values = width * jax.random.normal(rng, shape, jnp.float32)
    if cuts:
        values = values * block_levels(rng, shape, cuts, -0.22, 0.18)
    return jnp.clip(values, -bound, bound).astype(held_as)


def setup_inputs(seed: int = 0) -> dict:
    key_list = jax.random.split(jax.random.key(seed), 15)
    tokens = centred(key_list[0], (GROUPS, MICRO, CAP, D), 1.0, 6.0, ((0, 16), (2, 8)))
    lengths = draw_lengths(jax.random.fold_in(key_list[14], 71), 0)
    cotangent = centred(key_list[2], (GROUPS, MICRO, CAP, D), 1.0, 6.0, ((0, 16), (2, 8)))
    attn_gain = jnp.clip(1.0 + 0.18 * jax.random.normal(key_list[3], (D,), jnp.float32), 0.1, 1.9)
    mixer_in = centred(key_list[4], (D, 4, HK), D ** -0.5, 0.125, ((2, 8),))
    rate_proj = centred(key_list[5], (D, 2, H), D ** -0.5, 0.125, ((2, 8),))
    conv_weight = centred(key_list[6], (3, CONV, HK), 0.5, 2.5, ((2, 8),), jnp.float32)
    decay_rate = jnp.clip(jnp.exp(math.log(4.0) - 4.3820266 * jax.random.uniform(key_list[7], (H,), jnp.float32) ** block_levels(key_list[7], (H,), ((0, 8),), -0.2, 0.2)), 0.05, 4.0)
    decay_bias = jnp.clip(-5.0 + 3.0 * jax.random.uniform(key_list[8], (H,), jnp.float32) ** block_levels(key_list[8], (H,), ((0, 8),), -0.2, 0.2), -5.0, -2.0)
    out_gain = jnp.clip(1.0 + 0.15 * jax.random.normal(key_list[9], (DK,), jnp.float32), 0.25, 1.75)
    out_proj = centred(key_list[10], (HK, D), (HK // 4) ** -0.5, 0.25, ((0, 8),))
    ffn_gain = jnp.clip(1.0 + 0.18 * jax.random.normal(key_list[11], (D,), jnp.float32), 0.1, 1.9)
    gate_up = centred(key_list[12], (D, 2, FF), D ** -0.5, 0.125, ((2, 8),))
    down_proj = centred(key_list[13], (FF, D), (FF // 2) ** -0.5, 0.109375, ((0, 8),))
    return {"tokens": tokens, "lengths": lengths, "cotangent": cotangent, "attn_gain": attn_gain, "mixer_in": mixer_in, "rate_proj": rate_proj, "conv_weight": conv_weight, "decay_rate": decay_rate, "decay_bias": decay_bias, "out_gain": out_gain, "out_proj": out_proj, "ffn_gain": ffn_gain, "gate_up": gate_up, "down_proj": down_proj}


EPS = 1e-06
HIGH = lax.Precision.HIGHEST

@jax.custom_vjp
def low(v):
    return lax.optimization_barrier(v.astype(jnp.bfloat16)).astype(jnp.float32)

@jax.custom_vjp
def low_back(v):
    return v

def low_keep(v):
    return (low(v), None)

def low_pass(kept, grad):
    return (grad,)

def back_keep(v):
    return (v, None)

def back_low(kept, grad):
    return (low(grad),)
low.defvjp(low_keep, low_pass)
low_back.defvjp(back_keep, back_low)

def unit_lower_inverse(lower):
    size = lower.shape[-1]
    if size == 1:
        return jnp.ones_like(lower)
    half = size // 2
    top = unit_lower_inverse(lower[..., :half, :half])
    bottom = unit_lower_inverse(lower[..., half:, half:])
    middle = jnp.einsum('...ij,...jk->...ik', lower[..., half:, :half], top, precision=HIGH)
    corner = -jnp.einsum('...ij,...jk->...ik', bottom, middle, precision=HIGH)
    upper_rows = jnp.concatenate([top, jnp.zeros(top.shape[:-1] + (size - half,), lower.dtype)], axis=-1)
    lower_rows = jnp.concatenate([corner, bottom], axis=-1)
    return jnp.concatenate([upper_rows, lower_rows], axis=-2)

def state_step(carried, pieces):
    queries, solved_keys, solved_values, attend, decay_to, tail_keys, last_decay = pieces
    errors = solved_values - jnp.einsum('htd,hde->hte', solved_keys, carried, precision=HIGH)
    block_out = decay_to[..., None] * jnp.einsum('htd,hde->hte', queries, carried, precision=HIGH)
    block_out = block_out + jnp.einsum('htj,hje->hte', attend, errors, precision=HIGH)
    new_state = last_decay[:, None, None] * carried + jnp.einsum('hjd,hje->hde', tail_keys, errors, precision=HIGH)
    return (new_state, block_out)

def mixer_core(projected, rates, conv_weight, decay_rate, decay_bias, out_gain):
    positions = projected.shape[0]
    head_count = rates.shape[2]
    head_size = projected.shape[2] // head_count
    kernel_taps = conv_weight.shape[1]
    padded = jnp.pad(projected[:, :3, :], ((kernel_taps - 1, 0), (0, 0), (0, 0)))
    conv_out = padded[0:positions] * conv_weight[:, 0, :]
    for offset in range(1, kernel_taps):
        conv_out = conv_out + padded[offset:offset + positions] * conv_weight[:, offset, :]
    conv_out = jax.nn.silu(conv_out).reshape(positions, 3, head_count, head_size)
    queries = conv_out[:, 0]
    key_rows = conv_out[:, 1]
    values = conv_out[:, 2]
    queries = queries * lax.rsqrt(lax.optimization_barrier(jnp.sum(queries * queries, -1, keepdims=True)) + EPS) * head_size ** (-0.5)
    key_rows = key_rows * lax.rsqrt(lax.optimization_barrier(jnp.sum(key_rows * key_rows, -1, keepdims=True)) + EPS)
    update_rate = jax.nn.sigmoid(rates[:, 1])
    logdecay = -decay_rate * jax.nn.softplus(rates[:, 0] + decay_bias)
    blocks = positions // BLOCK

    def arrange(array):
        return array.reshape(blocks, BLOCK, head_count, head_size).transpose(0, 2, 1, 3)

    def arrange_flat(array):
        return array.reshape(blocks, BLOCK, head_count).transpose(0, 2, 1)
    queries = arrange(queries)
    key_rows = arrange(key_rows)
    values = arrange(values)
    update_rate = arrange_flat(update_rate)
    cumul = jnp.cumsum(arrange_flat(logdecay), axis=2)
    row_index = jnp.arange(BLOCK)[:, None]
    col_index = jnp.arange(BLOCK)[None, :]
    lower_mask = row_index >= col_index
    strict_mask = row_index > col_index
    spread = cumul[..., :, None] - cumul[..., None, :]
    decay_ratio = jnp.where(lower_mask, jnp.exp(jnp.where(lower_mask, spread, 0.0)), 0.0)
    keys_keys = jnp.einsum('bhtd,bhjd->bhtj', key_rows, key_rows, precision=HIGH)
    system = jnp.where(strict_mask, decay_ratio * keys_keys * update_rate[..., None, :], 0.0) + jnp.eye(BLOCK, dtype=keys_keys.dtype)
    inverse = unit_lower_inverse(system)
    decay_to = jnp.exp(cumul)
    solved_values = jnp.einsum('bhtj,bhjd->bhtd', inverse, values, precision=HIGH)
    solved_keys = jnp.einsum('bhtj,bhjd->bhtd', inverse, decay_to[..., None] * key_rows, precision=HIGH)
    attend = decay_ratio * jnp.einsum('bhtd,bhjd->bhtj', queries, key_rows, precision=HIGH) * update_rate[..., None, :]
    tail_keys = key_rows * (jnp.exp(cumul[..., -1:] - cumul) * update_rate)[..., None]
    last_decay = jnp.exp(cumul[..., -1])
    start_state = jnp.zeros((head_count, head_size, head_size), projected.dtype)
    _, outputs = lax.scan(jax.checkpoint(state_step), start_state, (queries, solved_keys, solved_values, attend, decay_to, tail_keys, last_decay))
    outputs = outputs.transpose(0, 2, 1, 3).reshape(positions, head_count, head_size)
    norm_scale = lax.rsqrt(lax.optimization_barrier(jnp.mean(outputs * outputs, -1, keepdims=True)) + EPS)
    out_gate = projected[:, 3].reshape(positions, head_count, head_size)
    return (outputs * norm_scale * out_gain * jax.nn.silu(out_gate)).reshape(positions, head_count * head_size)

def layer(source, attn_gain, mixer_in, rate_proj, conv_weight, decay_rate, decay_bias, out_gain, out_proj, ffn_gain, gate_up, down_proj):
    scale_one = lax.rsqrt(lax.optimization_barrier(jnp.mean(source * source, -1, keepdims=True)) + EPS)
    normed_one = low(source * scale_one * attn_gain)
    projected = low_back(jnp.einsum('ld,dkf->lkf', normed_one, mixer_in, precision=HIGH))
    rates = low_back(jnp.einsum('ld,dkh->lkh', normed_one, rate_proj, precision=HIGH))
    mixer_rows = low(mixer_core(projected, rates, conv_weight, decay_rate, decay_bias, out_gain))
    attended = low_back(jnp.dot(mixer_rows, out_proj, precision=HIGH))
    hidden = source + attended
    scale_two = lax.rsqrt(lax.optimization_barrier(jnp.mean(hidden * hidden, -1, keepdims=True)) + EPS)
    normed_two = low(hidden * scale_two * ffn_gain)
    both = low_back(jnp.einsum('ld,dkf->lkf', normed_two, gate_up, precision=HIGH))
    inner = low(jax.nn.silu(both[:, 0]) * both[:, 1])
    branch = low_back(jnp.dot(inner, down_proj, precision=HIGH))
    return hidden + branch

def reference(tokens, lengths, cotangent, attn_gain, mixer_in, rate_proj, conv_weight, decay_rate, decay_bias, out_gain, out_proj, ffn_gain, gate_up, down_proj):
    groups, micro, capacity, model_width = tokens.shape
    places = jnp.arange(capacity, dtype=jnp.int32)
    valid = (places[None, None, :] < lengths[:, :, None]).astype(jnp.float32)[..., None]
    params = tuple((p.astype(jnp.float32) for p in (attn_gain, mixer_in, rate_proj, conv_weight, decay_rate, decay_bias, out_gain, out_proj, ffn_gain, gate_up, down_proj)))
    sequences = tokens.astype(jnp.float32).reshape(groups * micro, capacity, model_width)

    def forward(sequences, *weights):

        def per_sequence(carry, source):
            return (carry, jax.checkpoint(layer)(source, *weights))
        _, outputs = lax.scan(per_sequence, jnp.zeros((), jnp.float32), sequences)
        return outputs
    outputs, backward = jax.vjp(forward, sequences, *params)
    seeds = (cotangent.astype(jnp.float32) * valid).reshape(groups * micro, capacity, model_width)
    grads = backward(seeds)
    layer_out = (outputs.reshape(tokens.shape) * valid).astype(jnp.bfloat16)
    d_tokens = grads[0].reshape(tokens.shape).astype(jnp.bfloat16)
    return (layer_out, d_tokens, grads[1], grads[2], grads[3], grads[4], grads[5], grads[6], grads[7], grads[8], grads[9], grads[10], grads[11])
```

```python
import jax, jax.numpy as jnp
from jax import lax
from jax.experimental import pallas as pl
from jax.experimental.pallas import tpu as pltpu
from jax.sharding import Mesh, PartitionSpec as P

EPS = 1e-06
BLOCK = 64
HS = 128
HEADS = 2
WIDTH = HEADS * HS
F32 = jnp.float32
HIGHEST = lax.Precision.HIGHEST
HIGH = lax.Precision.HIGH
LOW = lax.Precision.DEFAULT
P_INV = HIGH
P_ST = HIGH
P_GR = HIGH


def dot2(a, b, ca, cb, precision):
    return lax.dot_general(a, b, (((ca,), (cb,)), ((), ())), precision=precision, preferred_element_type=F32)


def bdot(a, b, ca, cb, precision):
    if precision == LOW:
        a, b = a.astype(jnp.bfloat16), b.astype(jnp.bfloat16)
    return jnp.stack([dot2(a[i], b[i], ca, cb, precision) for i in range(a.shape[0])])


def split_heads(rows):
    blocks = rows.shape[0] // BLOCK
    return jnp.concatenate(
        [rows[:, h * HS : (h + 1) * HS].reshape(blocks, BLOCK, HS) for h in range(HEADS)], axis=0
    )


def join_heads(stacked):
    blocks = stacked.shape[0] // HEADS
    return jnp.concatenate(
        [stacked[h * blocks : (h + 1) * blocks].reshape(blocks * BLOCK, HS) for h in range(HEADS)], axis=1
    )


def shift_down(rows, steps):
    if steps == 0:
        return rows
    place = lax.broadcasted_iota(jnp.int32, rows.shape, 0)
    return jnp.where(place >= steps, pltpu.roll(rows, steps, 0), 0.0)


def shift_up(rows, steps):
    if steps == 0:
        return rows
    size = rows.shape[0]
    place = lax.broadcasted_iota(jnp.int32, rows.shape, 0)
    return jnp.where(place < size - steps, pltpu.roll(rows, size - steps, 0), 0.0)


def sigmoid(v):
    return 1.0 / (1.0 + jnp.exp(-v))


def softplus(v):
    return jnp.maximum(v, 0.0) + jnp.log1p(jnp.exp(-jnp.abs(v)))


def convolve(rows, taps):
    out = rows * taps[3:4, :]
    for j in range(3):
        out = out + shift_down(rows, 3 - j) * taps[j : j + 1, :]
    return out


def columns(table, blocks, first):
    return jnp.concatenate(
        [table[:, first + h : first + h + 1].reshape(blocks, BLOCK, 1) for h in range(HEADS)], axis=0
    )


def rows_of(turned, first):
    return jnp.concatenate([turned[:, first + h : first + h + 1, :] for h in range(HEADS)], axis=0)


def gates(rates, decay_rate, decay_bias):
    blocks = rates.shape[0] // BLOCK
    soft = softplus(rates + decay_bias)
    logdecay = (-decay_rate * soft).reshape(blocks, BLOCK, 128)
    row = lax.broadcasted_iota(jnp.int32, (BLOCK, BLOCK), 0)
    col = lax.broadcasted_iota(jnp.int32, (BLOCK, BLOCK), 1)
    ones = (row >= col).astype(F32)
    cumul = jnp.stack([dot2(ones, logdecay[n], 1, 0, HIGHEST) for n in range(blocks)])
    update = sigmoid(rates).reshape(blocks, BLOCK, 128)
    lane = lax.broadcasted_iota(jnp.int32, (blocks, BLOCK, 128), 2)
    table = jnp.where(lane < 2, cumul, update)
    turned = jnp.stack([jnp.transpose(table[n], (1, 0)) for n in range(blocks)])
    flat = table.reshape(blocks * BLOCK, 128)
    return soft, columns(flat, blocks, 0), rows_of(turned, 0), columns(flat, blocks, 2), rows_of(turned, 2)


def activate(rows, taps):
    pre = convolve(rows, taps)
    sig = sigmoid(pre)
    return pre, sig, pre * sig


def lower_inverse(strict):
    row = lax.broadcasted_iota(jnp.int32, strict.shape, 1)
    col = lax.broadcasted_iota(jnp.int32, strict.shape, 2)
    size = 1
    inverse = jnp.where(row == col, 1.0, 0.0)
    while size < BLOCK:
        lower = jnp.where((row // (2 * size) == col // (2 * size)) & (row // size != col // size), strict, 0.0)
        if size == 1:
            inverse = inverse - lower
        else:
            inverse = inverse - bdot(inverse, bdot(lower, inverse, 2 - 1, 0, P_INV), 1, 0, P_INV)
        size *= 2
    return inverse


def parts(queries, keys, cum_c, cum_r, upd_r):
    shape = (queries.shape[0], BLOCK, BLOCK)
    row = lax.broadcasted_iota(jnp.int32, shape, 1)
    col = lax.broadcasted_iota(jnp.int32, shape, 2)
    both = bdot(jnp.concatenate([keys, queries], axis=1), keys, 1, 1, P_GR)
    ratio = jnp.where(row >= col, jnp.exp(jnp.where(row >= col, cum_c - cum_r, 0.0)), 0.0)
    scaled = ratio * upd_r
    return row, col, scaled, ratio, both[:, :BLOCK], both[:, BLOCK:]


def unit(v):
    return lax.rsqrt(jnp.sum(v * v, -1, keepdims=True) + EPS)


def in_order(slots, source, target):
    for n in range(target.shape[0] // BLOCK):
        target[n * BLOCK : (n + 1) * BLOCK, :] = source[pl.ds(pl.multiple_of(slots[n] * BLOCK, BLOCK), BLOCK), :]


def to_slots(slots, rows, target, lanes):
    for n in range(rows.shape[0] // BLOCK):
        target[pl.ds(pl.multiple_of(slots[n] * BLOCK, BLOCK), BLOCK), lanes] = rows[n * BLOCK : (n + 1) * BLOCK]


def fwd_kernel(
    slots, mixed_ref, conv_ref, dec_ref, gain_ref,
    rows_ref, out_ref, err_ref, inv_ref, sk_ref, state_ref, step_ref, proj_ref,
):
    width = WIDTH
    in_order(slots, mixed_ref, proj_ref)
    _, _, act_q = activate(proj_ref[:, 0:width], conv_ref[0])
    _, _, act_k = activate(proj_ref[:, width : 2 * width], conv_ref[1])
    _, _, act_v = activate(proj_ref[:, 2 * width : 3 * width], conv_ref[2])
    act_q, act_k, values = split_heads(act_q), split_heads(act_k), split_heads(act_v)
    queries = act_q * (unit(act_q) * HS**-0.5)
    keys = act_k * unit(act_k)
    _, cum_c, cum_r, upd_c, upd_r = gates(proj_ref[:, 4 * width :], dec_ref[0:1, :], dec_ref[1:2, :])
    row, col, scaled, _, kk, qk = parts(queries, keys, cum_c, cum_r, upd_r)
    inverse = lower_inverse(jnp.where(row > col, scaled * kk, 0.0))
    inv_ref[...] = inverse
    attend = scaled * qk
    grow = jnp.exp(cum_c)
    last = cum_c[:, BLOCK - 1 :, :]
    tail = keys * (jnp.exp(last - cum_c) * upd_c)
    solved = bdot(inverse, jnp.concatenate([values, grow * keys], axis=2), 1, 0, P_ST)
    sk_ref[...] = solved[:, :, HS:]
    carried = bdot(tail, solved, 0, 0, P_ST)
    n = carried.shape[0]
    row2 = lax.broadcasted_iota(jnp.int32, (n, HS, HS), 1)
    col2 = lax.broadcasted_iota(jnp.int32, (n, HS, HS), 2)
    step = jnp.where(row2 == col2, jnp.exp(last), 0.0) - carried[:, :, HS:]
    step_ref[...] = step
    blocks = n // HEADS
    states = []
    for h in range(HEADS):
        state = jnp.zeros((HS, HS), F32)
        states.append(state)
        for i in range(blocks - 1):
            at = h * blocks + i
            state = carried[at, :, :HS] + (dot2(step[at], state, 1, 0, P_ST) if i else 0.0)
            states.append(state)
    states = jnp.stack(states)
    state_ref[...] = states
    seen = bdot(jnp.concatenate([solved[:, :, HS:], grow * queries], axis=1), states, 1, 0, P_ST)
    errors = solved[:, :, :HS] - seen[:, :BLOCK]
    err_ref[...] = errors
    outputs = seen[:, BLOCK:] + bdot(attend, errors, 1, 0, P_ST)
    out_ref[...] = outputs
    scale = lax.rsqrt(jnp.mean(outputs * outputs, -1, keepdims=True) + EPS)
    gate = proj_ref[:, 3 * width : 4 * width]
    rows = (join_heads(outputs * scale * gain_ref[...]) * (gate * sigmoid(gate))).astype(jnp.bfloat16)
    to_slots(slots, rows, rows_ref, slice(0, width))


def unit_back(act, d_norm, factor):
    r = unit(act)
    return factor * (r * d_norm - act * (r * r * r) * jnp.sum(d_norm * act, -1, keepdims=True))


def bwd_kernel(
    slots, mixed_ref, conv_ref, dec_ref, gain_ref, drows_mixed_ref,
    out_ref, err_ref, inv_ref, sk_ref, state_ref, step_ref,
    dproj_ref, dconv_ref, dsmall_ref, proj_ref, drows_ref,
):
    width = WIDTH
    in_order(slots, mixed_ref, proj_ref)
    in_order(slots, drows_mixed_ref, drows_ref)
    n = err_ref.shape[0]
    blocks = n // HEADS
    rates = proj_ref[:, 4 * width :]
    pre_q, sig_q, full_q = activate(proj_ref[:, 0:width], conv_ref[0])
    pre_k, sig_k, full_k = activate(proj_ref[:, width : 2 * width], conv_ref[1])
    act_q, act_k = split_heads(full_q), split_heads(full_k)
    queries = act_q * (unit(act_q) * HS**-0.5)
    keys = act_k * unit(act_k)
    soft, cum_c, cum_r, upd_c, upd_r = gates(rates, dec_ref[0:1, :], dec_ref[1:2, :])
    row, col, scaled, ratio, kk, qk = parts(queries, keys, cum_c, cum_r, upd_r)
    attend = scaled * qk
    grow = jnp.exp(cum_c)
    last = cum_c[:, BLOCK - 1 :, :]
    fade = jnp.exp(last - cum_c)
    weight = fade * upd_c
    tail = keys * weight
    outputs, errors, states = out_ref[...], err_ref[...], state_ref[...]

    gate = proj_ref[:, 3 * width : 4 * width]
    sig_g = sigmoid(gate)
    d_rows = drows_ref[...]
    scale = lax.rsqrt(jnp.mean(outputs * outputs, -1, keepdims=True) + EPS)
    gain = gain_ref[...]
    normal = outputs * scale
    d_gained = split_heads(d_rows * (gate * sig_g))
    d_gate = d_rows * join_heads(normal * gain) * (sig_g * (1.0 + gate * (1.0 - sig_g)))
    to_slots(slots, d_gate.astype(jnp.bfloat16), dproj_ref, slice(3 * width, 4 * width))
    d_gain = jnp.sum((d_gained * normal).reshape(n * BLOCK, HS), 0, keepdims=True)
    d_normal = d_gained * gain
    d_out = scale * d_normal - outputs * (scale * scale * scale) * jnp.mean(d_normal * outputs, -1, keepdims=True)

    d_err_own = bdot(attend, d_out, 0, 0, P_ST)
    to_state = bdot(
        jnp.concatenate([grow * queries, -sk_ref[...]], axis=1),
        jnp.concatenate([d_out, d_err_own], axis=1), 0, 0, P_ST,
    )
    d_ends = [None] * n
    for h in range(HEADS):
        d_end = jnp.zeros((HS, HS), F32)
        for i in range(blocks - 1, -1, -1):
            at = h * blocks + i
            d_ends[at] = d_end
            if i:
                d_end = to_state[at] + (dot2(step_ref[at], d_end, 0, 0, P_ST) if i < blocks - 1 else 0.0)
    d_ends = jnp.stack(d_ends)
    d_err = d_err_own + bdot(tail, d_ends, 1, 0, P_ST)
    d_val = bdot(inv_ref[...], d_err, 0, 0, P_ST)
    pair = jnp.concatenate([d_out, d_val], axis=1)
    by_err = bdot(pair, errors, 1, 1, P_GR)
    by_state = bdot(pair, states, 1, 1, P_GR)
    d_tail = bdot(errors, d_ends, 1, 1, P_GR)
    raw_attend = jnp.where(row >= col, by_err[:, :BLOCK], 0.0)
    raw_system = jnp.where(row > col, -by_err[:, BLOCK:], 0.0)
    d_qk = raw_attend * scaled
    d_kk = raw_system * scaled
    d_seen_q, d_seen_k = by_state[:, :BLOCK], -by_state[:, BLOCK:]
    stacked = jnp.concatenate([d_qk, d_kk], axis=1)
    from_left = bdot(stacked, keys, 1, 0, P_GR)
    from_right = bdot(stacked, jnp.concatenate([queries, keys], axis=1), 0, 0, P_GR)
    d_queries = grow * d_seen_q + from_left[:, :BLOCK]
    d_keys = grow * d_seen_k + weight * d_tail + from_left[:, BLOCK:] + from_right

    mixed = ratio * (raw_attend * qk + raw_system * kk)
    moved = mixed * upd_r
    eye = row == col
    over_upd = jnp.sum(mixed, 1, keepdims=True)
    tail_dot = jnp.sum(keys * d_tail, -1, keepdims=True)
    tail_part = weight * tail_dot
    d_upd = jnp.sum(jnp.where(eye, over_upd, 0.0), -1, keepdims=True) + fade * tail_dot
    d_cum = jnp.sum(moved - jnp.where(eye, over_upd * upd_r, 0.0), -1, keepdims=True)
    d_cum = d_cum + grow * jnp.sum(d_seen_q * queries + d_seen_k * keys, -1, keepdims=True) - tail_part
    d_last = jnp.sum(tail_part, 1, keepdims=True) + jnp.exp(last) * jnp.sum(
        jnp.sum(states * d_ends, 1, keepdims=True), 2, keepdims=True
    )
    ones = (lax.broadcasted_iota(jnp.int32, (BLOCK, BLOCK), 0) <= lax.broadcasted_iota(jnp.int32, (BLOCK, BLOCK), 1)).astype(F32)
    lane = lax.broadcasted_iota(jnp.int32, (blocks, BLOCK, 128), 2)
    spread = jnp.where(lane == 0, d_cum[:blocks], jnp.where(lane == 1, d_cum[blocks:], 0.0))
    d_log = jnp.stack([dot2(ones, spread[i], 1, 0, HIGHEST) for i in range(blocks)])
    d_log = d_log + jnp.where(lane == 0, d_last[:blocks], jnp.where(lane == 1, d_last[blocks:], 0.0))
    d_update = jnp.where(lane == 2, d_upd[:blocks], jnp.where(lane == 3, d_upd[blocks:], 0.0))
    d_log = d_log.reshape(blocks * BLOCK, 128)
    d_update = d_update.reshape(blocks * BLOCK, 128)
    update = sigmoid(rates)
    decay_rate, decay_bias = dec_ref[0:1, :], dec_ref[1:2, :]
    d_first = d_log * -decay_rate * sigmoid(rates + decay_bias)
    d_rates = (d_first + d_update * update * (1.0 - update)).astype(jnp.bfloat16)
    to_slots(slots, d_rates, dproj_ref, slice(4 * width, 4 * width + 128))
    small = jnp.concatenate(
        [
            jnp.sum(d_log * -soft, 0, keepdims=True),
            jnp.sum(d_first, 0, keepdims=True),
            d_gain,
            jnp.zeros((5, 128), F32),
        ],
        axis=0,
    )
    dsmall_ref[...] = small

    for c, (pre, sig, d_act) in enumerate(
        (
            (pre_q, sig_q, join_heads(unit_back(act_q, d_queries, HS**-0.5))),
            (pre_k, sig_k, join_heads(unit_back(act_k, d_keys, 1.0))),
            (None, None, join_heads(d_val)),
        )
    ):
        rows = proj_ref[:, c * width : (c + 1) * width]
        taps = conv_ref[c]
        if pre is None:
            pre, sig, _ = activate(rows, taps)
        d_pre = d_act * (sig * (1.0 + pre * (1.0 - sig)))
        d_in = d_pre * taps[3:4, :]
        sums = []
        for j in range(3):
            d_in = d_in + shift_up(d_pre, 3 - j) * taps[j : j + 1, :]
            sums.append(jnp.sum(d_pre * shift_down(rows, 3 - j), 0, keepdims=True))
        sums.append(jnp.sum(d_pre * rows, 0, keepdims=True))
        to_slots(slots, d_in.astype(jnp.bfloat16), dproj_ref, slice(c * width, (c + 1) * width))
        dconv_ref[c] = jnp.concatenate(sums, axis=0)


def whole(shape):
    return pl.BlockSpec(tuple(shape), lambda i, slots: (0,) * len(shape))


def kernel_call(kernel, name, outs, ins, scratch):
    slots, rest = ins[0], ins[1:]
    return pl.pallas_call(
        kernel,
        grid_spec=pltpu.PrefetchScalarGridSpec(
            num_scalar_prefetch=1,
            grid=(1,),
            in_specs=[whole(a.shape) for a in rest],
            out_specs=[whole(o.shape) for o in outs],
            scratch_shapes=[pltpu.VMEM(shape, F32) for shape in scratch],
        ),
        out_shape=outs,
        compiler_params=pltpu.CompilerParams(vmem_limit_bytes=48 * 2**20),
        name=name,
    )(slots, *rest)


def mixer_fwd(slots, mixed, conv, dec, gain):
    positions = mixed.shape[0]
    n = HEADS * positions // BLOCK
    outs = [jax.ShapeDtypeStruct((positions, WIDTH), jnp.bfloat16)] + [
        jax.ShapeDtypeStruct(shape, F32)
        for shape in (
            (n, BLOCK, HS), (n, BLOCK, HS), (n, BLOCK, BLOCK), (n, BLOCK, HS), (n, HS, HS), (n, HS, HS),
        )
    ]
    return kernel_call(fwd_kernel, "mixer_fwd", outs, (slots, mixed, conv, dec, gain), [mixed.shape])


def mixer_bwd(slots, mixed, conv, dec, gain, d_rows, saved):
    outs = [
        jax.ShapeDtypeStruct(mixed.shape, jnp.bfloat16),
        jax.ShapeDtypeStruct(conv.shape, F32),
        jax.ShapeDtypeStruct((8, 128), F32),
    ]
    ins = (slots, mixed, conv, dec, gain, d_rows, *saved)
    return kernel_call(bwd_kernel, "mixer_bwd", outs, ins, [mixed.shape, d_rows.shape])


UP = [(i, (i + 1) % 4) for i in range(4)]
DOWN = [(i, (i - 1) % 4) for i in range(4)]
SWAP = [(0, 1), (1, 0)]
LOWP = jnp.bfloat16


def up(a):
    return lax.ppermute(a, "z", UP)


def down(a):
    return lax.ppermute(a, "z", DOWN)


def across(a):
    return lax.ppermute(a, "yl", SWAP)


def cuts(rows):
    first = (rows // 3 + 15) // 16 * 16
    return first, 2 * first


def gather(own):
    s, t = cuts(own.shape[0])
    b0, am, ap = across(own), up(own), down(own)
    bm, a2, bp = up(b0), down(ap), across(ap)
    return jnp.concatenate([own, b0, ap, bp, a2, up(bm[:s]), down(bp[s:t]), across(a2[t:]), am, bm], axis=0)


def add(*parts):
    total = parts[0].astype(F32)
    for part in parts[1:]:
        total = total + part.astype(F32)
    return total


def scatter(whole):
    rows = whole.shape[0] // 8
    s, t = cuts(rows)
    a0, b0, ap, bp, a2, b2, am, bm = (whole[i * rows : (i + 1) * rows] for i in range(8))
    r1, r2, r3 = down(b2[:s]), up(b2[s:t]), across(b2[t:])
    bm = jnp.concatenate([add(bm[:s], r1).astype(LOWP), bm[s:]], axis=0)
    bp = jnp.concatenate([bp[:s], add(bp[s:t], r2).astype(LOWP), bp[t:]], axis=0)
    a2 = jnp.concatenate([a2[:t], add(a2[t:], r3).astype(LOWP)], axis=0)
    q1, q2, q3 = down(bm), up(a2), across(bp)
    b0, ap = add(b0, q1).astype(LOWP), add(ap, q2, q3).astype(LOWP)
    return add(a0, across(b0), down(am), up(ap))


def dot(a, b, ca, cb):
    return lax.dot_general(a, b, (((ca,), (cb,)), ((), ())), preferred_element_type=F32)


def rms(v):
    return lax.rsqrt(jnp.mean(v * v, -1, keepdims=True) + EPS)


def norm_back(values, scale, gain, d_normed):
    weighted = d_normed * gain
    d_gain = jnp.sum(d_normed * values * scale, 0)
    d_values = scale * weighted - values * scale**3 * jnp.mean(weighted * values, -1, keepdims=True)
    return d_values, d_gain


def reduce_rows(rows):
    part = lax.psum_scatter(rows, "c", scatter_dimension=0, tiled=True)
    part = lax.psum_scatter(part, "x", scatter_dimension=0, tiled=True)
    part = add(part, lax.ppermute(part, "yh", SWAP)).astype(LOWP)
    part = lax.all_gather(part, "x", axis=0, tiled=True)
    return lax.all_gather(part, "c", axis=0, tiled=True)


def shards(
    tokens, lengths, cotangent, attn_gain, mixer_in, rate_proj, conv_weight, decay_rate, decay_bias,
    out_gain, out_proj, ffn_gain, gate_up, down_proj,
):
    rows = tokens.shape[2]
    micros = range(tokens.shape[1])
    z, yl = lax.axis_index("z"), lax.axis_index("yl")
    places = (2 * z + yl) * rows + jnp.arange(rows, dtype=jnp.int32)
    block = jnp.arange(8, dtype=jnp.int32)
    slots = 2 * ((block // 2 - z) % 4) + (block % 2 + yl) % 2

    width = mixer_in.shape[1] * mixer_in.shape[2]
    rate_pad = jnp.pad(rate_proj.reshape(rate_proj.shape[0], 4), ((0, 0), (0, 124)))
    w_in = jnp.concatenate([mixer_in.reshape(mixer_in.shape[0], width), rate_pad], axis=1)
    hidden_units = down_proj.shape[0]
    w_gate, w_up = gate_up[:, 0, :].T, gate_up[:, 1, :].T
    dec = jnp.pad(jnp.stack([decay_rate, decay_bias]), ((0, 0), (0, 126)))
    gain_row = out_gain[None]

    source = [tokens[0, m].astype(F32) for m in micros]
    valid = [(places < lengths[0, m]).astype(F32)[:, None] for m in micros]
    scale_one = [rms(source[m]) for m in micros]
    rows_one = [gather((source[m] * scale_one[m] * attn_gain).astype(LOWP)) for m in micros]
    grad_out = [cotangent[0, m].astype(F32) * valid[m] for m in micros]
    grad_rows = [gather(grad_out[m].astype(LOWP)) for m in micros]

    mixed, saved, mixer_rows, hidden, scale_two, rows_two = [], [], [], [], [], []
    for m in micros:
        mixed.append(dot(rows_one[m], w_in, 1, 0))
        out, *keep = mixer_fwd(slots, mixed[m], conv_weight, dec, gain_row)
        mixer_rows.append(out)
        saved.append(keep)
        attended = scatter(dot(out, out_proj, 1, 0).astype(LOWP))
        hidden.append(source[m] + attended)
        scale_two.append(rms(hidden[m]))
        rows_two.append(gather((hidden[m] * scale_two[m] * ffn_gain).astype(LOWP)))

    layer_out, d_hidden, grad_attn = [], [], []
    d_ffn_gain = 0.0
    d_down, d_gate, d_up = 0.0, 0.0, 0.0
    for m in micros:
        gate = dot(w_gate, rows_two[m], 1, 1)
        lift = dot(w_up, rows_two[m], 1, 1)
        sigma = jax.nn.sigmoid(gate)
        inner = (gate * sigma * lift).astype(LOWP)
        branch = scatter(dot(inner, down_proj, 0, 0).astype(LOWP))
        layer_out.append(((hidden[m] + branch) * valid[m]).astype(LOWP))
        d_inner = dot(down_proj, grad_rows[m], 1, 1)
        dg = (d_inner * lift * sigma * (1.0 + gate * (1.0 - sigma))).astype(LOWP)
        du = (d_inner * gate * sigma).astype(LOWP)
        d_normed = (dot(dg, w_gate, 0, 0) + dot(du, w_up, 0, 0)).astype(LOWP)
        d_normed = scatter(d_normed)
        d_down = d_down + dot(inner, grad_rows[m], 1, 0)
        d_gate = d_gate + dot(dg, rows_two[m], 1, 0)
        d_up = d_up + dot(du, rows_two[m], 1, 0)
        d_from, part = norm_back(hidden[m], scale_two[m], ffn_gain, d_normed)
        d_ffn_gain = d_ffn_gain + part
        d_hidden.append(grad_out[m] + d_from)
        grad_attn.append(gather(d_hidden[m].astype(LOWP)))
    ffn = reduce_rows(jnp.concatenate([d_gate.astype(LOWP), d_up.astype(LOWP), d_down.astype(LOWP)], axis=0))

    d_tokens = []
    d_attn_gain, d_conv, d_small, d_out, d_in = 0.0, 0.0, 0.0, 0.0, 0.0
    for m in micros:
        d_out = d_out + dot(mixer_rows[m], grad_attn[m], 0, 0)
        d_mixer_rows = dot(grad_attn[m], out_proj, 1, 1)
        d_mixed, conv_part, small_part = mixer_bwd(slots, mixed[m], conv_weight, dec, gain_row, d_mixer_rows, saved[m])
        d_normed = scatter(dot(d_mixed, w_in, 1, 1).astype(LOWP))
        d_in = d_in + dot(rows_one[m], d_mixed, 0, 0)
        d_conv, d_small = d_conv + conv_part, d_small + small_part
        d_from, part = norm_back(source[m], scale_one[m], attn_gain, d_normed)
        d_attn_gain = d_attn_gain + part
        d_tokens.append((d_hidden[m] + d_from).astype(LOWP))
    d_out = reduce_rows(d_out.astype(LOWP))
    d_mixer_in = reduce_rows(d_in[:, :width].astype(LOWP))
    dp = ("x", "yh", "c")
    d_rate, d_conv, d_pair = lax.psum(
        (d_in[:, width : width + 4], d_conv, d_small[:2, :2]), dp
    )
    d_attn_gain, d_ffn_gain, d_out_gain = lax.psum((d_attn_gain, d_ffn_gain, d_small[2]), dp + ("z", "yl"))
    ffn = ffn.astype(F32)
    d_gate_up = ffn[: 2 * hidden_units].reshape(2, hidden_units, -1).transpose(2, 0, 1)
    return (
        jnp.stack(layer_out)[None],
        jnp.stack(d_tokens)[None],
        d_attn_gain,
        d_mixer_in.astype(F32).reshape(mixer_in.shape),
        d_rate.reshape(rate_proj.shape),
        d_conv,
        d_pair[0],
        d_pair[1],
        d_out_gain,
        d_out.astype(F32),
        d_ffn_gain,
        d_gate_up,
        ffn[2 * hidden_units :],
    )


def solution(mesh):
    fine = Mesh(mesh.devices.reshape(4, 2, 2, 4, 2), ("x", "yh", "c", "z", "yl"))
    dp, tensor = ("x", "yh", "c"), ("z", "yl")
    in_specs = (
        P(dp, None, tensor, None),
        P(dp, None),
        P(dp, None, tensor, None),
        P(),
        P(None, None, tensor),
        P(None, None, tensor),
        P(None, None, tensor),
        P(tensor),
        P(tensor),
        P(),
        P(tensor, None),
        P(),
        P(None, None, tensor),
        P(tensor, None),
    )
    out_specs = (
        P(dp, None, tensor, None),
        P(dp, None, tensor, None),
        P(),
        P(None, None, tensor),
        P(None, None, tensor),
        P(None, None, tensor),
        P(tensor),
        P(tensor),
        P(),
        P(tensor, None),
        P(),
        P(None, None, tensor),
        P(tensor, None),
    )
    return jax.shard_map(shards, mesh=fine, in_specs=in_specs, out_specs=out_specs, check_vma=False)
```

```python
import jax, jax.numpy as jnp
from jax import lax
from jax.experimental import pallas as pl
from jax.experimental.pallas import tpu as pltpu
from jax.sharding import Mesh, PartitionSpec as P

EPS = 1e-06
BLOCK = 64
HS = 128
HEADS = 2
WIDTH = HEADS * HS
F32 = jnp.float32
HIGHEST = lax.Precision.HIGHEST
HIGH = lax.Precision.HIGH
LOW = lax.Precision.DEFAULT
P_INV = HIGH
P_ST = HIGH
P_GR = HIGH


def dot2(a, b, ca, cb, precision):
    return lax.dot_general(a, b, (((ca,), (cb,)), ((), ())), precision=precision, preferred_element_type=F32)


def bdot(a, b, ca, cb, precision):
    if precision == LOW:
        a, b = a.astype(jnp.bfloat16), b.astype(jnp.bfloat16)
    return jnp.stack([dot2(a[i], b[i], ca, cb, precision) for i in range(a.shape[0])])


def split_heads(rows):
    blocks = rows.shape[0] // BLOCK
    return jnp.concatenate(
        [rows[:, h * HS : (h + 1) * HS].reshape(blocks, BLOCK, HS) for h in range(HEADS)], axis=0
    )


def join_heads(stacked):
    blocks = stacked.shape[0] // HEADS
    return jnp.concatenate(
        [stacked[h * blocks : (h + 1) * blocks].reshape(blocks * BLOCK, HS) for h in range(HEADS)], axis=1
    )


def shift_down(rows, steps):
    if steps == 0:
        return rows
    place = lax.broadcasted_iota(jnp.int32, rows.shape, 0)
    return jnp.where(place >= steps, pltpu.roll(rows, steps, 0), 0.0)


def shift_up(rows, steps):
    if steps == 0:
        return rows
    size = rows.shape[0]
    place = lax.broadcasted_iota(jnp.int32, rows.shape, 0)
    return jnp.where(place < size - steps, pltpu.roll(rows, size - steps, 0), 0.0)


def sigmoid(v):
    return 1.0 / (1.0 + jnp.exp(-v))


def softplus(v):
    return jnp.maximum(v, 0.0) + jnp.log1p(jnp.exp(-jnp.abs(v)))


def convolve(rows, taps):
    out = rows * taps[3:4, :]
    for j in range(3):
        out = out + shift_down(rows, 3 - j) * taps[j : j + 1, :]
    return out


def columns(table, blocks, first):
    return jnp.concatenate(
        [table[:, first + h : first + h + 1].reshape(blocks, BLOCK, 1) for h in range(HEADS)], axis=0
    )


def rows_of(turned, first):
    return jnp.concatenate([turned[:, first + h : first + h + 1, :] for h in range(HEADS)], axis=0)


def gates(rates, decay_rate, decay_bias):
    blocks = rates.shape[0] // BLOCK
    soft = softplus(rates + decay_bias)
    logdecay = (-decay_rate * soft).reshape(blocks, BLOCK, 128)
    row = lax.broadcasted_iota(jnp.int32, (BLOCK, BLOCK), 0)
    col = lax.broadcasted_iota(jnp.int32, (BLOCK, BLOCK), 1)
    ones = (row >= col).astype(F32)
    cumul = jnp.stack([dot2(ones, logdecay[n], 1, 0, HIGHEST) for n in range(blocks)])
    update = sigmoid(rates).reshape(blocks, BLOCK, 128)
    lane = lax.broadcasted_iota(jnp.int32, (blocks, BLOCK, 128), 2)
    table = jnp.where(lane < 2, cumul, update)
    turned = jnp.stack([jnp.transpose(table[n], (1, 0)) for n in range(blocks)])
    flat = table.reshape(blocks * BLOCK, 128)
    return soft, columns(flat, blocks, 0), rows_of(turned, 0), columns(flat, blocks, 2), rows_of(turned, 2)


def activate(rows, taps):
    pre = convolve(rows, taps)
    sig = sigmoid(pre)
    return pre, sig, pre * sig


def lower_inverse(strict):
    row = lax.broadcasted_iota(jnp.int32, strict.shape, 1)
    col = lax.broadcasted_iota(jnp.int32, strict.shape, 2)
    size = 1
    inverse = jnp.where(row == col, 1.0, 0.0)
    while size < BLOCK:
        lower = jnp.where((row // (2 * size) == col // (2 * size)) & (row // size != col // size), strict, 0.0)
        if size == 1:
            inverse = inverse - lower
        else:
            inverse = inverse - bdot(inverse, bdot(lower, inverse, 2 - 1, 0, P_INV), 1, 0, P_INV)
        size *= 2
    return inverse


def parts(queries, keys, cum_c, cum_r, upd_r):
    shape = (queries.shape[0], BLOCK, BLOCK)
    row = lax.broadcasted_iota(jnp.int32, shape, 1)
    col = lax.broadcasted_iota(jnp.int32, shape, 2)
    both = bdot(jnp.concatenate([keys, queries], axis=1), keys, 1, 1, P_GR)
    ratio = jnp.where(row >= col, jnp.exp(jnp.where(row >= col, cum_c - cum_r, 0.0)), 0.0)
    scaled = ratio * upd_r
    return row, col, scaled, ratio, both[:, :BLOCK], both[:, BLOCK:]


def unit(v):
    return lax.rsqrt(jnp.sum(v * v, -1, keepdims=True) + EPS)


def place(slots, n):
    first = (slots[n] * pl.num_programs(0) + pl.program_id(0)) * BLOCK
    return pl.ds(pl.multiple_of(first, BLOCK), BLOCK)


def in_order(slots, pieces, held, target):
    @pl.when(pl.program_id(0) == 0)
    def _():
        first = 0
        for piece in pieces:
            held[first : first + piece.shape[0], :] = piece[...]
            first += piece.shape[0]

    for n in range(target.shape[0] // BLOCK):
        target[n * BLOCK : (n + 1) * BLOCK, :] = held[place(slots, n), :]


def out_slots(held, outs):
    @pl.when(pl.program_id(0) == pl.num_programs(0) - 1)
    def _():
        size = outs[0].shape[0]
        for i, out in enumerate(outs):
            out[...] = held[i * size : (i + 1) * size, :]


def fwd_kernel(slots, *refs):
    pieces, refs = refs[:9], refs[9:]
    w_ref, conv_ref, dec_ref, gain_ref, out_w_ref, *sums, normed_ref, proj_ref, rows_ref = refs[:16]
    out_ref, err_ref, inv_ref, sk_ref, state_ref, step_ref, held_ref = refs[16:]
    width = WIDTH
    in_order(slots, pieces, held_ref, normed_ref)
    proj_ref[...] = dot2(normed_ref[...], w_ref[...], 1, 0, None)
    _, _, act_q = activate(proj_ref[:, 0:width], conv_ref[0])
    _, _, act_k = activate(proj_ref[:, width : 2 * width], conv_ref[1])
    _, _, act_v = activate(proj_ref[:, 2 * width : 3 * width], conv_ref[2])
    act_q, act_k, values = split_heads(act_q), split_heads(act_k), split_heads(act_v)
    queries = act_q * (unit(act_q) * HS**-0.5)
    keys = act_k * unit(act_k)
    _, cum_c, cum_r, upd_c, upd_r = gates(proj_ref[:, 4 * width :], dec_ref[0:1, :], dec_ref[1:2, :])
    row, col, scaled, _, kk, qk = parts(queries, keys, cum_c, cum_r, upd_r)
    inverse = lower_inverse(jnp.where(row > col, scaled * kk, 0.0))
    inv_ref[...] = inverse
    attend = scaled * qk
    grow = jnp.exp(cum_c)
    last = cum_c[:, BLOCK - 1 :, :]
    tail = keys * (jnp.exp(last - cum_c) * upd_c)
    solved = bdot(inverse, jnp.concatenate([values, grow * keys], axis=2), 1, 0, P_ST)
    sk_ref[...] = solved[:, :, HS:]
    carried = bdot(tail, solved, 0, 0, P_ST)
    n = carried.shape[0]
    row2 = lax.broadcasted_iota(jnp.int32, (n, HS, HS), 1)
    col2 = lax.broadcasted_iota(jnp.int32, (n, HS, HS), 2)
    step = jnp.where(row2 == col2, jnp.exp(last), 0.0) - carried[:, :, HS:]
    step_ref[...] = step
    blocks = n // HEADS
    states = []
    for h in range(HEADS):
        state = jnp.zeros((HS, HS), F32)
        states.append(state)
        for i in range(blocks - 1):
            at = h * blocks + i
            state = carried[at, :, :HS] + (dot2(step[at], state, 1, 0, P_ST) if i else 0.0)
            states.append(state)
    states = jnp.stack(states)
    state_ref[...] = states
    seen = bdot(jnp.concatenate([solved[:, :, HS:], grow * queries], axis=1), states, 1, 0, P_ST)
    errors = solved[:, :, :HS] - seen[:, :BLOCK]
    err_ref[...] = errors
    outputs = seen[:, BLOCK:] + bdot(attend, errors, 1, 0, P_ST)
    out_ref[...] = outputs
    scale = lax.rsqrt(jnp.mean(outputs * outputs, -1, keepdims=True) + EPS)
    gate = proj_ref[:, 3 * width : 4 * width]
    rows = (join_heads(outputs * scale * gain_ref[...]) * (gate * sigmoid(gate))).astype(jnp.bfloat16)
    rows_ref[...] = rows
    product = dot2(rows, out_w_ref[...], 1, 0, None).astype(jnp.bfloat16)
    for n in range(blocks):
        held_ref[place(slots, n), :] = product[n * BLOCK : (n + 1) * BLOCK]
    out_slots(held_ref, sums)


def unit_back(act, d_norm, factor):
    r = unit(act)
    return factor * (r * d_norm - act * (r * r * r) * jnp.sum(d_norm * act, -1, keepdims=True))


def bwd_kernel(slots, *refs):
    pieces, refs = refs[:9], refs[9:]
    proj_ref, conv_ref, dec_ref, gain_ref, out_w_ref, out_ref, err_ref, inv_ref, sk_ref, state_ref, step_ref = refs[:11]
    grad_ref, dproj_ref, dconv_ref, dsmall_ref, held_ref = refs[11:]
    width = WIDTH
    in_order(slots, pieces, held_ref, grad_ref)
    d_rows = dot2(grad_ref[...], out_w_ref[...], 1, 1, None)
    n = err_ref.shape[0]
    blocks = n // HEADS
    rates = proj_ref[:, 4 * width :]
    pre_q, sig_q, full_q = activate(proj_ref[:, 0:width], conv_ref[0])
    pre_k, sig_k, full_k = activate(proj_ref[:, width : 2 * width], conv_ref[1])
    act_q, act_k = split_heads(full_q), split_heads(full_k)
    queries = act_q * (unit(act_q) * HS**-0.5)
    keys = act_k * unit(act_k)
    soft, cum_c, cum_r, upd_c, upd_r = gates(rates, dec_ref[0:1, :], dec_ref[1:2, :])
    row, col, scaled, ratio, kk, qk = parts(queries, keys, cum_c, cum_r, upd_r)
    attend = scaled * qk
    grow = jnp.exp(cum_c)
    last = cum_c[:, BLOCK - 1 :, :]
    fade = jnp.exp(last - cum_c)
    weight = fade * upd_c
    tail = keys * weight
    outputs, errors, states = out_ref[...], err_ref[...], state_ref[...]

    gate = proj_ref[:, 3 * width : 4 * width]
    sig_g = sigmoid(gate)
    scale = lax.rsqrt(jnp.mean(outputs * outputs, -1, keepdims=True) + EPS)
    gain = gain_ref[...]
    normal = outputs * scale
    d_gained = split_heads(d_rows * (gate * sig_g))
    d_gate = d_rows * join_heads(normal * gain) * (sig_g * (1.0 + gate * (1.0 - sig_g)))
    dproj_ref[:, 3 * width : 4 * width] = d_gate.astype(jnp.bfloat16)
    d_gain = jnp.sum((d_gained * normal).reshape(n * BLOCK, HS), 0, keepdims=True)
    d_normal = d_gained * gain
    d_out = scale * d_normal - outputs * (scale * scale * scale) * jnp.mean(d_normal * outputs, -1, keepdims=True)

    d_err_own = bdot(attend, d_out, 0, 0, P_ST)
    to_state = bdot(
        jnp.concatenate([grow * queries, -sk_ref[...]], axis=1),
        jnp.concatenate([d_out, d_err_own], axis=1), 0, 0, P_ST,
    )
    d_ends = [None] * n
    for h in range(HEADS):
        d_end = jnp.zeros((HS, HS), F32)
        for i in range(blocks - 1, -1, -1):
            at = h * blocks + i
            d_ends[at] = d_end
            if i:
                d_end = to_state[at] + (dot2(step_ref[at], d_end, 0, 0, P_ST) if i < blocks - 1 else 0.0)
    d_ends = jnp.stack(d_ends)
    d_err = d_err_own + bdot(tail, d_ends, 1, 0, P_ST)
    d_val = bdot(inv_ref[...], d_err, 0, 0, P_ST)
    pair = jnp.concatenate([d_out, d_val], axis=1)
    by_err = bdot(pair, errors, 1, 1, P_GR)
    by_state = bdot(pair, states, 1, 1, P_GR)
    d_tail = bdot(errors, d_ends, 1, 1, P_GR)
    raw_attend = jnp.where(row >= col, by_err[:, :BLOCK], 0.0)
    raw_system = jnp.where(row > col, -by_err[:, BLOCK:], 0.0)
    d_qk = raw_attend * scaled
    d_kk = raw_system * scaled
    d_seen_q, d_seen_k = by_state[:, :BLOCK], -by_state[:, BLOCK:]
    stacked = jnp.concatenate([d_qk, d_kk], axis=1)
    from_left = bdot(stacked, keys, 1, 0, P_GR)
    from_right = bdot(stacked, jnp.concatenate([queries, keys], axis=1), 0, 0, P_GR)
    d_queries = grow * d_seen_q + from_left[:, :BLOCK]
    d_keys = grow * d_seen_k + weight * d_tail + from_left[:, BLOCK:] + from_right

    mixed = ratio * (raw_attend * qk + raw_system * kk)
    moved = mixed * upd_r
    eye = row == col
    over_upd = jnp.sum(mixed, 1, keepdims=True)
    tail_dot = jnp.sum(keys * d_tail, -1, keepdims=True)
    tail_part = weight * tail_dot
    d_upd = jnp.sum(jnp.where(eye, over_upd, 0.0), -1, keepdims=True) + fade * tail_dot
    d_cum = jnp.sum(moved - jnp.where(eye, over_upd * upd_r, 0.0), -1, keepdims=True)
    d_cum = d_cum + grow * jnp.sum(d_seen_q * queries + d_seen_k * keys, -1, keepdims=True) - tail_part
    d_last = jnp.sum(tail_part, 1, keepdims=True) + jnp.exp(last) * jnp.sum(
        jnp.sum(states * d_ends, 1, keepdims=True), 2, keepdims=True
    )
    ones = (lax.broadcasted_iota(jnp.int32, (BLOCK, BLOCK), 0) <= lax.broadcasted_iota(jnp.int32, (BLOCK, BLOCK), 1)).astype(F32)
    lane = lax.broadcasted_iota(jnp.int32, (blocks, BLOCK, 128), 2)
    spread = jnp.where(lane == 0, d_cum[:blocks], jnp.where(lane == 1, d_cum[blocks:], 0.0))
    d_log = jnp.stack([dot2(ones, spread[i], 1, 0, HIGHEST) for i in range(blocks)])
    d_log = d_log + jnp.where(lane == 0, d_last[:blocks], jnp.where(lane == 1, d_last[blocks:], 0.0))
    d_update = jnp.where(lane == 2, d_upd[:blocks], jnp.where(lane == 3, d_upd[blocks:], 0.0))
    d_log = d_log.reshape(blocks * BLOCK, 128)
    d_update = d_update.reshape(blocks * BLOCK, 128)
    update = sigmoid(rates)
    decay_rate, decay_bias = dec_ref[0:1, :], dec_ref[1:2, :]
    d_first = d_log * -decay_rate * sigmoid(rates + decay_bias)
    d_rates = (d_first + d_update * update * (1.0 - update)).astype(jnp.bfloat16)
    dproj_ref[:, 4 * width :] = d_rates
    small = jnp.concatenate(
        [
            jnp.sum(d_log * -soft, 0, keepdims=True),
            jnp.sum(d_first, 0, keepdims=True),
            d_gain,
            jnp.zeros((5, 128), F32),
        ],
        axis=0,
    )
    dsmall_ref[...] = small

    for c, (pre, sig, d_act) in enumerate(
        (
            (pre_q, sig_q, join_heads(unit_back(act_q, d_queries, HS**-0.5))),
            (pre_k, sig_k, join_heads(unit_back(act_k, d_keys, 1.0))),
            (None, None, join_heads(d_val)),
        )
    ):
        rows = proj_ref[:, c * width : (c + 1) * width]
        taps = conv_ref[c]
        if pre is None:
            pre, sig, _ = activate(rows, taps)
        d_pre = d_act * (sig * (1.0 + pre * (1.0 - sig)))
        d_in = d_pre * taps[3:4, :]
        sums = []
        for j in range(3):
            d_in = d_in + shift_up(d_pre, 3 - j) * taps[j : j + 1, :]
            sums.append(jnp.sum(d_pre * shift_down(rows, 3 - j), 0, keepdims=True))
        sums.append(jnp.sum(d_pre * rows, 0, keepdims=True))
        dproj_ref[:, c * width : (c + 1) * width] = d_in.astype(jnp.bfloat16)
        dconv_ref[c] = jnp.concatenate(sums, axis=0)


def whole(shape):
    return pl.BlockSpec(tuple(shape), lambda i, slots: (0,) * len(shape), pipeline_mode=pl.Buffered(1))


def each(shape):
    return pl.BlockSpec((None,) + tuple(shape[1:]), lambda i, slots: (i,) + (0,) * (len(shape) - 1))


def kernel_call(kernel, name, micros, outs, ins, held, time):
    slots, rest = ins[0], ins[1:]
    spec = lambda a: each(a.shape) if len(a.shape) > 2 and a.shape[0] == micros else whole(a.shape)
    return pl.pallas_call(
        kernel,
        grid_spec=pltpu.PrefetchScalarGridSpec(
            num_scalar_prefetch=1,
            grid=(micros,),
            in_specs=[spec(a) for a in rest],
            out_specs=[spec(o) for o in outs],
            scratch_shapes=[pltpu.VMEM(held, jnp.bfloat16)],
        ),
        out_shape=outs,
        compiler_params=pltpu.CompilerParams(vmem_limit_bytes=62 * 2**20),
        cost_estimate=cost(time),
        name=name,
    )(slots, *rest)


def mixer_fwd(slots, pieces, w_in, conv, dec, gain, out_proj, micros):
    rows, features = 8 * pieces[0].shape[0], pieces[0].shape[1]
    own = rows // micros
    n = HEADS * own // BLOCK
    low = lambda *shape: jax.ShapeDtypeStruct(shape, jnp.bfloat16)
    wide = lambda *shape: jax.ShapeDtypeStruct((micros,) + shape, F32)
    outs = [low(rows // 8, features)] * 8
    outs += [low(micros, own, features), wide(own, w_in.shape[1]), low(micros, own, WIDTH)]
    outs += [wide(n, BLOCK, HS), wide(n, BLOCK, HS), wide(n, BLOCK, BLOCK), wide(n, BLOCK, HS)]
    outs += [wide(n, HS, HS), wide(n, HS, HS)]
    ins = (slots, *pieces, w_in, conv, dec, gain, out_proj)
    done = kernel_call(fwd_kernel, "mixer_fwd", micros, outs, ins, (rows, features), 30)
    return done[:8], done[8:11], done[11:]


def mixer_bwd(slots, pieces, mixed, conv, dec, gain, out_proj, saved, micros):
    rows, features = 8 * pieces[0].shape[0], pieces[0].shape[1]
    outs = [
        jax.ShapeDtypeStruct((micros, rows // micros, features), jnp.bfloat16),
        jax.ShapeDtypeStruct(mixed.shape, jnp.bfloat16),
        jax.ShapeDtypeStruct((micros,) + conv.shape, F32),
        jax.ShapeDtypeStruct((micros, 8, 128), F32),
    ]
    ins = (slots, *pieces, mixed, conv, dec, gain, out_proj, *saved)
    return kernel_call(bwd_kernel, "mixer_bwd", micros, outs, ins, (rows, features), 32)


def normed_kernel(slots, d_ref, w_ref, *refs):
    outs, held = refs[:-1], refs[-1]
    micros, blocks, size, _ = d_ref.shape
    for n in range(blocks):
        for m in range(micros):
            first = pl.multiple_of((slots[n] * micros + m) * size, size)
            held[pl.ds(first, size), :] = d_ref[m, n]
    product = dot2(held[...], w_ref[...], 1, 1, None).astype(jnp.bfloat16)
    for i, out in enumerate(outs):
        out[...] = product[i * size * micros : (i + 1) * size * micros]


def normed_grad(slots, d_mixed, w_in):
    micros, own, width = d_mixed.shape
    slot = jax.ShapeDtypeStruct((micros * own // 8, w_in.shape[0]), jnp.bfloat16)
    shape = (micros, 8, own // 8, width)
    spec = lambda shape: pl.BlockSpec(tuple(shape), lambda i, slots: (0,) * len(shape))
    return pl.pallas_call(
        normed_kernel,
        grid_spec=pltpu.PrefetchScalarGridSpec(
            num_scalar_prefetch=1,
            grid=(1,),
            in_specs=[spec(shape), spec(w_in.shape)],
            out_specs=[spec(slot.shape)] * 8,
            scratch_shapes=[pltpu.VMEM((micros * own, width), jnp.bfloat16)],
        ),
        out_shape=[slot] * 8,
        compiler_params=pltpu.CompilerParams(vmem_limit_bytes=48 * 2**20),
        cost_estimate=cost(8),
        name="normed_grad",
    )(slots, d_mixed.reshape(shape), w_in)


UP = [(i, (i + 1) % 4) for i in range(4)]
DOWN = [(i, (i - 1) % 4) for i in range(4)]
SWAP = [(0, 1), (1, 0)]
LOWP = jnp.bfloat16


def up(a):
    return lax.ppermute(a, "z", UP)


def down(a):
    return lax.ppermute(a, "z", DOWN)


def across(a):
    return lax.ppermute(a, "yl", SWAP)


def phase(*arrays):
    return lax.optimization_barrier(arrays)


def gather(own, aside=None, needed=None):
    half = own.shape[0] // 2
    b0, am, ap = phase(across(own), up(own), down(own))
    bm, a2, bp, needed = phase(up(b0), down(ap), across(ap), needed(b0) if needed else ())
    other = [] if aside is None else [across(after(aside, bm))]
    low, high, *other = phase(up(bm[:half]), down(bp[half:]), *other)
    return [own, b0, ap, bp, a2, low, high, am, bm], other, needed


def add(*parts):
    total = parts[0].astype(F32)
    for part in parts[1:]:
        total = total + part.astype(F32)
    return total


def scatter(*lists, one=(), two=None, late=None):
    half = lists[0][0].shape[0] // 2
    steps = [(down(b2[:half]), up(b2[half:])) for _, _, _, _, _, b2, _, _ in lists]
    steps, one = phase(steps, one)
    held = []
    for (a0, b0, ap, bp, a2, _, am, bm), (r1, r2) in zip(lists, steps):
        bm = jnp.concatenate([add(bm[:half], r1).astype(LOWP), bm[half:]], axis=0)
        bp = jnp.concatenate([bp[:half], add(bp[half:], r2).astype(LOWP)], axis=0)
        held.append((a0, b0, ap, am, down(bm), up(a2), across(bp)))
    if two:
        held, one = phase(held, two(one))
    else:
        (held,) = phase(held)
    sent = []
    for a0, b0, ap, am, q1, q2, q3 in held:
        b0, ap = add(b0, q1).astype(LOWP), add(ap, q2, q3).astype(LOWP)
        sent.append((a0, across(b0), down(am), up(ap)))
    sent, one = phase(sent, late(one) if late else one)
    return [add(*parts) for parts in sent], one


def dot(a, b, ca, cb):
    return lax.dot_general(a, b, (((ca,), (cb,)), ((), ())), preferred_element_type=F32)


def rms(v):
    return lax.rsqrt(jnp.mean(v * v, -1, keepdims=True) + EPS)


def norm_back(values, scale, gain, d_normed):
    weighted = d_normed * gain
    d_gain = jnp.sum(d_normed * values * scale, 0)
    d_values = scale * weighted - values * scale**3 * jnp.mean(weighted * values, -1, keepdims=True)
    return d_values, d_gain


def ffn_kernel(at, *refs):
    pieces, (grad_ref, gate_w, up_w, down_w) = refs[:-17], refs[-17:-13]
    rows_ref, inner_ref, slots_ref, dgu_ref = refs[-13:-9]
    outs, total = refs[-9:-1], refs[-1]
    step = pl.program_id(0)
    quarter = grad_ref.shape[0] // 4

    @pl.when(step == 0)
    def _():
        first = 0
        for piece in pieces:
            rows_ref[first : first + piece.shape[0], :] = piece[...]
            first += piece.shape[0]

    rows = rows_ref[...]
    gate = dot(gate_w[...], rows, 1, 1)
    lift = dot(up_w[...], rows, 1, 1)
    for dz in range(4):
        lanes = slice(dz * quarter, (dz + 1) * quarter)
        place = pl.ds(pl.multiple_of(lax.rem(at[0] + dz, 4) * quarter, quarter), quarter)
        d_inner = dot(down_w[...], grad_ref[place, :], 1, 1)
        g, u = gate[:, lanes], lift[:, lanes]
        sigma = sigmoid(g)
        inner = (g * sigma * u).astype(LOWP)
        inner_ref[:, place] = inner
        slots_ref[:, lanes] = inner
        dgu_ref[0, :, lanes] = (d_inner * u * sigma * (1.0 + g * (1.0 - sigma))).astype(LOWP)
        dgu_ref[1, :, lanes] = (d_inner * g * sigma).astype(LOWP)
    both = dgu_ref[...].reshape(-1, dgu_ref.shape[2])
    weights = jnp.concatenate([gate_w[...], up_w[...]], axis=0)
    part = dot(both, weights, 0, 0)

    @pl.when(step == 0)
    def _():
        total[...] = part

    @pl.when(step == pl.num_programs(0) - 1)
    def _():
        size = outs[0].shape[0]
        done = total[...] + part
        for i, out in enumerate(outs):
            out[...] = done[i * size : (i + 1) * size].astype(LOWP)


def cost(microseconds):
    return pl.CostEstimate(flops=microseconds * 10**9, bytes_accessed=microseconds * 3 * 10**6, transcendentals=0)


def ffn_back(at, pieces, grad_rows, gate_up, down_proj):
    rows, features = grad_rows.shape
    units = down_proj.shape[0]
    tile = units // 2
    full = lambda shape: pl.BlockSpec(tuple(shape), lambda i, at: (0,) * len(shape))
    part = pl.BlockSpec((tile, features), lambda i, at: (i, 0))
    gate, lift = (pl.BlockSpec((None, tile, features), lambda i, at, k=k: (k, i, 0)) for k in range(2))
    lines = pl.BlockSpec((tile, rows), lambda i, at: (i, 0))
    pair = pl.BlockSpec((2, tile, rows), lambda i, at: (0, i, 0))
    slot = (rows // 8, features)
    return pl.pallas_call(
        ffn_kernel,
        grid_spec=pltpu.PrefetchScalarGridSpec(
            num_scalar_prefetch=1,
            grid=(2,),
            in_specs=[full(p.shape) for p in pieces] + [full(grad_rows.shape), gate, lift, part],
            out_specs=[full(grad_rows.shape), lines, lines, pair] + [full(slot)] * 8,
            scratch_shapes=[pltpu.VMEM((rows, features), F32)],
        ),
        out_shape=[jax.ShapeDtypeStruct(grad_rows.shape, LOWP)]
        + [jax.ShapeDtypeStruct((units, rows), LOWP)] * 2
        + [jax.ShapeDtypeStruct((2, units, rows), LOWP)]
        + [jax.ShapeDtypeStruct(slot, LOWP)] * 8,
        compiler_params=pltpu.CompilerParams(vmem_limit_bytes=60 * 2**20),
        cost_estimate=cost(28),
        name="ffn",
    )(at, *pieces, grad_rows, gate_up, gate_up, down_proj)


def ffn_grads_kernel(at, dgu_ref, inner_ref, rows_ref, grad_ref, *refs):
    out_ref = refs[-1]
    width = rows_ref.shape[1]
    for first, value in ((0, dot(dgu_ref[...], rows_ref[...], 1, 0)), (width, dot(inner_ref[...], grad_ref[...], 1, 0))):
        lanes = slice(first, first + value.shape[1])
        for ref in refs[:-1]:
            value = value + ref[:, lanes].astype(F32)
        out_ref[:, lanes] = value.astype(LOWP)


def ffn_grads(half, dgu, inner, rows, grad_rows, *came):
    units, count = inner.shape
    tile = units // 4
    features = rows.shape[1]
    out = pl.BlockSpec((tile, features + features // 2), lambda i, at: (i, 0))
    return pl.pallas_call(
        ffn_grads_kernel,
        grid_spec=pltpu.PrefetchScalarGridSpec(
            num_scalar_prefetch=1,
            grid=(4,),
            in_specs=[
                pl.BlockSpec((None, tile, count), lambda i, at: (at[0], i, 0)),
                pl.BlockSpec((tile, count), lambda i, at: (2 * at[0] + i % 2, 0)),
                pl.BlockSpec(rows.shape, lambda i, at: (0, 0)),
                pl.BlockSpec((count, features // 2), lambda i, at: (0, i // 2)),
            ]
            + [out] * len(came),
            out_specs=out,
        ),
        out_shape=jax.ShapeDtypeStruct((units, features + features // 2), LOWP),
        compiler_params=pltpu.CompilerParams(vmem_limit_bytes=48 * 2**20),
        cost_estimate=cost(9),
        name="ffn_grads",
    )(half, dgu, inner, rows, grad_rows, *came)


def place_ffn_kernel(where, own_ref, other_ref, two_ref, down_ref):
    def write(ref):
        width = two_ref.shape[1]
        two_ref[...] = ref[:, :width].astype(F32)
        down_ref[...] = ref[:, width:].astype(F32)

    pl.when(pl.program_id(0) < 4)(lambda: write(own_ref))
    pl.when(pl.program_id(0) >= 4)(lambda: write(other_ref))


def place_ffn(where, own, other, units, features):
    tile = units // 4
    core = lambda i, at: (at[0] + i // 4) % 2
    part = lambda i, at: i % 4
    return pl.pallas_call(
        place_ffn_kernel,
        grid_spec=pltpu.PrefetchScalarGridSpec(
            num_scalar_prefetch=1,
            grid=(8,),
            in_specs=[
                pl.BlockSpec((tile, own.shape[1]), lambda i, at: (jnp.minimum(i, 3), 0)),
                pl.BlockSpec((tile, own.shape[1]), lambda i, at: (jnp.maximum(i - 4, 0), 0)),
            ],
            out_specs=[
                pl.BlockSpec((None, tile, features), lambda i, at: (core(i, at), part(i, at), 0)),
                pl.BlockSpec((tile, features // 2), lambda i, at: (2 * core(i, at) + part(i, at) % 2, part(i, at) // 2)),
            ],
        ),
        out_shape=[jax.ShapeDtypeStruct((2, units, features), F32), jax.ShapeDtypeStruct((units, features), F32)],
        compiler_params=pltpu.CompilerParams(vmem_limit_bytes=32 * 2**20),
        cost_estimate=cost(9),
        name="place_ffn",
    )(where, own, other)


def grads_kernel(at, rows_ref, proj_ref, mixed_ref, attn_ref, *refs):
    out_ref = refs[-1]
    came = [ref[...].astype(F32) for ref in refs[:-1]]

    def write(value, first):
        for more in came:
            value = value + more[first : first + value.shape[0]]
        out_ref[first : first + value.shape[0], :] = value.astype(LOWP)

    @pl.when(pl.program_id(0) < pl.num_programs(0) - 1)
    def _():
        write(dot(rows_ref[...], proj_ref[...], 0, 0), 0)

    @pl.when(pl.program_id(0) == pl.num_programs(0) - 1)
    def _():
        value = dot(mixed_ref[...], attn_ref[...], 0, 0)
        width = out_ref.shape[1]
        for i in range(2):
            write(value[:, i * width : (i + 1) * width], i * value.shape[0])


def mixer_grads(half, rows, d_mixed, mixer_rows, grad_attn, *came):
    features, width = rows.shape[1] // 2, 4 * WIDTH
    tile, steps = 256, features // 256
    heads = mixer_rows.shape[1] // 2
    out = pl.BlockSpec((tile, width), lambda i, at: (i, 0))
    return pl.pallas_call(
        grads_kernel,
        grid_spec=pltpu.PrefetchScalarGridSpec(
            num_scalar_prefetch=1,
            grid=(steps + 1,),
            in_specs=[
                pl.BlockSpec((rows.shape[0], tile), lambda i, at: (0, at[0] * steps + jnp.minimum(i, steps - 1))),
                pl.BlockSpec((rows.shape[0], width), lambda i, at: (0, 0)),
                pl.BlockSpec((rows.shape[0], heads), lambda i, at: (0, at[0])),
                pl.BlockSpec(grad_attn.shape, lambda i, at: (0, 0)),
            ]
            + [out] * len(came),
            out_specs=out,
        ),
        out_shape=jax.ShapeDtypeStruct((features + tile, width), LOWP),
        compiler_params=pltpu.CompilerParams(vmem_limit_bytes=48 * 2**20),
        cost_estimate=cost(6),
        name="mixer_grads",
    )(half, rows, d_mixed, mixer_rows, grad_attn, *came)


def place_kernel(core, part_ref, *refs):
    out_ref = refs[-1]
    width = out_ref.shape[2]
    for k in range(out_ref.shape[1]):
        out_ref[:, k, :] = part_ref[:, k * width : (k + 1) * width].astype(F32)


def place_rows(core, half, shape, *rest):
    steps = 4
    rows = shape[0] // 2 // steps
    return pl.pallas_call(
        place_kernel,
        grid_spec=pltpu.PrefetchScalarGridSpec(
            num_scalar_prefetch=1,
            grid=(steps,),
            in_specs=[pl.BlockSpec((rows, half.shape[1]), lambda i, at: (i, 0))] + [pl.BlockSpec(memory_space=pl.ANY)] * len(rest),
            out_specs=pl.BlockSpec((rows,) + shape[1:], lambda i, at: (at[0] * steps + i, 0, 0)),
        ),
        out_shape=jax.ShapeDtypeStruct(shape, F32),
        input_output_aliases={2: 0} if rest else {},
        cost_estimate=cost(5),
        name="place_rows",
    )(core, half, *rest)


def after(value, *others):
    return lax.optimization_barrier((value, others))[0]


def over_yh(part):
    return add(part, lax.ppermute(part, "yh", SWAP)).astype(LOWP)


def butterfly(value, axis, size):
    step = 1
    while step < size:
        value = value + lax.ppermute(value, axis, [(i, i ^ step) for i in range(size)])
        step *= 2
    return value


def shards(
    tokens, lengths, cotangent, attn_gain, mixer_in, rate_proj, conv_weight, decay_rate, decay_bias,
    out_gain, out_proj, ffn_gain, gate_up, down_proj,
):
    rows = tokens.shape[2]
    micros = tokens.shape[1]
    z, yl = lax.axis_index("z"), lax.axis_index("yl")
    places = (2 * z + yl) * rows + jnp.arange(rows, dtype=jnp.int32)
    block = jnp.arange(8, dtype=jnp.int32)
    slots = 2 * ((block // 2 - z) % 4) + (block % 2 + yl) % 2

    width = mixer_in.shape[1] * mixer_in.shape[2]
    both_in = gate_up.transpose(1, 2, 0)
    dec = jnp.pad(jnp.stack([decay_rate, decay_bias]), ((0, 0), (0, 126)))
    gain_row = out_gain[None]

    source = tokens[0].astype(F32).reshape(-1, tokens.shape[3])
    valid = jnp.concatenate([(places < lengths[0, m]).astype(F32)[:, None] for m in range(micros)], axis=0)
    scale_one = rms(source)
    grad_out = cotangent[0].astype(F32).reshape(source.shape) * valid
    grad_low = grad_out.astype(LOWP)
    swap = lambda a: lax.ppermute(a, "c", SWAP)
    scatter_x = lambda a: lax.psum_scatter(a, "x", scatter_dimension=0, tiled=True)
    core = lax.axis_index("c")

    normed = (source * scale_one * attn_gain).astype(LOWP)

    def weights(start):
        parts, rates = after((mixer_in, rate_proj), start)
        rates = jnp.pad(rates.reshape(rates.shape[0], 4), ((0, 0), (0, 124)))
        return jnp.concatenate([parts.reshape(parts.shape[0], width), rates], axis=1)

    pieces, (grad_other,), w_in = gather(normed, grad_low, weights)
    pieces = after(pieces, grad_other)
    grad_rows = lax.all_gather(jnp.concatenate([grad_low, grad_other], axis=0), "z", axis=0, tiled=True)

    sums, (rows_one, mixed, mixer_rows), saved = mixer_fwd(
        slots, pieces, w_in, conv_weight, dec, gain_row, out_proj, micros
    )
    (attended,), grad_rows = scatter(sums, two=lambda _: grad_rows)
    hidden = source + attended
    scale_two = rms(hidden)
    pieces, _, _ = gather((hidden * scale_two * ffn_gain).astype(LOWP))

    rows_two, inner, inner_slots, dgu, *parts = ffn_back(z[None], pieces, grad_rows, both_in, down_proj)
    half_of = lambda core, inner, *came: ffn_grads(core[None], dgu, inner, rows_two, grad_rows, *came)
    (d_normed,), d_ffn = scatter(
        parts,
        one=half_of(1 - core, inner),
        two=swap,
        late=lambda came: half_of(core, inner, came),
    )
    d_ffn = scatter_x(d_ffn)
    d_from, d_ffn_gain = norm_back(hidden, scale_two, ffn_gain, d_normed)
    d_hidden = grad_out + d_from
    branch = dot(inner_slots, down_proj, 0, 0).astype(LOWP)
    branch = [branch[i * source.shape[0] : (i + 1) * source.shape[0]] for i in range(8)]
    pieces, _, branch = gather(d_hidden.astype(LOWP), None, lambda _: branch)
    pieces, d_ffn = phase(pieces, d_ffn)
    d_ffn = over_yh(d_ffn)

    grad_attn, d_mixed, d_conv, d_small = mixer_bwd(
        slots, pieces, mixed, conv_weight, dec, gain_row, out_proj, saved, micros
    )
    d_mixed, d_ffn = phase(d_mixed, d_ffn)
    half_of = lambda core, *came: mixer_grads(
        core[None], *(a.reshape(-1, a.shape[2]) for a in (rows_one, d_mixed, mixer_rows, grad_attn)), *came
    )
    d_ffn = lax.all_gather(d_ffn, "x", axis=0, tiled=True)
    came, parts = phase(swap(half_of(1 - core)), normed_grad(slots, d_mixed, w_in))
    (d_normed, branch), (d_ffn, d_in) = scatter(
        parts,
        branch,
        one=half_of(core, came),
        late=lambda d_in: ((d_ffn, swap(d_ffn)), scatter_x(after(d_in, d_ffn))),
    )
    layer_out = ((hidden + branch) * valid).astype(LOWP)
    d_two, d_down = place_ffn(core[None], *d_ffn, dgu.shape[1], rows_two.shape[1])
    across_yh, d_two, d_down, layer_out = phase(lax.ppermute(d_in, "yh", SWAP), d_two, d_down, layer_out)
    d_in = lax.all_gather(add(d_in, across_yh).astype(LOWP), "x", axis=0, tiled=True)
    d_rate = dot(d_mixed[:, :, width:].reshape(-1, 128), rows_one.reshape(-1, rows_one.shape[2]), 0, 0)[:4]
    d_conv, d_small = d_conv.sum(0), d_small.sum(0)
    d_from, d_attn_gain = norm_back(source, scale_one, attn_gain, d_normed)
    d_tokens = (d_hidden + d_from).astype(LOWP)

    flat = [d_rate, d_conv, d_small[:2], d_attn_gain, d_ffn_gain, d_small[2]]
    sizes = [a.size for a in flat]
    small = jnp.concatenate([a.reshape(-1) for a in flat]).reshape(-1, 128)
    small = butterfly(butterfly(butterfly(small, "c", 2), "x", 4), "yh", 2)
    own = small.reshape(-1)[: sum(sizes[:3])]
    gains = butterfly(butterfly(small[sum(sizes[:3]) // 128 :], "yl", 2), "z", 4).reshape(-1)
    d_rate = own[: sizes[0]].reshape(2, 2, -1).transpose(2, 0, 1)
    d_conv = own[sizes[0] : sizes[0] + sizes[1]].reshape(conv_weight.shape)
    d_pair = own[sizes[0] + sizes[1] :].reshape(2, 128)
    d_in, d_rate, d_conv, d_pair, gains, d_tokens = phase(d_in, d_rate, d_conv, d_pair, gains, d_tokens)

    other = swap(d_in)
    d_mixer_in, other = phase(place_rows(core[None], d_in, mixer_in.shape), other)
    d_mixer_in = place_rows(1 - core[None], other, mixer_in.shape, d_mixer_in)
    d_out = [a[4 * WIDTH :].reshape(2, -1, 4 * WIDTH).transpose(1, 0, 2).reshape(-1, 8 * WIDTH) for a in (d_in, other)]
    d_out = jnp.concatenate([jnp.where(core == 0, *d_out), jnp.where(core == 0, *d_out[::-1])], axis=0).astype(F32)
    return (
        layer_out.reshape(tokens.shape),
        d_tokens.reshape(tokens.shape),
        gains[: sizes[3]],
        d_mixer_in,
        d_rate,
        d_conv,
        d_pair[0, :2],
        d_pair[1, :2],
        gains[sizes[3] + sizes[4] :],
        d_out,
        gains[sizes[3] : sizes[3] + sizes[4]],
        d_two.transpose(2, 0, 1),
        d_down,
    )


def solution(mesh):
    fine = Mesh(mesh.devices.reshape(4, 2, 2, 4, 2), ("x", "yh", "c", "z", "yl"))
    dp, tensor = ("x", "yh", "c"), ("z", "yl")
    in_specs = (
        P(dp, None, tensor, None),
        P(dp, None),
        P(dp, None, tensor, None),
        P(),
        P(None, None, tensor),
        P(None, None, tensor),
        P(None, None, tensor),
        P(tensor),
        P(tensor),
        P(),
        P(tensor, None),
        P(),
        P(None, None, tensor),
        P(tensor, None),
    )
    out_specs = (
        P(dp, None, tensor, None),
        P(dp, None, tensor, None),
        P(),
        P(None, None, tensor),
        P(None, None, tensor),
        P(None, None, tensor),
        P(tensor),
        P(tensor),
        P(),
        P(tensor, None),
        P(),
        P(None, None, tensor),
        P(tensor, None),
    )
    return jax.shard_map(shards, mesh=fine, in_specs=in_specs, out_specs=out_specs, check_vma=False)
```

```python
import jax, jax.numpy as jnp
from jax import lax
from jax.experimental import pallas as pl
from jax.experimental.pallas import tpu as pltpu
from jax.sharding import Mesh, PartitionSpec as P

EPS = 1e-06
BLOCK = 64
HS = 128
HEADS = 2
WIDTH = HEADS * HS
F32 = jnp.float32
HIGHEST = lax.Precision.HIGHEST
HIGH = lax.Precision.HIGH
LOW = lax.Precision.DEFAULT
P_INV = HIGH
P_ST = HIGH
P_GR = HIGH
P_BST = LOW
P_BGR = LOW


def dot2(a, b, ca, cb, precision):
    return lax.dot_general(a, b, (((ca,), (cb,)), ((), ())), precision=precision, preferred_element_type=F32)


def bdot(a, b, ca, cb, precision):
    if precision == LOW:
        a, b = a.astype(jnp.bfloat16), b.astype(jnp.bfloat16)
    return jnp.stack([dot2(a[i], b[i], ca, cb, precision) for i in range(a.shape[0])])


def split_heads(rows):
    blocks = rows.shape[0] // BLOCK
    return jnp.concatenate(
        [rows[:, h * HS : (h + 1) * HS].reshape(blocks, BLOCK, HS) for h in range(HEADS)], axis=0
    )


def join_heads(stacked):
    blocks = stacked.shape[0] // HEADS
    return jnp.concatenate(
        [stacked[h * blocks : (h + 1) * blocks].reshape(blocks * BLOCK, HS) for h in range(HEADS)], axis=1
    )


def shift_down(rows, steps):
    if steps == 0:
        return rows
    place = lax.broadcasted_iota(jnp.int32, rows.shape, 0)
    return jnp.where(place >= steps, pltpu.roll(rows, steps, 0), 0.0)


def shift_up(rows, steps):
    if steps == 0:
        return rows
    size = rows.shape[0]
    place = lax.broadcasted_iota(jnp.int32, rows.shape, 0)
    return jnp.where(place < size - steps, pltpu.roll(rows, size - steps, 0), 0.0)


def sigmoid(v):
    return 1.0 / (1.0 + jnp.exp(-v))


def softplus(v):
    return jnp.maximum(v, 0.0) + jnp.log1p(jnp.exp(-jnp.abs(v)))


def convolve(rows, taps):
    out = rows * taps[3:4, :]
    for j in range(3):
        out = out + shift_down(rows, 3 - j) * taps[j : j + 1, :]
    return out


def columns(table, blocks, first):
    return jnp.concatenate(
        [table[:, first + h : first + h + 1].reshape(blocks, BLOCK, 1) for h in range(HEADS)], axis=0
    )


def rows_of(turned, first):
    return jnp.concatenate([turned[:, first + h : first + h + 1, :] for h in range(HEADS)], axis=0)


def gates(rates, decay_rate, decay_bias):
    blocks = rates.shape[0] // BLOCK
    soft = softplus(rates + decay_bias)
    logdecay = (-decay_rate * soft).reshape(blocks, BLOCK, 128)
    row = lax.broadcasted_iota(jnp.int32, (BLOCK, BLOCK), 0)
    col = lax.broadcasted_iota(jnp.int32, (BLOCK, BLOCK), 1)
    ones = (row >= col).astype(F32)
    cumul = jnp.stack([dot2(ones, logdecay[n], 1, 0, HIGHEST) for n in range(blocks)])
    update = sigmoid(rates).reshape(blocks, BLOCK, 128)
    lane = lax.broadcasted_iota(jnp.int32, (blocks, BLOCK, 128), 2)
    table = jnp.where(lane < 2, cumul, update)
    turned = jnp.stack([jnp.transpose(table[n], (1, 0)) for n in range(blocks)])
    flat = table.reshape(blocks * BLOCK, 128)
    return soft, columns(flat, blocks, 0), rows_of(turned, 0), columns(flat, blocks, 2), rows_of(turned, 2)


def activate(rows, taps):
    pre = convolve(rows, taps)
    sig = sigmoid(pre)
    return pre, sig, pre * sig


def lower_inverse(strict):
    row = lax.broadcasted_iota(jnp.int32, strict.shape, 1)
    col = lax.broadcasted_iota(jnp.int32, strict.shape, 2)
    size = 1
    inverse = jnp.where(row == col, 1.0, 0.0)
    while size < BLOCK:
        lower = jnp.where((row // (2 * size) == col // (2 * size)) & (row // size != col // size), strict, 0.0)
        if size == 1:
            inverse = inverse - lower
        else:
            inverse = inverse - bdot(inverse, bdot(lower, inverse, 2 - 1, 0, P_INV), 1, 0, P_INV)
        size *= 2
    return inverse


def parts(queries, keys, cum_c, cum_r, upd_r, precision):
    shape = (queries.shape[0], BLOCK, BLOCK)
    row = lax.broadcasted_iota(jnp.int32, shape, 1)
    col = lax.broadcasted_iota(jnp.int32, shape, 2)
    both = bdot(jnp.concatenate([keys, queries], axis=1), keys, 1, 1, precision)
    ratio = jnp.where(row >= col, jnp.exp(jnp.where(row >= col, cum_c - cum_r, 0.0)), 0.0)
    scaled = ratio * upd_r
    return row, col, scaled, ratio, both[:, :BLOCK], both[:, BLOCK:]


def unit(v):
    return lax.rsqrt(jnp.sum(v * v, -1, keepdims=True) + EPS)


def place(slots, n):
    first = (slots[n] * pl.num_programs(0) + pl.program_id(0)) * BLOCK
    return pl.ds(pl.multiple_of(first, BLOCK), BLOCK)


def in_order(slots, pieces, held, target):
    @pl.when(pl.program_id(0) == 0)
    def _():
        first = 0
        for piece in pieces:
            held[first : first + piece.shape[0], :] = piece[...]
            first += piece.shape[0]

    for n in range(target.shape[0] // BLOCK):
        target[n * BLOCK : (n + 1) * BLOCK, :] = held[place(slots, n), :]


def out_slots(held, outs):
    @pl.when(pl.program_id(0) == pl.num_programs(0) - 1)
    def _():
        size = outs[0].shape[0]
        for i, out in enumerate(outs):
            out[...] = held[i * size : (i + 1) * size, :]


def fwd_kernel(slots, *refs):
    pieces, refs = refs[:9], refs[9:]
    w_ref, conv_ref, dec_ref, gain_ref, out_w_ref, *sums, normed_ref, proj_ref, rows_ref = refs[:16]
    out_ref, err_ref, inv_ref, sk_ref, state_ref, step_ref, held_ref = refs[16:]
    width = WIDTH
    in_order(slots, pieces, held_ref, normed_ref)
    proj_ref[...] = dot2(normed_ref[...], w_ref[...], 1, 0, None)
    _, _, act_q = activate(proj_ref[:, 0:width], conv_ref[0])
    _, _, act_k = activate(proj_ref[:, width : 2 * width], conv_ref[1])
    _, _, act_v = activate(proj_ref[:, 2 * width : 3 * width], conv_ref[2])
    act_q, act_k, values = split_heads(act_q), split_heads(act_k), split_heads(act_v)
    queries = act_q * (unit(act_q) * HS**-0.5)
    keys = act_k * unit(act_k)
    _, cum_c, cum_r, upd_c, upd_r = gates(proj_ref[:, 4 * width :], dec_ref[0:1, :], dec_ref[1:2, :])
    row, col, scaled, _, kk, qk = parts(queries, keys, cum_c, cum_r, upd_r, P_GR)
    inverse = lower_inverse(jnp.where(row > col, scaled * kk, 0.0))
    inv_ref[...] = inverse
    attend = scaled * qk
    grow = jnp.exp(cum_c)
    last = cum_c[:, BLOCK - 1 :, :]
    tail = keys * (jnp.exp(last - cum_c) * upd_c)
    solved = bdot(inverse, jnp.concatenate([values, grow * keys], axis=2), 1, 0, P_ST)
    sk_ref[...] = solved[:, :, HS:]
    carried = bdot(tail, solved, 0, 0, P_ST)
    n = carried.shape[0]
    row2 = lax.broadcasted_iota(jnp.int32, (n, HS, HS), 1)
    col2 = lax.broadcasted_iota(jnp.int32, (n, HS, HS), 2)
    step = jnp.where(row2 == col2, jnp.exp(last), 0.0) - carried[:, :, HS:]
    step_ref[...] = step
    blocks = n // HEADS
    states = []
    for h in range(HEADS):
        state = jnp.zeros((HS, HS), F32)
        states.append(state)
        for i in range(blocks - 1):
            at = h * blocks + i
            state = carried[at, :, :HS] + (dot2(step[at], state, 1, 0, P_ST) if i else 0.0)
            states.append(state)
    states = jnp.stack(states)
    state_ref[...] = states
    seen = bdot(jnp.concatenate([solved[:, :, HS:], grow * queries], axis=1), states, 1, 0, P_ST)
    errors = solved[:, :, :HS] - seen[:, :BLOCK]
    err_ref[...] = errors
    outputs = seen[:, BLOCK:] + bdot(attend, errors, 1, 0, P_ST)
    out_ref[...] = outputs
    scale = lax.rsqrt(jnp.mean(outputs * outputs, -1, keepdims=True) + EPS)
    gate = proj_ref[:, 3 * width : 4 * width]
    rows = (join_heads(outputs * scale * gain_ref[...]) * (gate * sigmoid(gate))).astype(jnp.bfloat16)
    rows_ref[...] = rows
    product = dot2(rows, out_w_ref[...], 1, 0, None).astype(jnp.bfloat16)
    for n in range(blocks):
        held_ref[place(slots, n), :] = product[n * BLOCK : (n + 1) * BLOCK]
    out_slots(held_ref, sums)


def unit_back(act, d_norm, factor):
    r = unit(act)
    return factor * (r * d_norm - act * (r * r * r) * jnp.sum(d_norm * act, -1, keepdims=True))


def bwd_kernel(slots, *refs):
    pieces, refs = refs[:9], refs[9:]
    proj_ref, conv_ref, dec_ref, gain_ref, out_w_ref, out_ref, err_ref, inv_ref, sk_ref, state_ref, step_ref = refs[:11]
    grad_ref, dproj_ref, dconv_ref, dsmall_ref, held_ref = refs[11:]
    width = WIDTH
    in_order(slots, pieces, held_ref, grad_ref)
    d_rows = dot2(grad_ref[...], out_w_ref[...], 1, 1, None)
    n = err_ref.shape[0]
    blocks = n // HEADS
    rates = proj_ref[:, 4 * width :]
    pre_q, sig_q, full_q = activate(proj_ref[:, 0:width], conv_ref[0])
    pre_k, sig_k, full_k = activate(proj_ref[:, width : 2 * width], conv_ref[1])
    act_q, act_k = split_heads(full_q), split_heads(full_k)
    queries = act_q * (unit(act_q) * HS**-0.5)
    keys = act_k * unit(act_k)
    soft, cum_c, cum_r, upd_c, upd_r = gates(rates, dec_ref[0:1, :], dec_ref[1:2, :])
    row, col, scaled, ratio, kk, qk = parts(queries, keys, cum_c, cum_r, upd_r, P_BGR)
    attend = scaled * qk
    grow = jnp.exp(cum_c)
    last = cum_c[:, BLOCK - 1 :, :]
    fade = jnp.exp(last - cum_c)
    weight = fade * upd_c
    tail = keys * weight
    outputs, errors, states = out_ref[...], err_ref[...], state_ref[...]

    gate = proj_ref[:, 3 * width : 4 * width]
    sig_g = sigmoid(gate)
    scale = lax.rsqrt(jnp.mean(outputs * outputs, -1, keepdims=True) + EPS)
    gain = gain_ref[...]
    normal = outputs * scale
    d_gained = split_heads(d_rows * (gate * sig_g))
    d_gate = d_rows * join_heads(normal * gain) * (sig_g * (1.0 + gate * (1.0 - sig_g)))
    dproj_ref[:, 3 * width : 4 * width] = d_gate.astype(jnp.bfloat16)
    d_gain = jnp.sum((d_gained * normal).reshape(n * BLOCK, HS), 0, keepdims=True)
    d_normal = d_gained * gain
    d_out = scale * d_normal - outputs * (scale * scale * scale) * jnp.mean(d_normal * outputs, -1, keepdims=True)

    d_err_own = bdot(attend, d_out, 0, 0, P_BST)
    to_state = bdot(
        jnp.concatenate([grow * queries, -sk_ref[...]], axis=1),
        jnp.concatenate([d_out, d_err_own], axis=1), 0, 0, P_BST,
    )
    d_ends = [None] * n
    for h in range(HEADS):
        d_end = jnp.zeros((HS, HS), F32)
        for i in range(blocks - 1, -1, -1):
            at = h * blocks + i
            d_ends[at] = d_end
            if i:
                d_end = to_state[at] + (dot2(step_ref[at], d_end, 0, 0, P_BST) if i < blocks - 1 else 0.0)
    d_ends = jnp.stack(d_ends)
    d_err = d_err_own + bdot(tail, d_ends, 1, 0, P_BST)
    d_val = bdot(inv_ref[...], d_err, 0, 0, P_BST)
    pair = jnp.concatenate([d_out, d_val], axis=1)
    by_err = bdot(pair, errors, 1, 1, P_BGR)
    by_state = bdot(pair, states, 1, 1, P_BGR)
    d_tail = bdot(errors, d_ends, 1, 1, P_BGR)
    raw_attend = jnp.where(row >= col, by_err[:, :BLOCK], 0.0)
    raw_system = jnp.where(row > col, -by_err[:, BLOCK:], 0.0)
    d_qk = raw_attend * scaled
    d_kk = raw_system * scaled
    d_seen_q, d_seen_k = by_state[:, :BLOCK], -by_state[:, BLOCK:]
    stacked = jnp.concatenate([d_qk, d_kk], axis=1)
    from_left = bdot(stacked, keys, 1, 0, P_BGR)
    from_right = bdot(stacked, jnp.concatenate([queries, keys], axis=1), 0, 0, P_BGR)
    d_queries = grow * d_seen_q + from_left[:, :BLOCK]
    d_keys = grow * d_seen_k + weight * d_tail + from_left[:, BLOCK:] + from_right

    mixed = ratio * (raw_attend * qk + raw_system * kk)
    moved = mixed * upd_r
    eye = row == col
    over_upd = jnp.sum(mixed, 1, keepdims=True)
    tail_dot = jnp.sum(keys * d_tail, -1, keepdims=True)
    tail_part = weight * tail_dot
    d_upd = jnp.sum(jnp.where(eye, over_upd, 0.0), -1, keepdims=True) + fade * tail_dot
    d_cum = jnp.sum(moved - jnp.where(eye, over_upd * upd_r, 0.0), -1, keepdims=True)
    d_cum = d_cum + grow * jnp.sum(d_seen_q * queries + d_seen_k * keys, -1, keepdims=True) - tail_part
    d_last = jnp.sum(tail_part, 1, keepdims=True) + jnp.exp(last) * jnp.sum(
        jnp.sum(states * d_ends, 1, keepdims=True), 2, keepdims=True
    )
    ones = (lax.broadcasted_iota(jnp.int32, (BLOCK, BLOCK), 0) <= lax.broadcasted_iota(jnp.int32, (BLOCK, BLOCK), 1)).astype(F32)
    lane = lax.broadcasted_iota(jnp.int32, (blocks, BLOCK, 128), 2)
    spread = jnp.where(lane == 0, d_cum[:blocks], jnp.where(lane == 1, d_cum[blocks:], 0.0))
    d_log = jnp.stack([dot2(ones, spread[i], 1, 0, HIGHEST) for i in range(blocks)])
    d_log = d_log + jnp.where(lane == 0, d_last[:blocks], jnp.where(lane == 1, d_last[blocks:], 0.0))
    d_update = jnp.where(lane == 2, d_upd[:blocks], jnp.where(lane == 3, d_upd[blocks:], 0.0))
    d_log = d_log.reshape(blocks * BLOCK, 128)
    d_update = d_update.reshape(blocks * BLOCK, 128)
    update = sigmoid(rates)
    decay_rate, decay_bias = dec_ref[0:1, :], dec_ref[1:2, :]
    d_first = d_log * -decay_rate * sigmoid(rates + decay_bias)
    d_rates = (d_first + d_update * update * (1.0 - update)).astype(jnp.bfloat16)
    dproj_ref[:, 4 * width :] = d_rates
    small = jnp.concatenate(
        [
            jnp.sum(d_log * -soft, 0, keepdims=True),
            jnp.sum(d_first, 0, keepdims=True),
            d_gain,
            jnp.zeros((5, 128), F32),
        ],
        axis=0,
    )
    dsmall_ref[...] = small

    for c, (pre, sig, d_act) in enumerate(
        (
            (pre_q, sig_q, join_heads(unit_back(act_q, d_queries, HS**-0.5))),
            (pre_k, sig_k, join_heads(unit_back(act_k, d_keys, 1.0))),
            (None, None, join_heads(d_val)),
        )
    ):
        rows = proj_ref[:, c * width : (c + 1) * width]
        taps = conv_ref[c]
        if pre is None:
            pre, sig, _ = activate(rows, taps)
        d_pre = d_act * (sig * (1.0 + pre * (1.0 - sig)))
        d_in = d_pre * taps[3:4, :]
        sums = []
        for j in range(3):
            d_in = d_in + shift_up(d_pre, 3 - j) * taps[j : j + 1, :]
            sums.append(jnp.sum(d_pre * shift_down(rows, 3 - j), 0, keepdims=True))
        sums.append(jnp.sum(d_pre * rows, 0, keepdims=True))
        dproj_ref[:, c * width : (c + 1) * width] = d_in.astype(jnp.bfloat16)
        dconv_ref[c] = jnp.concatenate(sums, axis=0)


def whole(shape):
    return pl.BlockSpec(tuple(shape), lambda i, slots: (0,) * len(shape), pipeline_mode=pl.Buffered(1))


def each(shape):
    return pl.BlockSpec((None,) + tuple(shape[1:]), lambda i, slots: (i,) + (0,) * (len(shape) - 1))


def kernel_call(kernel, name, micros, outs, ins, held, time):
    slots, rest = ins[0], ins[1:]
    spec = lambda a: each(a.shape) if len(a.shape) > 2 and a.shape[0] == micros else whole(a.shape)
    return pl.pallas_call(
        kernel,
        grid_spec=pltpu.PrefetchScalarGridSpec(
            num_scalar_prefetch=1,
            grid=(micros,),
            in_specs=[spec(a) for a in rest],
            out_specs=[spec(o) for o in outs],
            scratch_shapes=[pltpu.VMEM(held, jnp.bfloat16)],
        ),
        out_shape=outs,
        compiler_params=pltpu.CompilerParams(vmem_limit_bytes=62 * 2**20),
        cost_estimate=cost(time),
        name=name,
    )(slots, *rest)


def mixer_fwd(slots, pieces, w_in, conv, dec, gain, out_proj, micros):
    rows, features = 8 * pieces[0].shape[0], pieces[0].shape[1]
    own = rows // micros
    n = HEADS * own // BLOCK
    low = lambda *shape: jax.ShapeDtypeStruct(shape, jnp.bfloat16)
    wide = lambda *shape: jax.ShapeDtypeStruct((micros,) + shape, F32)
    outs = [low(rows // 8, features)] * 8
    outs += [low(micros, own, features), wide(own, w_in.shape[1]), low(micros, own, WIDTH)]
    outs += [wide(n, BLOCK, HS), wide(n, BLOCK, HS), wide(n, BLOCK, BLOCK), wide(n, BLOCK, HS)]
    outs += [wide(n, HS, HS), wide(n, HS, HS)]
    ins = (slots, *pieces, w_in, conv, dec, gain, out_proj)
    done = kernel_call(fwd_kernel, "mixer_fwd", micros, outs, ins, (rows, features), 30)
    return done[:8], done[8:11], done[11:]


def mixer_bwd(slots, pieces, mixed, conv, dec, gain, out_proj, saved, micros):
    rows, features = 8 * pieces[0].shape[0], pieces[0].shape[1]
    outs = [
        jax.ShapeDtypeStruct((micros, rows // micros, features), jnp.bfloat16),
        jax.ShapeDtypeStruct(mixed.shape, jnp.bfloat16),
        jax.ShapeDtypeStruct((micros,) + conv.shape, F32),
        jax.ShapeDtypeStruct((micros, 8, 128), F32),
    ]
    ins = (slots, *pieces, mixed, conv, dec, gain, out_proj, *saved)
    return kernel_call(bwd_kernel, "mixer_bwd", micros, outs, ins, (rows, features), 32)


def normed_kernel(slots, d_ref, w_ref, *refs):
    outs, held = refs[:-1], refs[-1]
    micros, blocks, size, _ = d_ref.shape

    @pl.when(pl.program_id(0) == 0)
    def _():
        for n in range(blocks):
            for m in range(micros):
                first = pl.multiple_of((slots[n] * micros + m) * size, size)
                held[pl.ds(first, size), :] = d_ref[m, n]

    product = dot2(held[...], w_ref[...], 1, 1, None).astype(jnp.bfloat16)
    for i, out in enumerate(outs):
        out[...] = product[i * size * micros : (i + 1) * size * micros]


def normed_grad(slots, d_mixed, w_in):
    micros, own, width = d_mixed.shape
    features = w_in.shape[0]
    slot = jax.ShapeDtypeStruct((micros * own // 8, features), jnp.bfloat16)
    shape = (micros, 8, own // 8, width)
    steps = 4
    return pl.pallas_call(
        normed_kernel,
        grid_spec=pltpu.PrefetchScalarGridSpec(
            num_scalar_prefetch=1,
            grid=(steps,),
            in_specs=[
                pl.BlockSpec(shape, lambda i, slots: (0, 0, 0, 0)),
                pl.BlockSpec((features // steps, width), lambda i, slots: (i, 0)),
            ],
            out_specs=[pl.BlockSpec((slot.shape[0], features // steps), lambda i, slots: (0, i))] * 8,
            scratch_shapes=[pltpu.VMEM((micros * own, width), jnp.bfloat16)],
        ),
        out_shape=[slot] * 8,
        compiler_params=pltpu.CompilerParams(vmem_limit_bytes=48 * 2**20),
        cost_estimate=cost(8),
        name="normed_grad",
    )(slots, d_mixed.reshape(shape), w_in)


UP = [(i, (i + 1) % 4) for i in range(4)]
DOWN = [(i, (i - 1) % 4) for i in range(4)]
SWAP = [(0, 1), (1, 0)]
LOWP = jnp.bfloat16


def up(a):
    return lax.ppermute(a, "z", UP)


def down(a):
    return lax.ppermute(a, "z", DOWN)


def across(a):
    return lax.ppermute(a, "yl", SWAP)


def phase(*arrays):
    return lax.optimization_barrier(arrays)


def gather(own, aside=None, needed=None):
    half = own.shape[0] // 2
    b0, am, ap = phase(across(own), up(own), down(own))
    bm, a2, bp, needed = phase(up(b0), down(ap), across(ap), needed(b0) if needed else ())
    other = [] if aside is None else [across(after(aside, bm))]
    low, high, *other = phase(up(bm[:half]), down(bp[half:]), *other)
    return [own, b0, ap, bp, a2, low, high, am, bm], other, needed


def add(*parts):
    total = parts[0].astype(F32)
    for part in parts[1:]:
        total = total + part.astype(F32)
    return total


def scatter(*lists, one=(), two=None, late=None):
    half = lists[0][0].shape[0] // 2
    steps = [(down(b2[:half]), up(b2[half:])) for _, _, _, _, _, b2, _, _ in lists]
    steps, one = phase(steps, one)
    held = []
    for (a0, b0, ap, bp, a2, _, am, bm), (r1, r2) in zip(lists, steps):
        bm = add(bm, jnp.pad(r1, ((0, half), (0, 0)))).astype(LOWP)
        bp = add(bp, jnp.pad(r2, ((half, 0), (0, 0)))).astype(LOWP)
        held.append((a0, b0, ap, am, down(bm), up(a2), across(bp)))
    if two:
        held, one = phase(held, two(one))
    else:
        (held,) = phase(held)
    sent = []
    for a0, b0, ap, am, q1, q2, q3 in held:
        b0, ap = add(b0, q1).astype(LOWP), add(ap, q2, q3).astype(LOWP)
        sent.append((a0, across(b0), down(am), up(ap)))
    sent, one = phase(sent, late(one) if late else one)
    return [add(*parts) for parts in sent], one


def dot(a, b, ca, cb):
    return lax.dot_general(a, b, (((ca,), (cb,)), ((), ())), preferred_element_type=F32)


def rms(v):
    return lax.rsqrt(jnp.mean(v * v, -1, keepdims=True) + EPS)


def norm_back(values, scale, cube, gain, d_normed):
    weighted = d_normed * gain
    d_gain = jnp.sum(d_normed * values * scale, 0)
    d_values = scale * weighted - values * cube * jnp.mean(weighted * values, -1, keepdims=True)
    return d_values, d_gain


def ffn_kernel(at, *refs):
    pieces, (grad_ref, gate_w, up_w, down_w) = refs[:-16], refs[-16:-12]
    rows_ref, inner_ref, dgu_ref = refs[-12:-9]
    outs, total = refs[-9:-1], refs[-1]
    step = pl.program_id(0)
    quarter = grad_ref.shape[0] // 4

    @pl.when(step == 0)
    def _():
        first = 0
        for piece in pieces:
            rows_ref[first : first + piece.shape[0], :] = piece[...]
            first += piece.shape[0]

    rows = rows_ref[...]
    gate = dot(gate_w[...], rows, 1, 1)
    lift = dot(up_w[...], rows, 1, 1)
    for dz in range(4):
        lanes = slice(dz * quarter, (dz + 1) * quarter)
        place = pl.ds(pl.multiple_of(lax.rem(at[0] + dz, 4) * quarter, quarter), quarter)
        d_inner = dot(down_w[...], grad_ref[place, :], 1, 1)
        g, u = gate[:, lanes], lift[:, lanes]
        sigma = sigmoid(g)
        inner_ref[:, place] = (g * sigma * u).astype(LOWP)
        dgu_ref[0, :, lanes] = (d_inner * u * sigma * (1.0 + g * (1.0 - sigma))).astype(LOWP)
        dgu_ref[1, :, lanes] = (d_inner * g * sigma).astype(LOWP)
    both = dgu_ref[...].reshape(-1, dgu_ref.shape[2])
    weights = jnp.concatenate([gate_w[...], up_w[...]], axis=0)
    part = dot(both, weights, 0, 0)

    @pl.when(step == 0)
    def _():
        total[...] = part

    @pl.when(step == pl.num_programs(0) - 1)
    def _():
        size = outs[0].shape[0]
        done = total[...] + part
        for i, out in enumerate(outs):
            out[...] = done[i * size : (i + 1) * size].astype(LOWP)


def cost(microseconds):
    return pl.CostEstimate(flops=microseconds * 10**9, bytes_accessed=microseconds * 3 * 10**6, transcendentals=0)


def ffn_back(at, pieces, grad_rows, gate_up, down_proj):
    rows, features = grad_rows.shape
    units = down_proj.shape[0]
    tile = units // 2
    full = lambda shape: pl.BlockSpec(tuple(shape), lambda i, at: (0,) * len(shape))
    part = pl.BlockSpec((tile, features), lambda i, at: (i, 0))
    gate, lift = (pl.BlockSpec((None, tile, features), lambda i, at, k=k: (k, i, 0)) for k in range(2))
    lines = pl.BlockSpec((tile, rows), lambda i, at: (i, 0))
    pair = pl.BlockSpec((2, tile, rows), lambda i, at: (0, i, 0))
    slot = (rows // 8, features)
    return pl.pallas_call(
        ffn_kernel,
        grid_spec=pltpu.PrefetchScalarGridSpec(
            num_scalar_prefetch=1,
            grid=(2,),
            in_specs=[full(p.shape) for p in pieces] + [full(grad_rows.shape), gate, lift, part],
            out_specs=[full(grad_rows.shape), lines, pair] + [full(slot)] * 8,
            scratch_shapes=[pltpu.VMEM((rows, features), F32)],
        ),
        out_shape=[jax.ShapeDtypeStruct(grad_rows.shape, LOWP)]
        + [jax.ShapeDtypeStruct((units, rows), LOWP)]
        + [jax.ShapeDtypeStruct((2, units, rows), LOWP)]
        + [jax.ShapeDtypeStruct(slot, LOWP)] * 8,
        compiler_params=pltpu.CompilerParams(vmem_limit_bytes=60 * 2**20),
        cost_estimate=cost(28),
        name="ffn",
    )(at, *pieces, grad_rows, gate_up, gate_up, down_proj)


def ffn_grads_kernel(at, dgu_ref, inner_ref, rows_ref, grad_ref, *refs):
    out_ref = refs[-1]
    width = rows_ref.shape[1]
    for first, value in ((0, dot(dgu_ref[...], rows_ref[...], 1, 0)), (width, dot(inner_ref[...], grad_ref[...], 1, 0))):
        lanes = slice(first, first + value.shape[1])
        for ref in refs[:-1]:
            value = value + ref[:, lanes].astype(F32)
        out_ref[:, lanes] = value.astype(LOWP)


def ffn_grads(half, dgu, inner, rows, grad_rows, *came):
    units, count = inner.shape
    tile = units // 4
    features = rows.shape[1]
    out = pl.BlockSpec((tile, features + features // 2), lambda i, at: (i, 0))
    return pl.pallas_call(
        ffn_grads_kernel,
        grid_spec=pltpu.PrefetchScalarGridSpec(
            num_scalar_prefetch=1,
            grid=(4,),
            in_specs=[
                pl.BlockSpec((None, tile, count), lambda i, at: (at[0], i, 0)),
                pl.BlockSpec((tile, count), lambda i, at: (2 * at[0] + i % 2, 0)),
                pl.BlockSpec(rows.shape, lambda i, at: (0, 0)),
                pl.BlockSpec((count, features // 2), lambda i, at: (0, i // 2)),
            ]
            + [out] * len(came),
            out_specs=out,
        ),
        out_shape=jax.ShapeDtypeStruct((units, features + features // 2), LOWP),
        compiler_params=pltpu.CompilerParams(vmem_limit_bytes=48 * 2**20),
        cost_estimate=cost(9),
        name="ffn_grads",
    )(half, dgu, inner, rows, grad_rows, *came)


def place_ffn_kernel(where, own_ref, other_ref, two_ref, down_ref):
    def write(ref):
        width = two_ref.shape[1]
        two_ref[...] = ref[:, :width].astype(F32)
        down_ref[...] = ref[:, width:].astype(F32)

    pl.when(pl.program_id(0) < 4)(lambda: write(own_ref))
    pl.when(pl.program_id(0) >= 4)(lambda: write(other_ref))


def place_ffn(where, own, other, units, features):
    tile = units // 4
    core = lambda i, at: (at[0] + i // 4) % 2
    part = lambda i, at: i % 4
    return pl.pallas_call(
        place_ffn_kernel,
        grid_spec=pltpu.PrefetchScalarGridSpec(
            num_scalar_prefetch=1,
            grid=(8,),
            in_specs=[
                pl.BlockSpec((tile, own.shape[1]), lambda i, at: (jnp.minimum(i, 3), 0)),
                pl.BlockSpec((tile, own.shape[1]), lambda i, at: (jnp.maximum(i - 4, 0), 0)),
            ],
            out_specs=[
                pl.BlockSpec((None, tile, features), lambda i, at: (core(i, at), part(i, at), 0)),
                pl.BlockSpec((tile, features // 2), lambda i, at: (2 * core(i, at) + part(i, at) % 2, part(i, at) // 2)),
            ],
        ),
        out_shape=[jax.ShapeDtypeStruct((2, units, features), F32), jax.ShapeDtypeStruct((units, features), F32)],
        compiler_params=pltpu.CompilerParams(vmem_limit_bytes=32 * 2**20),
        cost_estimate=cost(9),
        name="place_ffn",
    )(where, own, other)


def grads_kernel(at, rows_ref, proj_ref, mixed_ref, attn_ref, *refs):
    came = refs[: (len(refs) - 1) // 6]
    outs, turn = refs[len(came) : -1], refs[-1]
    step = pl.program_id(0)
    turn[...] = dot(mixed_ref[...], attn_ref[...], 0, 0)
    size = turn.shape[0] // 2
    part = turn[pl.ds(pl.multiple_of(lax.rem(at[1] + step, 2) * size, size), size), :]
    value = jnp.concatenate([dot(rows_ref[...], proj_ref[...], 0, 0), part], axis=0)
    for ref in came:
        value = value + ref[...].astype(F32)
    value = value.astype(LOWP)
    if len(outs) == 1:
        outs[0][...] = value
        return
    half = value.shape[0] // 2

    def write(*pairs):
        for out, part in pairs:
            out[...] = part

    pl.when(step == 0)(lambda: write((outs[0], value)))
    pl.when(step == 1)(lambda: write((outs[1], value)))
    pl.when(step == 2)(lambda: write((outs[2], value[:half]), (outs[3], value[half:])))
    pl.when(step == 3)(lambda: write((outs[4], value)))


def mixer_grads(where, rows, d_mixed, mixer_rows, grad_attn, *came):
    features, width = rows.shape[1], 4 * WIDTH
    tile = features // 8
    heads = mixer_rows.shape[1] // 2
    size = tile + heads // 2
    part = lambda i, at: lax.rem(at[1] + i, 4)
    stacked = pl.BlockSpec((None, size, width), lambda i, at: (i, 0, 0))
    if came:
        sizes = [size, size, size // 2, size // 2, size]
        out_specs = [pl.BlockSpec((n, width), lambda i, at: (0, 0)) for n in sizes]
        out_shape = [jax.ShapeDtypeStruct((n, width), LOWP) for n in sizes]
    else:
        out_specs, out_shape = stacked, jax.ShapeDtypeStruct((4, size, width), LOWP)
    return pl.pallas_call(
        grads_kernel,
        grid_spec=pltpu.PrefetchScalarGridSpec(
            num_scalar_prefetch=1,
            grid=(4,),
            in_specs=[
                pl.BlockSpec((rows.shape[0], tile), lambda i, at: (0, at[0] * 4 + part(i, at))),
                pl.BlockSpec((rows.shape[0], width), lambda i, at: (0, 0)),
                pl.BlockSpec((rows.shape[0], heads), lambda i, at: (0, at[0])),
                pl.BlockSpec((rows.shape[0], width), lambda i, at: (0, part(i, at) // 2)),
            ]
            + [stacked] * len(came),
            out_specs=out_specs,
            scratch_shapes=[pltpu.VMEM((heads, width), F32)],
        ),
        out_shape=out_shape,
        compiler_params=pltpu.CompilerParams(vmem_limit_bytes=48 * 2**20),
        cost_estimate=cost(8),
        name="mixer_grads",
    )(where, rows, d_mixed, mixer_rows, grad_attn, *came)


def place_kernel(order, *refs):
    out_ref, low_ref = refs[-2:]
    parts = refs[:-2]
    width, tile = out_ref.shape[2], out_ref.shape[0]
    step = pl.program_id(0)

    def write(*group):
        value = jnp.concatenate([ref[...] for ref in group], axis=0) if len(group) > 1 else group[0][...]
        for k in range(out_ref.shape[1]):
            out_ref[:, k, :] = value[:tile, k * width : (k + 1) * width].astype(F32)
        low_ref[...] = value[tile:].astype(F32)

    at = 0
    done = 0
    while at < len(parts):
        size = tile + low_ref.shape[0]
        group = parts[at : at + (1 if parts[at].shape[0] == size else 2)]
        pl.when(step == done)(lambda group=group: write(*group))
        at, done = at + len(group), done + 1


def place_rows(where, parts, eighth, shape, low, *rest):
    rows = shape[0] // 8
    size = rows + low[0] // 4
    full = lambda a: pl.BlockSpec(a.shape, lambda i, at: (0, 0))
    steps = sum(p.shape[0] for p in parts) // size
    core = lambda i, at: lax.rem(eighth(i, at)[0], 2)
    x = lambda i, at: lax.rem(eighth(i, at)[1], 4)
    return pl.pallas_call(
        place_kernel if not rest else lambda at, *refs: place_kernel(at, *refs[: len(parts)], *refs[-2:]),
        grid_spec=pltpu.PrefetchScalarGridSpec(
            num_scalar_prefetch=1,
            grid=(steps,),
            in_specs=[full(p) for p in parts] + [pl.BlockSpec(memory_space=pl.ANY)] * len(rest),
            out_specs=[
                pl.BlockSpec((rows,) + shape[1:], lambda i, at: (4 * core(i, at) + x(i, at), 0, 0)),
                pl.BlockSpec((size - rows, low[1] // 2), lambda i, at: (2 * core(i, at) + lax.rem(x(i, at), 2), x(i, at) // 2)),
            ],
        ),
        out_shape=[jax.ShapeDtypeStruct(shape, F32), jax.ShapeDtypeStruct(low, F32)],
        input_output_aliases={1 + len(parts) + i: i for i in range(len(rest))},
        cost_estimate=cost(5),
        name="place_rows",
    )(where, *parts, *rest)


def after(value, *others):
    return lax.optimization_barrier((value, others))[0]


def over_yh(part):
    return add(part, lax.ppermute(part, "yh", SWAP)).astype(LOWP)


def butterfly(value, axis, size):
    step = 1
    while step < size:
        value = value + lax.ppermute(value, axis, [(i, i ^ step) for i in range(size)])
        step *= 2
    return value


def shards(
    tokens, lengths, cotangent, attn_gain, mixer_in, rate_proj, conv_weight, decay_rate, decay_bias,
    out_gain, out_proj, ffn_gain, gate_up, down_proj,
):
    rows = tokens.shape[2]
    micros = tokens.shape[1]
    z, yl = lax.axis_index("z"), lax.axis_index("yl")
    places = (2 * z + yl) * rows + jnp.arange(rows, dtype=jnp.int32)
    block = jnp.arange(8, dtype=jnp.int32)
    slots = 2 * ((block // 2 - z) % 4) + (block % 2 + yl) % 2

    width = mixer_in.shape[1] * mixer_in.shape[2]
    both_in = gate_up.transpose(1, 2, 0)
    dec = jnp.pad(jnp.stack([decay_rate, decay_bias]), ((0, 0), (0, 126)))
    gain_row = out_gain[None]

    source = tokens[0].astype(F32).reshape(-1, tokens.shape[3])
    valid = jnp.concatenate([(places < lengths[0, m]).astype(F32)[:, None] for m in range(micros)], axis=0)
    scale_one = rms(source)
    grad_out = cotangent[0].astype(F32).reshape(source.shape) * valid
    grad_low = grad_out.astype(LOWP)
    swap = lambda a: lax.ppermute(a, "c", SWAP)
    scatter_x = lambda a: lax.psum_scatter(a, "x", scatter_dimension=0, tiled=True)
    core, x = lax.axis_index("c"), lax.axis_index("x")
    where, elsewhere = jnp.stack([core, x]), jnp.stack([1 - core, x])

    normed = (source * scale_one * attn_gain).astype(LOWP)

    def weights(start):
        parts, rates = after((mixer_in, rate_proj), start)
        rates = jnp.pad(rates.reshape(rates.shape[0], 4), ((0, 0), (0, 124)))
        return jnp.concatenate([parts.reshape(parts.shape[0], width), rates], axis=1)

    pieces, (grad_other,), w_in = gather(normed, grad_low, weights)
    pieces = after(pieces, grad_other)
    grad_rows = lax.all_gather(jnp.concatenate([grad_low, grad_other], axis=0), "z", axis=0, tiled=True)

    sums, (rows_one, mixed, mixer_rows), saved = mixer_fwd(
        slots, pieces, w_in, conv_weight, dec, gain_row, out_proj, micros
    )
    (attended,), grad_rows = scatter(sums, two=lambda _: grad_rows)
    hidden = source + attended
    scale_two = rms(hidden)
    pieces, _, _ = gather((hidden * scale_two * ffn_gain).astype(LOWP))

    rows_two, inner, dgu, *parts = ffn_back(z[None], pieces, grad_rows, both_in, down_proj)
    half_of = lambda where, inner, *came: ffn_grads(where, dgu, inner, rows_two, grad_rows, *came)
    (d_normed,), d_ffn = scatter(
        parts,
        one=half_of(elsewhere, inner),
        two=swap,
        late=lambda came: half_of(where, inner, came),
    )
    d_ffn = scatter_x(d_ffn)
    d_from, d_ffn_gain = norm_back(hidden, scale_two, scale_two**3, ffn_gain, d_normed)
    d_hidden = grad_out + d_from
    branch = dot(inner, down_proj, 0, 0).astype(LOWP)
    pieces, _, branch = gather(d_hidden.astype(LOWP), None, lambda _: branch)
    pieces, d_ffn = phase(pieces, d_ffn)
    d_ffn = over_yh(d_ffn)

    grad_attn, d_mixed, d_conv, d_small = mixer_bwd(
        slots, pieces, mixed, conv_weight, dec, gain_row, out_proj, saved, micros
    )
    d_mixed, d_ffn = phase(d_mixed, d_ffn)
    half_of = lambda where, *came: mixer_grads(
        where, *(a.reshape(-1, a.shape[2]) for a in (rows_one, d_mixed, mixer_rows, grad_attn)), *came
    )
    x_up, x_down = (lambda a: lax.ppermute(a, "x", UP)), (lambda a: lax.ppermute(a, "x", DOWN))
    d_ffn = lax.all_gather(d_ffn, "x", axis=0, tiled=True)
    came, parts = phase(swap(half_of(elsewhere)), normed_grad(slots, d_mixed, w_in))

    def far(kept):
        p0, p1, p2, p2_end, p3 = kept
        r1, r3 = x_up(p2), x_down(p2_end)
        return p0, p1, r1, p3, r3

    def near(kept):
        p0, p1, r1, p3, r3 = kept
        half = r1.shape[0]
        p1 = add(p1, jnp.pad(r1, ((0, half), (0, 0)))).astype(LOWP)
        p3 = add(p3, jnp.pad(r3, ((half, 0), (0, 0)))).astype(LOWP)
        d_rate = dot(d_mixed[:, :, width:].reshape(-1, 128), rows_one.reshape(-1, rows_one.shape[2]), 0, 0)[:4]
        return (p0, x_up(p1), x_down(p3)), d_ffn, (d_rate, d_conv.sum(0), d_small.sum(0), scale_one**3)

    (d_normed,), (kept, d_ffn, (d_rate, d_conv, d_small, cube_one)) = scatter(parts, one=half_of(where, came), two=far, late=near)
    own = add(*kept).astype(LOWP)
    branch, own = phase(branch, own)
    branch = lax.psum_scatter(after(branch, d_ffn), "z", scatter_dimension=0, tiled=True)
    d_from, d_attn_gain = norm_back(source, scale_one, cube_one, attn_gain, d_normed)
    d_tokens = (d_hidden + d_from).astype(LOWP)
    flat = [d_rate, d_conv, d_small[:2], d_attn_gain, d_ffn_gain, d_small[2]]
    sizes = [a.size for a in flat]
    small = jnp.concatenate([a.reshape(-1) for a in flat]).reshape(-1, 128)
    came, d_ffn, small = phase(lax.ppermute(own, "yh", SWAP), (d_ffn, swap(d_ffn)), butterfly(butterfly(small, "c", 2), "x", 4))
    own = add(own, came).astype(LOWP)
    d_two, d_down = place_ffn(where, *d_ffn, dgu.shape[1], rows_two.shape[1])
    p3, p1, own_other, small, d_two, d_down, d_tokens = phase(
        x_up(own), x_down(own), swap(own), butterfly(small, "yh", 2), d_two, d_down, d_tokens
    )
    rates_end = sum(sizes[:3])
    half = own.shape[0] // 2
    shape, low = mixer_in.shape, out_proj.shape
    placed = place_rows(where, [own, p1, p3], lambda i, at: (at[0], at[1] + i + i // 2), shape, low)
    low_half, high_half, p1_other, p3_other, gains, branch, placed = phase(
        x_down(p1[:half]), x_up(p3[half:]), swap(p1), swap(p3), butterfly(small[rates_end // 128 :], "yl", 2), branch, placed
    )
    half = branch.shape[0] // 2
    gains, small, came, low_other, high_other, placed = phase(
        butterfly(gains, "z", 4),
        small,
        across(branch[half:]),
        swap(low_half),
        swap(high_half),
        place_rows(
            where, [own_other, p1_other, p3_other], lambda i, at: (at[0] + 1, at[1] + i + i // 2), shape, low, *placed
        ),
    )
    branch = add(branch[:half], came)
    layer_out = ((hidden + branch) * valid).astype(LOWP)
    last = [low_half, high_half, low_other, high_other]
    d_mixer_in, d_out = place_rows(where, last, lambda i, at: (at[0] + i, at[1] + 2), shape, low, *placed)
    gains = gains.reshape(-1)
    own = small.reshape(-1)[:rates_end]
    d_rate = own[: sizes[0]].reshape(2, 2, -1).transpose(2, 0, 1)
    d_conv = own[sizes[0] : sizes[0] + sizes[1]].reshape(conv_weight.shape)
    d_pair = own[sizes[0] + sizes[1] :].reshape(2, 128)
    return (
        layer_out.reshape(tokens.shape),
        d_tokens.reshape(tokens.shape),
        gains[: sizes[3]],
        d_mixer_in,
        d_rate,
        d_conv,
        d_pair[0, :2],
        d_pair[1, :2],
        gains[sizes[3] + sizes[4] :],
        d_out,
        gains[sizes[3] : sizes[3] + sizes[4]],
        d_two.transpose(2, 0, 1),
        d_down,
    )


def solution(mesh):
    fine = Mesh(mesh.devices.reshape(4, 2, 2, 4, 2), ("x", "yh", "c", "z", "yl"))
    dp, tensor = ("x", "yh", "c"), ("z", "yl")
    in_specs = (
        P(dp, None, tensor, None),
        P(dp, None),
        P(dp, None, tensor, None),
        P(),
        P(None, None, tensor),
        P(None, None, tensor),
        P(None, None, tensor),
        P(tensor),
        P(tensor),
        P(),
        P(tensor, None),
        P(),
        P(None, None, tensor),
        P(tensor, None),
    )
    out_specs = (
        P(dp, None, tensor, None),
        P(dp, None, tensor, None),
        P(),
        P(None, None, tensor),
        P(None, None, tensor),
        P(None, None, tensor),
        P(tensor),
        P(tensor),
        P(),
        P(tensor, None),
        P(),
        P(None, None, tensor),
        P(tensor, None),
    )
    return jax.shard_map(shards, mesh=fine, in_specs=in_specs, out_specs=out_specs, check_vma=False)
```

```python
import jax, jax.numpy as jnp
from jax import lax
from jax.experimental import pallas as pl
from jax.experimental.pallas import tpu as pltpu
from jax.sharding import Mesh, PartitionSpec as P

EPS = 1e-06
BLOCK = 64
HS = 128
HEADS = 2
WIDTH = HEADS * HS
F32 = jnp.float32
HIGHEST = lax.Precision.HIGHEST
HIGH = lax.Precision.HIGH
LOW = lax.Precision.DEFAULT
P_INV = HIGH
P_ST = HIGH
P_GR = HIGH
P_BST = LOW
P_BGR = LOW


def dot2(a, b, ca, cb, precision):
    return lax.dot_general(a, b, (((ca,), (cb,)), ((), ())), precision=precision, preferred_element_type=F32)


def bdot(a, b, ca, cb, precision):
    if precision == LOW:
        a, b = a.astype(jnp.bfloat16), b.astype(jnp.bfloat16)
    return jnp.stack([dot2(a[i], b[i], ca, cb, precision) for i in range(a.shape[0])])


def split_heads(rows):
    blocks = rows.shape[0] // BLOCK
    return jnp.concatenate(
        [rows[:, h * HS : (h + 1) * HS].reshape(blocks, BLOCK, HS) for h in range(HEADS)], axis=0
    )


def join_heads(stacked):
    blocks = stacked.shape[0] // HEADS
    return jnp.concatenate(
        [stacked[h * blocks : (h + 1) * blocks].reshape(blocks * BLOCK, HS) for h in range(HEADS)], axis=1
    )


def shift_down(rows, steps):
    if steps == 0:
        return rows
    place = lax.broadcasted_iota(jnp.int32, rows.shape, 0)
    return jnp.where(place >= steps, pltpu.roll(rows, steps, 0), 0.0)


def shift_up(rows, steps):
    if steps == 0:
        return rows
    size = rows.shape[0]
    place = lax.broadcasted_iota(jnp.int32, rows.shape, 0)
    return jnp.where(place < size - steps, pltpu.roll(rows, size - steps, 0), 0.0)


def sigmoid(v):
    return 1.0 / (1.0 + jnp.exp(-v))


def softplus(v):
    return jnp.maximum(v, 0.0) + jnp.log1p(jnp.exp(-jnp.abs(v)))


def convolve(rows, taps):
    out = rows * taps[3:4, :]
    for j in range(3):
        out = out + shift_down(rows, 3 - j) * taps[j : j + 1, :]
    return out


def columns(table, blocks, first):
    return jnp.concatenate(
        [table[:, first + h : first + h + 1].reshape(blocks, BLOCK, 1) for h in range(HEADS)], axis=0
    )


def rows_of(turned, first):
    return jnp.concatenate([turned[:, first + h : first + h + 1, :] for h in range(HEADS)], axis=0)


def gates(rates, decay_rate, decay_bias):
    blocks = rates.shape[0] // BLOCK
    soft = softplus(rates + decay_bias)
    logdecay = (-decay_rate * soft).reshape(blocks, BLOCK, 128)
    row = lax.broadcasted_iota(jnp.int32, (BLOCK, BLOCK), 0)
    col = lax.broadcasted_iota(jnp.int32, (BLOCK, BLOCK), 1)
    ones = (row >= col).astype(F32)
    cumul = jnp.stack([dot2(ones, logdecay[n], 1, 0, HIGHEST) for n in range(blocks)])
    update = sigmoid(rates).reshape(blocks, BLOCK, 128)
    lane = lax.broadcasted_iota(jnp.int32, (blocks, BLOCK, 128), 2)
    table = jnp.where(lane < 2, cumul, update)
    turned = jnp.stack([jnp.transpose(table[n], (1, 0)) for n in range(blocks)])
    flat = table.reshape(blocks * BLOCK, 128)
    return soft, columns(flat, blocks, 0), rows_of(turned, 0), columns(flat, blocks, 2), rows_of(turned, 2)


def activate(rows, taps):
    pre = convolve(rows, taps)
    sig = sigmoid(pre)
    return pre, sig, pre * sig


def lower_inverse(strict):
    row = lax.broadcasted_iota(jnp.int32, strict.shape, 1)
    col = lax.broadcasted_iota(jnp.int32, strict.shape, 2)
    size = 1
    inverse = jnp.where(row == col, 1.0, 0.0)
    while size < BLOCK:
        lower = jnp.where((row // (2 * size) == col // (2 * size)) & (row // size != col // size), strict, 0.0)
        if size == 1:
            inverse = inverse - lower
        else:
            inverse = inverse - bdot(inverse, bdot(lower, inverse, 2 - 1, 0, P_INV), 1, 0, P_INV)
        size *= 2
    return inverse


def parts(queries, keys, cum_c, cum_r, upd_r, precision):
    shape = (queries.shape[0], BLOCK, BLOCK)
    row = lax.broadcasted_iota(jnp.int32, shape, 1)
    col = lax.broadcasted_iota(jnp.int32, shape, 2)
    both = bdot(jnp.concatenate([keys, queries], axis=1), keys, 1, 1, precision)
    ratio = jnp.where(row >= col, jnp.exp(jnp.where(row >= col, cum_c - cum_r, 0.0)), 0.0)
    scaled = ratio * upd_r
    return row, col, scaled, ratio, both[:, :BLOCK], both[:, BLOCK:]


def unit(v):
    return lax.rsqrt(jnp.sum(v * v, -1, keepdims=True) + EPS)


def place(slots, n):
    first = (slots[n] * pl.num_programs(0) + pl.program_id(0)) * BLOCK
    return pl.ds(pl.multiple_of(first, BLOCK), BLOCK)


def in_order(slots, pieces, held, target):
    @pl.when(pl.program_id(0) == 0)
    def _():
        first = 0
        for piece in pieces:
            held[first : first + piece.shape[0], :] = piece[...]
            first += piece.shape[0]

    for n in range(target.shape[0] // BLOCK):
        target[n * BLOCK : (n + 1) * BLOCK, :] = held[place(slots, n), :]


def out_slots(held, outs):
    @pl.when(pl.program_id(0) == pl.num_programs(0) - 1)
    def _():
        size = outs[0].shape[0]
        for i, out in enumerate(outs):
            out[...] = held[i * size : (i + 1) * size, :]


def fwd_kernel(slots, *refs):
    pieces, refs = refs[:9], refs[9:]
    w_ref, conv_ref, dec_ref, gain_ref, out_w_ref, *sums, normed_ref, proj_ref, rows_ref = refs[:16]
    out_ref, err_ref, inv_ref, sk_ref, state_ref, step_ref, held_ref = refs[16:]
    width = WIDTH
    in_order(slots, pieces, held_ref, normed_ref)
    proj_ref[...] = dot2(normed_ref[...], w_ref[...], 1, 0, None)
    _, _, act_q = activate(proj_ref[:, 0:width], conv_ref[0])
    _, _, act_k = activate(proj_ref[:, width : 2 * width], conv_ref[1])
    _, _, act_v = activate(proj_ref[:, 2 * width : 3 * width], conv_ref[2])
    act_q, act_k, values = split_heads(act_q), split_heads(act_k), split_heads(act_v)
    queries = act_q * (unit(act_q) * HS**-0.5)
    keys = act_k * unit(act_k)
    _, cum_c, cum_r, upd_c, upd_r = gates(proj_ref[:, 4 * width :], dec_ref[0:1, :], dec_ref[1:2, :])
    row, col, scaled, _, kk, qk = parts(queries, keys, cum_c, cum_r, upd_r, P_GR)
    inverse = lower_inverse(jnp.where(row > col, scaled * kk, 0.0))
    inv_ref[...] = inverse
    attend = scaled * qk
    grow = jnp.exp(cum_c)
    last = cum_c[:, BLOCK - 1 :, :]
    tail = keys * (jnp.exp(last - cum_c) * upd_c)
    solved = bdot(inverse, jnp.concatenate([values, grow * keys], axis=2), 1, 0, P_ST)
    sk_ref[...] = solved[:, :, HS:]
    carried = bdot(tail, solved, 0, 0, P_ST)
    n = carried.shape[0]
    row2 = lax.broadcasted_iota(jnp.int32, (n, HS, HS), 1)
    col2 = lax.broadcasted_iota(jnp.int32, (n, HS, HS), 2)
    step = jnp.where(row2 == col2, jnp.exp(last), 0.0) - carried[:, :, HS:]
    step_ref[...] = step
    blocks = n // HEADS
    states = []
    for h in range(HEADS):
        state = jnp.zeros((HS, HS), F32)
        states.append(state)
        for i in range(blocks - 1):
            at = h * blocks + i
            state = carried[at, :, :HS] + (dot2(step[at], state, 1, 0, P_ST) if i else 0.0)
            states.append(state)
    states = jnp.stack(states)
    state_ref[...] = states
    seen = bdot(jnp.concatenate([solved[:, :, HS:], grow * queries], axis=1), states, 1, 0, P_ST)
    errors = solved[:, :, :HS] - seen[:, :BLOCK]
    err_ref[...] = errors
    outputs = seen[:, BLOCK:] + bdot(attend, errors, 1, 0, P_ST)
    out_ref[...] = outputs
    scale = lax.rsqrt(jnp.mean(outputs * outputs, -1, keepdims=True) + EPS)
    gate = proj_ref[:, 3 * width : 4 * width]
    rows = (join_heads(outputs * scale * gain_ref[...]) * (gate * sigmoid(gate))).astype(jnp.bfloat16)
    rows_ref[...] = rows
    product = dot2(rows, out_w_ref[...], 1, 0, None).astype(jnp.bfloat16)
    for n in range(blocks):
        held_ref[place(slots, n), :] = product[n * BLOCK : (n + 1) * BLOCK]
    out_slots(held_ref, sums)


def unit_back(act, d_norm, factor):
    r = unit(act)
    return factor * (r * d_norm - act * (r * r * r) * jnp.sum(d_norm * act, -1, keepdims=True))


def bwd_kernel(slots, *refs):
    pieces, refs = refs[:9], refs[9:]
    proj_ref, conv_ref, dec_ref, gain_ref, out_w_ref, out_ref, err_ref, inv_ref, sk_ref, state_ref, step_ref = refs[:11]
    grad_ref, dproj_ref, dconv_ref, dsmall_ref, held_ref = refs[11:]
    width = WIDTH
    in_order(slots, pieces, held_ref, grad_ref)
    d_rows = dot2(grad_ref[...], out_w_ref[...], 1, 1, None)
    n = err_ref.shape[0]
    blocks = n // HEADS
    rates = proj_ref[:, 4 * width :]
    pre_q, sig_q, full_q = activate(proj_ref[:, 0:width], conv_ref[0])
    pre_k, sig_k, full_k = activate(proj_ref[:, width : 2 * width], conv_ref[1])
    act_q, act_k = split_heads(full_q), split_heads(full_k)
    queries = act_q * (unit(act_q) * HS**-0.5)
    keys = act_k * unit(act_k)
    soft, cum_c, cum_r, upd_c, upd_r = gates(rates, dec_ref[0:1, :], dec_ref[1:2, :])
    row, col, scaled, ratio, kk, qk = parts(queries, keys, cum_c, cum_r, upd_r, P_BGR)
    attend = scaled * qk
    grow = jnp.exp(cum_c)
    last = cum_c[:, BLOCK - 1 :, :]
    fade = jnp.exp(last - cum_c)
    weight = fade * upd_c
    tail = keys * weight
    outputs, errors, states = out_ref[...], err_ref[...], state_ref[...]

    gate = proj_ref[:, 3 * width : 4 * width]
    sig_g = sigmoid(gate)
    scale = lax.rsqrt(jnp.mean(outputs * outputs, -1, keepdims=True) + EPS)
    gain = gain_ref[...]
    normal = outputs * scale
    d_gained = split_heads(d_rows * (gate * sig_g))
    d_gate = d_rows * join_heads(normal * gain) * (sig_g * (1.0 + gate * (1.0 - sig_g)))
    dproj_ref[:, 3 * width : 4 * width] = d_gate.astype(jnp.bfloat16)
    d_gain = jnp.sum((d_gained * normal).reshape(n * BLOCK, HS), 0, keepdims=True)
    d_normal = d_gained * gain
    d_out = scale * d_normal - outputs * (scale * scale * scale) * jnp.mean(d_normal * outputs, -1, keepdims=True)

    d_err_own = bdot(attend, d_out, 0, 0, P_BST)
    to_state = bdot(
        jnp.concatenate([grow * queries, -sk_ref[...]], axis=1),
        jnp.concatenate([d_out, d_err_own], axis=1), 0, 0, P_BST,
    )
    d_ends = [None] * n
    for h in range(HEADS):
        d_end = jnp.zeros((HS, HS), F32)
        for i in range(blocks - 1, -1, -1):
            at = h * blocks + i
            d_ends[at] = d_end
            if i:
                d_end = to_state[at] + (dot2(step_ref[at], d_end, 0, 0, P_BST) if i < blocks - 1 else 0.0)
    d_ends = jnp.stack(d_ends)
    d_err = d_err_own + bdot(tail, d_ends, 1, 0, P_BST)
    d_val = bdot(inv_ref[...], d_err, 0, 0, P_BST)
    pair = jnp.concatenate([d_out, d_val], axis=1)
    by_err = bdot(pair, errors, 1, 1, P_BGR)
    by_state = bdot(pair, states, 1, 1, P_BGR)
    d_tail = bdot(errors, d_ends, 1, 1, P_BGR)
    raw_attend = jnp.where(row >= col, by_err[:, :BLOCK], 0.0)
    raw_system = jnp.where(row > col, -by_err[:, BLOCK:], 0.0)
    d_qk = raw_attend * scaled
    d_kk = raw_system * scaled
    d_seen_q, d_seen_k = by_state[:, :BLOCK], -by_state[:, BLOCK:]
    stacked = jnp.concatenate([d_qk, d_kk], axis=1)
    from_left = bdot(stacked, keys, 1, 0, P_BGR)
    from_right = bdot(stacked, jnp.concatenate([queries, keys], axis=1), 0, 0, P_BGR)
    d_queries = grow * d_seen_q + from_left[:, :BLOCK]
    d_keys = grow * d_seen_k + weight * d_tail + from_left[:, BLOCK:] + from_right

    mixed = ratio * (raw_attend * qk + raw_system * kk)
    moved = mixed * upd_r
    eye = row == col
    over_upd = jnp.sum(mixed, 1, keepdims=True)
    tail_dot = jnp.sum(keys * d_tail, -1, keepdims=True)
    tail_part = weight * tail_dot
    d_upd = jnp.sum(jnp.where(eye, over_upd, 0.0), -1, keepdims=True) + fade * tail_dot
    d_cum = jnp.sum(moved - jnp.where(eye, over_upd * upd_r, 0.0), -1, keepdims=True)
    d_cum = d_cum + grow * jnp.sum(d_seen_q * queries + d_seen_k * keys, -1, keepdims=True) - tail_part
    d_last = jnp.sum(tail_part, 1, keepdims=True) + jnp.exp(last) * jnp.sum(
        jnp.sum(states * d_ends, 1, keepdims=True), 2, keepdims=True
    )
    ones = (lax.broadcasted_iota(jnp.int32, (BLOCK, BLOCK), 0) <= lax.broadcasted_iota(jnp.int32, (BLOCK, BLOCK), 1)).astype(F32)
    lane = lax.broadcasted_iota(jnp.int32, (blocks, BLOCK, 128), 2)
    spread = jnp.where(lane == 0, d_cum[:blocks], jnp.where(lane == 1, d_cum[blocks:], 0.0))
    d_log = jnp.stack([dot2(ones, spread[i], 1, 0, HIGHEST) for i in range(blocks)])
    d_log = d_log + jnp.where(lane == 0, d_last[:blocks], jnp.where(lane == 1, d_last[blocks:], 0.0))
    d_update = jnp.where(lane == 2, d_upd[:blocks], jnp.where(lane == 3, d_upd[blocks:], 0.0))
    d_log = d_log.reshape(blocks * BLOCK, 128)
    d_update = d_update.reshape(blocks * BLOCK, 128)
    update = sigmoid(rates)
    decay_rate, decay_bias = dec_ref[0:1, :], dec_ref[1:2, :]
    d_first = d_log * -decay_rate * sigmoid(rates + decay_bias)
    d_rates = (d_first + d_update * update * (1.0 - update)).astype(jnp.bfloat16)
    dproj_ref[:, 4 * width :] = d_rates
    small = jnp.concatenate(
        [
            jnp.sum(d_log * -soft, 0, keepdims=True),
            jnp.sum(d_first, 0, keepdims=True),
            d_gain,
            jnp.zeros((5, 128), F32),
        ],
        axis=0,
    )
    dsmall_ref[...] = small

    for c, (pre, sig, d_act) in enumerate(
        (
            (pre_q, sig_q, join_heads(unit_back(act_q, d_queries, HS**-0.5))),
            (pre_k, sig_k, join_heads(unit_back(act_k, d_keys, 1.0))),
            (None, None, join_heads(d_val)),
        )
    ):
        rows = proj_ref[:, c * width : (c + 1) * width]
        taps = conv_ref[c]
        if pre is None:
            pre, sig, _ = activate(rows, taps)
        d_pre = d_act * (sig * (1.0 + pre * (1.0 - sig)))
        d_in = d_pre * taps[3:4, :]
        sums = []
        for j in range(3):
            d_in = d_in + shift_up(d_pre, 3 - j) * taps[j : j + 1, :]
            sums.append(jnp.sum(d_pre * shift_down(rows, 3 - j), 0, keepdims=True))
        sums.append(jnp.sum(d_pre * rows, 0, keepdims=True))
        dproj_ref[:, c * width : (c + 1) * width] = d_in.astype(jnp.bfloat16)
        dconv_ref[c] = jnp.concatenate(sums, axis=0)


def whole(shape):
    return pl.BlockSpec(tuple(shape), lambda i, slots: (0,) * len(shape), pipeline_mode=pl.Buffered(1))


def each(shape):
    return pl.BlockSpec((None,) + tuple(shape[1:]), lambda i, slots: (i,) + (0,) * (len(shape) - 1))


def kernel_call(kernel, name, micros, outs, ins, held, time):
    slots, rest = ins[0], ins[1:]
    spec = lambda a: each(a.shape) if len(a.shape) > 2 and a.shape[0] == micros else whole(a.shape)
    return pl.pallas_call(
        kernel,
        grid_spec=pltpu.PrefetchScalarGridSpec(
            num_scalar_prefetch=1,
            grid=(micros,),
            in_specs=[spec(a) for a in rest],
            out_specs=[spec(o) for o in outs],
            scratch_shapes=[pltpu.VMEM(held, jnp.bfloat16)],
        ),
        out_shape=outs,
        compiler_params=pltpu.CompilerParams(vmem_limit_bytes=62 * 2**20),
        cost_estimate=cost(time),
        name=name,
    )(slots, *rest)


def mixer_fwd(slots, pieces, w_in, conv, dec, gain, out_proj, micros):
    rows, features = 8 * pieces[0].shape[0], pieces[0].shape[1]
    own = rows // micros
    n = HEADS * own // BLOCK
    low = lambda *shape: jax.ShapeDtypeStruct(shape, jnp.bfloat16)
    wide = lambda *shape: jax.ShapeDtypeStruct((micros,) + shape, F32)
    outs = [low(rows // 8, features)] * 8
    outs += [low(micros, own, features), wide(own, w_in.shape[1]), low(micros, own, WIDTH)]
    outs += [wide(n, BLOCK, HS), wide(n, BLOCK, HS), wide(n, BLOCK, BLOCK), wide(n, BLOCK, HS)]
    outs += [wide(n, HS, HS), wide(n, HS, HS)]
    ins = (slots, *pieces, w_in, conv, dec, gain, out_proj)
    done = kernel_call(fwd_kernel, "mixer_fwd", micros, outs, ins, (rows, features), 30)
    return done[:8], done[8:11], done[11:]


def mixer_bwd(slots, pieces, mixed, conv, dec, gain, out_proj, saved, micros):
    rows, features = 8 * pieces[0].shape[0], pieces[0].shape[1]
    outs = [
        jax.ShapeDtypeStruct((micros, rows // micros, features), jnp.bfloat16),
        jax.ShapeDtypeStruct(mixed.shape, jnp.bfloat16),
        jax.ShapeDtypeStruct((micros,) + conv.shape, F32),
        jax.ShapeDtypeStruct((micros, 8, 128), F32),
    ]
    ins = (slots, *pieces, mixed, conv, dec, gain, out_proj, *saved)
    return kernel_call(bwd_kernel, "mixer_bwd", micros, outs, ins, (rows, features), 32)


def normed_kernel(slots, d_ref, w_ref, *refs):
    outs, held = refs[:-1], refs[-1]
    micros, blocks, size, _ = d_ref.shape

    @pl.when(pl.program_id(0) == 0)
    def _():
        for n in range(blocks):
            for m in range(micros):
                first = pl.multiple_of((slots[n] * micros + m) * size, size)
                held[pl.ds(first, size), :] = d_ref[m, n]

    product = dot2(held[...], w_ref[...], 1, 1, None).astype(jnp.bfloat16)
    for i, out in enumerate(outs):
        out[...] = product[i * size * micros : (i + 1) * size * micros]


def normed_grad(slots, d_mixed, w_in):
    micros, own, width = d_mixed.shape
    features = w_in.shape[0]
    slot = jax.ShapeDtypeStruct((micros * own // 8, features), jnp.bfloat16)
    shape = (micros, 8, own // 8, width)
    steps = 4
    return pl.pallas_call(
        normed_kernel,
        grid_spec=pltpu.PrefetchScalarGridSpec(
            num_scalar_prefetch=1,
            grid=(steps,),
            in_specs=[
                pl.BlockSpec(shape, lambda i, slots: (0, 0, 0, 0)),
                pl.BlockSpec((features // steps, width), lambda i, slots: (i, 0)),
            ],
            out_specs=[pl.BlockSpec((slot.shape[0], features // steps), lambda i, slots: (0, i))] * 8,
            scratch_shapes=[pltpu.VMEM((micros * own, width), jnp.bfloat16)],
        ),
        out_shape=[slot] * 8,
        compiler_params=pltpu.CompilerParams(vmem_limit_bytes=48 * 2**20),
        cost_estimate=cost(8),
        name="normed_grad",
    )(slots, d_mixed.reshape(shape), w_in)


UP = [(i, (i + 1) % 4) for i in range(4)]
DOWN = [(i, (i - 1) % 4) for i in range(4)]
SWAP = [(0, 1), (1, 0)]
LOWP = jnp.bfloat16


def up(a):
    return lax.ppermute(a, "z", UP)


def down(a):
    return lax.ppermute(a, "z", DOWN)


def across(a):
    return lax.ppermute(a, "yl", SWAP)


def phase(*arrays):
    return lax.optimization_barrier(arrays)


def gather(own, aside=None, needed=None):
    half = own.shape[0] // 2
    b0, am, ap = phase(across(own), up(own), down(own))
    bm, a2, bp, needed = phase(up(b0), down(ap), across(ap), needed(b0) if needed else ())
    other = [] if aside is None else [across(after(aside, bm))]
    low, high, *other = phase(up(bm[:half]), down(bp[half:]), *other)
    return [own, b0, ap, bp, a2, low, high, am, bm], other, needed


def add(*parts):
    total = parts[0].astype(F32)
    for part in parts[1:]:
        total = total + part.astype(F32)
    return total


def scatter(*lists, one=(), two=None, late=None):
    half = lists[0][0].shape[0] // 2
    steps = [(down(b2[:half]), up(b2[half:])) for _, _, _, _, _, b2, _, _ in lists]
    steps, one = phase(steps, one)
    held = []
    for (a0, b0, ap, bp, a2, _, am, bm), (r1, r2) in zip(lists, steps):
        bm = add(bm, jnp.pad(r1, ((0, half), (0, 0)))).astype(LOWP)
        bp = add(bp, jnp.pad(r2, ((half, 0), (0, 0)))).astype(LOWP)
        bm, a2, bp, am = phase(bm, a2, bp, am)
        held.append((a0, b0, ap, am, down(bm), up(a2), across(bp)))
    if two:
        held, one = phase(held, two(one))
    else:
        (held,) = phase(held)
    sent = []
    for a0, b0, ap, am, q1, q2, q3 in held:
        b0, ap, am = phase(add(b0, q1).astype(LOWP), add(ap, q2, q3).astype(LOWP), am)
        sent.append((a0, across(b0), down(am), up(ap)))
    sent, one = phase(sent, late(one) if late else one)
    return [add(*parts) for parts in sent], one


def dot(a, b, ca, cb):
    return lax.dot_general(a, b, (((ca,), (cb,)), ((), ())), preferred_element_type=F32)


def rms(v):
    return lax.rsqrt(jnp.mean(v * v, -1, keepdims=True) + EPS)


def norm_back(values, scale, cube, gain, d_normed):
    weighted = d_normed * gain
    d_gain = jnp.sum(d_normed * values * scale, 0)
    d_values = scale * weighted - values * cube * jnp.mean(weighted * values, -1, keepdims=True)
    return d_values, d_gain


def ffn_kernel(at, *refs):
    pieces, (grad_ref, gate_w, up_w, down_w) = refs[:-16], refs[-16:-12]
    rows_ref, inner_ref, dgu_ref = refs[-12:-9]
    outs, total = refs[-9:-1], refs[-1]
    step = pl.program_id(0)
    quarter = grad_ref.shape[0] // 4

    @pl.when(step == 0)
    def _():
        first = 0
        for piece in pieces:
            rows_ref[first : first + piece.shape[0], :] = piece[...]
            first += piece.shape[0]

    rows = rows_ref[...]
    gate = dot(gate_w[...], rows, 1, 1)
    lift = dot(up_w[...], rows, 1, 1)
    for dz in range(4):
        lanes = slice(dz * quarter, (dz + 1) * quarter)
        place = pl.ds(pl.multiple_of(lax.rem(at[0] + dz, 4) * quarter, quarter), quarter)
        d_inner = dot(down_w[...], grad_ref[place, :], 1, 1)
        g, u = gate[:, lanes], lift[:, lanes]
        sigma = sigmoid(g)
        inner_ref[:, place] = (g * sigma * u).astype(LOWP)
        dgu_ref[0, :, lanes] = (d_inner * u * sigma * (1.0 + g * (1.0 - sigma))).astype(LOWP)
        dgu_ref[1, :, lanes] = (d_inner * g * sigma).astype(LOWP)
    both = dgu_ref[...].reshape(-1, dgu_ref.shape[2])
    weights = jnp.concatenate([gate_w[...], up_w[...]], axis=0)
    part = dot(both, weights, 0, 0)

    @pl.when(step == 0)
    def _():
        total[...] = part

    @pl.when(step == pl.num_programs(0) - 1)
    def _():
        size = outs[0].shape[0]
        done = total[...] + part
        for i, out in enumerate(outs):
            out[...] = done[i * size : (i + 1) * size].astype(LOWP)


def cost(microseconds):
    return pl.CostEstimate(flops=microseconds * 10**9, bytes_accessed=microseconds * 3 * 10**6, transcendentals=0)


def ffn_back(at, pieces, grad_rows, gate_up, down_proj):
    rows, features = grad_rows.shape
    units = down_proj.shape[0]
    tile = units // 2
    full = lambda shape: pl.BlockSpec(tuple(shape), lambda i, at: (0,) * len(shape))
    part = pl.BlockSpec((tile, features), lambda i, at: (i, 0))
    gate, lift = (pl.BlockSpec((None, tile, features), lambda i, at, k=k: (k, i, 0)) for k in range(2))
    lines = pl.BlockSpec((tile, rows), lambda i, at: (i, 0))
    pair = pl.BlockSpec((2, tile, rows), lambda i, at: (0, i, 0))
    slot = (rows // 8, features)
    return pl.pallas_call(
        ffn_kernel,
        grid_spec=pltpu.PrefetchScalarGridSpec(
            num_scalar_prefetch=1,
            grid=(2,),
            in_specs=[full(p.shape) for p in pieces] + [full(grad_rows.shape), gate, lift, part],
            out_specs=[full(grad_rows.shape), lines, pair] + [full(slot)] * 8,
            scratch_shapes=[pltpu.VMEM((rows, features), F32)],
        ),
        out_shape=[jax.ShapeDtypeStruct(grad_rows.shape, LOWP)]
        + [jax.ShapeDtypeStruct((units, rows), LOWP)]
        + [jax.ShapeDtypeStruct((2, units, rows), LOWP)]
        + [jax.ShapeDtypeStruct(slot, LOWP)] * 8,
        compiler_params=pltpu.CompilerParams(vmem_limit_bytes=60 * 2**20),
        cost_estimate=cost(28),
        name="ffn",
    )(at, *pieces, grad_rows, gate_up, gate_up, down_proj)


def ffn_grads_kernel(at, dgu_ref, inner_ref, rows_ref, grad_ref, *refs):
    out_ref = refs[-1]
    width = rows_ref.shape[1]
    for first, value in ((0, dot(dgu_ref[...], rows_ref[...], 1, 0)), (width, dot(inner_ref[...], grad_ref[...], 1, 0))):
        lanes = slice(first, first + value.shape[1])
        for ref in refs[:-1]:
            value = value + ref[:, lanes].astype(F32)
        out_ref[:, lanes] = value.astype(LOWP)


def ffn_grads(half, dgu, inner, rows, grad_rows, *came):
    units, count = inner.shape
    tile = units // 4
    features = rows.shape[1]
    out = pl.BlockSpec((tile, features + features // 2), lambda i, at: (i, 0))
    return pl.pallas_call(
        ffn_grads_kernel,
        grid_spec=pltpu.PrefetchScalarGridSpec(
            num_scalar_prefetch=1,
            grid=(4,),
            in_specs=[
                pl.BlockSpec((None, tile, count), lambda i, at: (at[0], i, 0)),
                pl.BlockSpec((tile, count), lambda i, at: (2 * at[0] + i % 2, 0)),
                pl.BlockSpec(rows.shape, lambda i, at: (0, 0)),
                pl.BlockSpec((count, features // 2), lambda i, at: (0, i // 2)),
            ]
            + [out] * len(came),
            out_specs=out,
        ),
        out_shape=jax.ShapeDtypeStruct((units, features + features // 2), LOWP),
        compiler_params=pltpu.CompilerParams(vmem_limit_bytes=48 * 2**20),
        cost_estimate=cost(9),
        name="ffn_grads",
    )(half, dgu, inner, rows, grad_rows, *came)


def place_ffn_kernel(where, own_ref, other_ref, two_ref, down_ref):
    def write(ref):
        width = two_ref.shape[1]
        two_ref[...] = ref[:, :width].astype(F32)
        down_ref[...] = ref[:, width:].astype(F32)

    pl.when(pl.program_id(0) < 4)(lambda: write(own_ref))
    pl.when(pl.program_id(0) >= 4)(lambda: write(other_ref))


def place_ffn(where, own, other, units, features):
    tile = units // 4
    core = lambda i, at: (at[0] + i // 4) % 2
    part = lambda i, at: i % 4
    return pl.pallas_call(
        place_ffn_kernel,
        grid_spec=pltpu.PrefetchScalarGridSpec(
            num_scalar_prefetch=1,
            grid=(8,),
            in_specs=[
                pl.BlockSpec((tile, own.shape[1]), lambda i, at: (jnp.minimum(i, 3), 0)),
                pl.BlockSpec((tile, own.shape[1]), lambda i, at: (jnp.maximum(i - 4, 0), 0)),
            ],
            out_specs=[
                pl.BlockSpec((None, tile, features), lambda i, at: (core(i, at), part(i, at), 0)),
                pl.BlockSpec((tile, features // 2), lambda i, at: (2 * core(i, at) + part(i, at) % 2, part(i, at) // 2)),
            ],
        ),
        out_shape=[jax.ShapeDtypeStruct((2, units, features), F32), jax.ShapeDtypeStruct((units, features), F32)],
        compiler_params=pltpu.CompilerParams(vmem_limit_bytes=32 * 2**20),
        cost_estimate=cost(9),
        name="place_ffn",
    )(where, own, other)


def grads_kernel(at, rows_ref, proj_ref, mixed_ref, attn_ref, *refs):
    came = refs[: (len(refs) - 1) // 6]
    outs, turn = refs[len(came) : -1], refs[-1]
    step = pl.program_id(0)
    turn[...] = dot(mixed_ref[...], attn_ref[...], 0, 0)
    size = turn.shape[0] // 2
    part = turn[pl.ds(pl.multiple_of(lax.rem(at[1] + step, 2) * size, size), size), :]
    value = jnp.concatenate([dot(rows_ref[...], proj_ref[...], 0, 0), part], axis=0)
    for ref in came:
        value = value + ref[...].astype(F32)
    value = value.astype(LOWP)
    if len(outs) == 1:
        outs[0][...] = value
        return
    half = value.shape[0] // 2

    def write(*pairs):
        for out, part in pairs:
            out[...] = part

    pl.when(step == 0)(lambda: write((outs[0], value)))
    pl.when(step == 1)(lambda: write((outs[1], value)))
    pl.when(step == 2)(lambda: write((outs[2], value[:half]), (outs[3], value[half:])))
    pl.when(step == 3)(lambda: write((outs[4], value)))


def mixer_grads(where, rows, d_mixed, mixer_rows, grad_attn, *came):
    features, width = rows.shape[1], 4 * WIDTH
    tile = features // 8
    heads = mixer_rows.shape[1] // 2
    size = tile + heads // 2
    part = lambda i, at: lax.rem(at[1] + i, 4)
    stacked = pl.BlockSpec((None, size, width), lambda i, at: (i, 0, 0))
    if came:
        sizes = [size, size, size // 2, size // 2, size]
        out_specs = [pl.BlockSpec((n, width), lambda i, at: (0, 0)) for n in sizes]
        out_shape = [jax.ShapeDtypeStruct((n, width), LOWP) for n in sizes]
    else:
        out_specs, out_shape = stacked, jax.ShapeDtypeStruct((4, size, width), LOWP)
    return pl.pallas_call(
        grads_kernel,
        grid_spec=pltpu.PrefetchScalarGridSpec(
            num_scalar_prefetch=1,
            grid=(4,),
            in_specs=[
                pl.BlockSpec((rows.shape[0], tile), lambda i, at: (0, at[0] * 4 + part(i, at))),
                pl.BlockSpec((rows.shape[0], width), lambda i, at: (0, 0)),
                pl.BlockSpec((rows.shape[0], heads), lambda i, at: (0, at[0])),
                pl.BlockSpec((rows.shape[0], width), lambda i, at: (0, part(i, at) // 2)),
            ]
            + [stacked] * len(came),
            out_specs=out_specs,
            scratch_shapes=[pltpu.VMEM((heads, width), F32)],
        ),
        out_shape=out_shape,
        compiler_params=pltpu.CompilerParams(vmem_limit_bytes=48 * 2**20),
        cost_estimate=cost(8),
        name="mixer_grads",
    )(where, rows, d_mixed, mixer_rows, grad_attn, *came)


def place_kernel(order, *refs):
    out_ref, low_ref = refs[-2:]
    parts = refs[:-2]
    width, tile = out_ref.shape[2], out_ref.shape[0]
    step = pl.program_id(0)

    def write(*group):
        value = jnp.concatenate([ref[...] for ref in group], axis=0) if len(group) > 1 else group[0][...]
        for k in range(out_ref.shape[1]):
            out_ref[:, k, :] = value[:tile, k * width : (k + 1) * width].astype(F32)
        low_ref[...] = value[tile:].astype(F32)

    at = 0
    done = 0
    while at < len(parts):
        size = tile + low_ref.shape[0]
        group = parts[at : at + (1 if parts[at].shape[0] == size else 2)]
        pl.when(step == done)(lambda group=group: write(*group))
        at, done = at + len(group), done + 1


def place_rows(where, parts, eighth, shape, low, *rest):
    rows = shape[0] // 8
    size = rows + low[0] // 4
    full = lambda a: pl.BlockSpec(a.shape, lambda i, at: (0, 0))
    steps = sum(p.shape[0] for p in parts) // size
    core = lambda i, at: lax.rem(eighth(i, at)[0], 2)
    x = lambda i, at: lax.rem(eighth(i, at)[1], 4)
    return pl.pallas_call(
        place_kernel if not rest else lambda at, *refs: place_kernel(at, *refs[: len(parts)], *refs[-2:]),
        grid_spec=pltpu.PrefetchScalarGridSpec(
            num_scalar_prefetch=1,
            grid=(steps,),
            in_specs=[full(p) for p in parts] + [pl.BlockSpec(memory_space=pl.ANY)] * len(rest),
            out_specs=[
                pl.BlockSpec((rows,) + shape[1:], lambda i, at: (4 * core(i, at) + x(i, at), 0, 0)),
                pl.BlockSpec((size - rows, low[1] // 2), lambda i, at: (2 * core(i, at) + lax.rem(x(i, at), 2), x(i, at) // 2)),
            ],
        ),
        out_shape=[jax.ShapeDtypeStruct(shape, F32), jax.ShapeDtypeStruct(low, F32)],
        input_output_aliases={1 + len(parts) + i: i for i in range(len(rest))},
        cost_estimate=cost(5),
        name="place_rows",
    )(where, *parts, *rest)


def after(value, *others):
    return lax.optimization_barrier((value, others))[0]


def over_yh(part):
    return add(part, lax.ppermute(part, "yh", SWAP)).astype(LOWP)


def butterfly(value, axis, size):
    step = 1
    while step < size:
        value = value + lax.ppermute(value, axis, [(i, i ^ step) for i in range(size)])
        step *= 2
    return value


def shards(
    tokens, lengths, cotangent, attn_gain, mixer_in, rate_proj, conv_weight, decay_rate, decay_bias,
    out_gain, out_proj, ffn_gain, gate_up, down_proj,
):
    rows = tokens.shape[2]
    micros = tokens.shape[1]
    z, yl = lax.axis_index("z"), lax.axis_index("yl")
    places = (2 * z + yl) * rows + jnp.arange(rows, dtype=jnp.int32)
    block = jnp.arange(8, dtype=jnp.int32)
    slots = 2 * ((block // 2 - z) % 4) + (block % 2 + yl) % 2

    width = mixer_in.shape[1] * mixer_in.shape[2]
    both_in = gate_up.transpose(1, 2, 0)
    dec = jnp.pad(jnp.stack([decay_rate, decay_bias]), ((0, 0), (0, 126)))
    gain_row = out_gain[None]

    source = tokens[0].astype(F32).reshape(-1, tokens.shape[3])
    valid = jnp.concatenate([(places < lengths[0, m]).astype(F32)[:, None] for m in range(micros)], axis=0)
    scale_one = rms(source)
    grad_out = cotangent[0].astype(F32).reshape(source.shape) * valid
    grad_low = grad_out.astype(LOWP)
    swap = lambda a: lax.ppermute(a, "c", SWAP)
    scatter_x = lambda a: lax.psum_scatter(a, "x", scatter_dimension=0, tiled=True)
    core, x = lax.axis_index("c"), lax.axis_index("x")
    where, elsewhere = jnp.stack([core, x]), jnp.stack([1 - core, x])

    normed = (source * scale_one * attn_gain).astype(LOWP)

    def weights(start):
        parts, rates = after((mixer_in, rate_proj), start)
        rates = jnp.pad(rates.reshape(rates.shape[0], 4), ((0, 0), (0, 124)))
        return jnp.concatenate([parts.reshape(parts.shape[0], width), rates], axis=1)

    pieces, (grad_other,), w_in = gather(normed, grad_low, weights)
    pieces = after(pieces, grad_other)
    grad_rows = lax.all_gather(jnp.concatenate([grad_low, grad_other], axis=0), "z", axis=0, tiled=True)

    sums, (rows_one, mixed, mixer_rows), saved = mixer_fwd(
        slots, pieces, w_in, conv_weight, dec, gain_row, out_proj, micros
    )
    (attended,), grad_rows = scatter(sums, two=lambda _: grad_rows)
    hidden = source + attended
    scale_two = rms(hidden)
    pieces, _, _ = gather((hidden * scale_two * ffn_gain).astype(LOWP))

    rows_two, inner, dgu, *parts = ffn_back(z[None], pieces, grad_rows, both_in, down_proj)
    half_of = lambda where, inner, *came: ffn_grads(where, dgu, inner, rows_two, grad_rows, *came)
    (d_normed,), d_ffn = scatter(
        parts,
        one=half_of(elsewhere, inner),
        two=swap,
        late=lambda came: half_of(where, inner, came),
    )
    d_ffn = scatter_x(d_ffn)
    d_from, d_ffn_gain = norm_back(hidden, scale_two, scale_two**3, ffn_gain, d_normed)
    d_hidden = grad_out + d_from
    branch = dot(inner, down_proj, 0, 0).astype(LOWP)
    pieces, _, branch = gather(d_hidden.astype(LOWP), None, lambda _: branch)
    pieces, d_ffn = phase(pieces, d_ffn)
    d_ffn = over_yh(d_ffn)

    grad_attn, d_mixed, d_conv, d_small = mixer_bwd(
        slots, pieces, mixed, conv_weight, dec, gain_row, out_proj, saved, micros
    )
    d_mixed, d_ffn = phase(d_mixed, d_ffn)
    half_of = lambda where, *came: mixer_grads(
        where, *(a.reshape(-1, a.shape[2]) for a in (rows_one, d_mixed, mixer_rows, grad_attn)), *came
    )
    x_up, x_down = (lambda a: lax.ppermute(a, "x", UP)), (lambda a: lax.ppermute(a, "x", DOWN))
    d_ffn = lax.all_gather(d_ffn, "x", axis=0, tiled=True)
    came, parts = phase(swap(half_of(elsewhere)), normed_grad(slots, d_mixed, w_in))

    def far(kept):
        p0, p1, p2, p2_end, p3 = kept
        r1, r3 = x_up(p2), x_down(p2_end)
        return p0, p1, r1, p3, r3

    def near(kept):
        p0, p1, r1, p3, r3 = kept
        half = r1.shape[0]
        p1 = add(p1, jnp.pad(r1, ((0, half), (0, 0)))).astype(LOWP)
        p3 = add(p3, jnp.pad(r3, ((half, 0), (0, 0)))).astype(LOWP)
        d_rate = dot(d_mixed[:, :, width:].reshape(-1, 128), rows_one.reshape(-1, rows_one.shape[2]), 0, 0)[:4]
        return (p0, x_up(p1), x_down(p3)), d_ffn, (d_rate, d_conv.sum(0), d_small.sum(0), scale_one**3)

    (d_normed,), (kept, d_ffn, (d_rate, d_conv, d_small, cube_one)) = scatter(parts, one=half_of(where, came), two=far, late=near)
    own = add(*kept).astype(LOWP)
    branch, own = phase(branch, own)
    branch = lax.psum_scatter(after(branch, d_ffn), "z", scatter_dimension=0, tiled=True)
    d_from, d_attn_gain = norm_back(source, scale_one, cube_one, attn_gain, d_normed)
    d_tokens = (d_hidden + d_from).astype(LOWP)
    flat = [d_rate, d_conv, d_small[:2], d_attn_gain, d_ffn_gain, d_small[2]]
    sizes = [a.size for a in flat]
    small = jnp.concatenate([a.reshape(-1) for a in flat]).reshape(-1, 128)
    came, d_ffn, small = phase(lax.ppermute(own, "yh", SWAP), (d_ffn, swap(d_ffn)), butterfly(butterfly(small, "c", 2), "x", 4))
    own = add(own, came).astype(LOWP)
    d_two, d_down = place_ffn(where, *d_ffn, dgu.shape[1], rows_two.shape[1])
    p3, p1, own_other, small, d_two, d_down, d_tokens = phase(
        x_up(own), x_down(own), swap(own), butterfly(small, "yh", 2), d_two, d_down, d_tokens
    )
    rates_end = sum(sizes[:3])
    half = own.shape[0] // 2
    shape, low = mixer_in.shape, out_proj.shape
    placed = place_rows(where, [own, p1, p3], lambda i, at: (at[0], at[1] + i + i // 2), shape, low)
    low_half, high_half, p1_other, p3_other, gains, branch, placed = phase(
        x_down(p1[:half]), x_up(p3[half:]), swap(p1), swap(p3), butterfly(small[rates_end // 128 :], "yl", 2), branch, placed
    )
    half = branch.shape[0] // 2
    gains, small, came, low_other, high_other, placed = phase(
        butterfly(gains, "z", 4),
        small,
        across(branch[half:]),
        swap(low_half),
        swap(high_half),
        place_rows(
            where, [own_other, p1_other, p3_other], lambda i, at: (at[0] + 1, at[1] + i + i // 2), shape, low, *placed
        ),
    )
    branch = add(branch[:half], came)
    layer_out = ((hidden + branch) * valid).astype(LOWP)
    last = [low_half, high_half, low_other, high_other]
    d_mixer_in, d_out = place_rows(where, last, lambda i, at: (at[0] + i, at[1] + 2), shape, low, *placed)
    gains = gains.reshape(-1)
    own = small.reshape(-1)[:rates_end]
    d_rate = own[: sizes[0]].reshape(2, 2, -1).transpose(2, 0, 1)
    d_conv = own[sizes[0] : sizes[0] + sizes[1]].reshape(conv_weight.shape)
    d_pair = own[sizes[0] + sizes[1] :].reshape(2, 128)
    return (
        layer_out.reshape(tokens.shape),
        d_tokens.reshape(tokens.shape),
        gains[: sizes[3]],
        d_mixer_in,
        d_rate,
        d_conv,
        d_pair[0, :2],
        d_pair[1, :2],
        gains[sizes[3] + sizes[4] :],
        d_out,
        gains[sizes[3] : sizes[3] + sizes[4]],
        d_two.transpose(2, 0, 1),
        d_down,
    )


def solution(mesh):
    fine = Mesh(mesh.devices.reshape(4, 2, 2, 4, 2), ("x", "yh", "c", "z", "yl"))
    dp, tensor = ("x", "yh", "c"), ("z", "yl")
    in_specs = (
        P(dp, None, tensor, None),
        P(dp, None),
        P(dp, None, tensor, None),
        P(),
        P(None, None, tensor),
        P(None, None, tensor),
        P(None, None, tensor),
        P(tensor),
        P(tensor),
        P(),
        P(tensor, None),
        P(),
        P(None, None, tensor),
        P(tensor, None),
    )
    out_specs = (
        P(dp, None, tensor, None),
        P(dp, None, tensor, None),
        P(),
        P(None, None, tensor),
        P(None, None, tensor),
        P(None, None, tensor),
        P(tensor),
        P(tensor),
        P(),
        P(tensor, None),
        P(),
        P(None, None, tensor),
        P(tensor, None),
    )
    return jax.shard_map(shards, mesh=fine, in_specs=in_specs, out_specs=out_specs, check_vma=False)
```

```python
import jax, jax.numpy as jnp
from jax import lax
from jax.experimental import pallas as pl
from jax.experimental.pallas import tpu as pltpu
from jax.sharding import Mesh, PartitionSpec as P

EPS = 1e-06
BLOCK = 64
HS = 128
HEADS = 2
WIDTH = HEADS * HS
F32 = jnp.float32
HIGHEST = lax.Precision.HIGHEST
HIGH = lax.Precision.HIGH
LOW = lax.Precision.DEFAULT
P_INV = HIGH
P_ST = HIGH
P_OUT = LOW
P_GR = HIGH
P_BST = LOW
P_BGR = LOW


def dot2(a, b, ca, cb, precision):
    return lax.dot_general(a, b, (((ca,), (cb,)), ((), ())), precision=precision, preferred_element_type=F32)


def bdot(a, b, ca, cb, precision):
    if precision == LOW:
        a, b = a.astype(jnp.bfloat16), b.astype(jnp.bfloat16)
    return jnp.stack([dot2(a[i], b[i], ca, cb, precision) for i in range(a.shape[0])])


def split_heads(rows):
    blocks = rows.shape[0] // BLOCK
    return jnp.concatenate(
        [rows[:, h * HS : (h + 1) * HS].reshape(blocks, BLOCK, HS) for h in range(HEADS)], axis=0
    )


def join_heads(stacked):
    blocks = stacked.shape[0] // HEADS
    return jnp.concatenate(
        [stacked[h * blocks : (h + 1) * blocks].reshape(blocks * BLOCK, HS) for h in range(HEADS)], axis=1
    )


def shift_down(rows, steps):
    if steps == 0:
        return rows
    place = lax.broadcasted_iota(jnp.int32, rows.shape, 0)
    return jnp.where(place >= steps, pltpu.roll(rows, steps, 0), 0.0)


def shift_up(rows, steps):
    if steps == 0:
        return rows
    size = rows.shape[0]
    place = lax.broadcasted_iota(jnp.int32, rows.shape, 0)
    return jnp.where(place < size - steps, pltpu.roll(rows, size - steps, 0), 0.0)


def sigmoid(v):
    return 1.0 / (1.0 + jnp.exp(-v))


def softplus(v):
    return jnp.maximum(v, 0.0) + jnp.log1p(jnp.exp(-jnp.abs(v)))


def convolve(rows, taps):
    out = rows * taps[3:4, :]
    for j in range(3):
        out = out + shift_down(rows, 3 - j) * taps[j : j + 1, :]
    return out


def columns(table, blocks, first):
    return jnp.concatenate(
        [table[:, first + h : first + h + 1].reshape(blocks, BLOCK, 1) for h in range(HEADS)], axis=0
    )


def rows_of(turned, first):
    return jnp.concatenate([turned[:, first + h : first + h + 1, :] for h in range(HEADS)], axis=0)


def gates(rates, decay_rate, decay_bias):
    blocks = rates.shape[0] // BLOCK
    soft = softplus(rates + decay_bias)
    logdecay = (-decay_rate * soft).reshape(blocks, BLOCK, 128)
    row = lax.broadcasted_iota(jnp.int32, (BLOCK, BLOCK), 0)
    col = lax.broadcasted_iota(jnp.int32, (BLOCK, BLOCK), 1)
    ones = (row >= col).astype(F32)
    cumul = jnp.stack([dot2(ones, logdecay[n], 1, 0, HIGHEST) for n in range(blocks)])
    update = sigmoid(rates).reshape(blocks, BLOCK, 128)
    lane = lax.broadcasted_iota(jnp.int32, (blocks, BLOCK, 128), 2)
    table = jnp.where(lane < 2, cumul, update)
    turned = jnp.stack([jnp.transpose(table[n], (1, 0)) for n in range(blocks)])
    flat = table.reshape(blocks * BLOCK, 128)
    return soft, columns(flat, blocks, 0), rows_of(turned, 0), columns(flat, blocks, 2), rows_of(turned, 2)


def activate(rows, taps):
    pre = convolve(rows, taps)
    sig = sigmoid(pre)
    return pre, sig, pre * sig


def lower_inverse(strict):
    row = lax.broadcasted_iota(jnp.int32, strict.shape, 1)
    col = lax.broadcasted_iota(jnp.int32, strict.shape, 2)
    size = 1
    inverse = jnp.where(row == col, 1.0, 0.0)
    while size < BLOCK:
        lower = jnp.where((row // (2 * size) == col // (2 * size)) & (row // size != col // size), strict, 0.0)
        if size == 1:
            inverse = inverse - lower
        else:
            inverse = inverse - bdot(inverse, bdot(lower, inverse, 2 - 1, 0, P_INV), 1, 0, P_INV)
        size *= 2
    return inverse


def parts(queries, keys, cum_c, cum_r, upd_r, precision):
    shape = (queries.shape[0], BLOCK, BLOCK)
    row = lax.broadcasted_iota(jnp.int32, shape, 1)
    col = lax.broadcasted_iota(jnp.int32, shape, 2)
    both = bdot(jnp.concatenate([keys, queries], axis=1), keys, 1, 1, precision)
    ratio = jnp.where(row >= col, jnp.exp(jnp.where(row >= col, cum_c - cum_r, 0.0)), 0.0)
    scaled = ratio * upd_r
    return row, col, scaled, ratio, both[:, :BLOCK], both[:, BLOCK:]


def unit(v):
    return lax.rsqrt(jnp.sum(v * v, -1, keepdims=True) + EPS)


def place(slots, n):
    first = (slots[n] * pl.num_programs(0) + pl.program_id(0)) * BLOCK
    return pl.ds(pl.multiple_of(first, BLOCK), BLOCK)


def in_order(slots, pieces, held, target):
    @pl.when(pl.program_id(0) == 0)
    def _():
        first = 0
        for piece in pieces:
            held[first : first + piece.shape[0], :] = piece[...]
            first += piece.shape[0]

    for n in range(target.shape[0] // BLOCK):
        target[n * BLOCK : (n + 1) * BLOCK, :] = held[place(slots, n), :]


def out_slots(held, outs):
    @pl.when(pl.program_id(0) == pl.num_programs(0) - 1)
    def _():
        size = outs[0].shape[0]
        for i, out in enumerate(outs):
            out[...] = held[i * size : (i + 1) * size, :]


def fwd_kernel(slots, *refs):
    pieces, refs = refs[:9], refs[9:]
    w_ref, conv_ref, dec_ref, gain_ref, out_w_ref, *sums, normed_ref, proj_ref, rows_ref = refs[:16]
    out_ref, err_ref, inv_ref, sk_ref, state_ref, step_ref, held_ref = refs[16:]
    width = WIDTH
    in_order(slots, pieces, held_ref, normed_ref)
    proj_ref[...] = dot2(normed_ref[...], w_ref[...], 1, 0, None)
    _, _, act_q = activate(proj_ref[:, 0:width], conv_ref[0])
    _, _, act_k = activate(proj_ref[:, width : 2 * width], conv_ref[1])
    _, _, act_v = activate(proj_ref[:, 2 * width : 3 * width], conv_ref[2])
    act_q, act_k, values = split_heads(act_q), split_heads(act_k), split_heads(act_v)
    queries = act_q * (unit(act_q) * HS**-0.5)
    keys = act_k * unit(act_k)
    _, cum_c, cum_r, upd_c, upd_r = gates(proj_ref[:, 4 * width :], dec_ref[0:1, :], dec_ref[1:2, :])
    row, col, scaled, _, kk, qk = parts(queries, keys, cum_c, cum_r, upd_r, P_GR)
    inverse = lower_inverse(jnp.where(row > col, scaled * kk, 0.0))
    inv_ref[...] = inverse
    attend = scaled * qk
    grow = jnp.exp(cum_c)
    last = cum_c[:, BLOCK - 1 :, :]
    tail = keys * (jnp.exp(last - cum_c) * upd_c)
    solved = bdot(inverse, jnp.concatenate([values, grow * keys], axis=2), 1, 0, P_ST)
    sk_ref[...] = solved[:, :, HS:]
    carried = bdot(tail, solved, 0, 0, P_ST)
    n = carried.shape[0]
    row2 = lax.broadcasted_iota(jnp.int32, (n, HS, HS), 1)
    col2 = lax.broadcasted_iota(jnp.int32, (n, HS, HS), 2)
    step = jnp.where(row2 == col2, jnp.exp(last), 0.0) - carried[:, :, HS:]
    step_ref[...] = step
    blocks = n // HEADS
    states = []
    for h in range(HEADS):
        state = jnp.zeros((HS, HS), F32)
        states.append(state)
        for i in range(blocks - 1):
            at = h * blocks + i
            state = carried[at, :, :HS] + (dot2(step[at], state, 1, 0, P_ST) if i else 0.0)
            states.append(state)
    states = jnp.stack(states)
    state_ref[...] = states
    seen = bdot(jnp.concatenate([solved[:, :, HS:], grow * queries], axis=1), states, 1, 0, P_OUT)
    errors = solved[:, :, :HS] - seen[:, :BLOCK]
    err_ref[...] = errors
    outputs = seen[:, BLOCK:] + bdot(attend, errors, 1, 0, P_OUT)
    out_ref[...] = outputs
    scale = lax.rsqrt(jnp.mean(outputs * outputs, -1, keepdims=True) + EPS)
    gate = proj_ref[:, 3 * width : 4 * width]
    rows = (join_heads(outputs * scale * gain_ref[...]) * (gate * sigmoid(gate))).astype(jnp.bfloat16)
    rows_ref[...] = rows
    product = dot2(rows, out_w_ref[...], 1, 0, None).astype(jnp.bfloat16)
    for n in range(blocks):
        held_ref[place(slots, n), :] = product[n * BLOCK : (n + 1) * BLOCK]
    out_slots(held_ref, sums)


def unit_back(act, d_norm, factor):
    r = unit(act)
    return factor * (r * d_norm - act * (r * r * r) * jnp.sum(d_norm * act, -1, keepdims=True))


def bwd_kernel(slots, *refs):
    pieces, refs = refs[:9], refs[9:]
    proj_ref, conv_ref, dec_ref, gain_ref, out_w_ref, out_ref, err_ref, inv_ref, sk_ref, state_ref, step_ref = refs[:11]
    grad_ref, dproj_ref, dconv_ref, dsmall_ref, held_ref = refs[11:]
    width = WIDTH
    in_order(slots, pieces, held_ref, grad_ref)
    d_rows = dot2(grad_ref[...], out_w_ref[...], 1, 1, None)
    n = err_ref.shape[0]
    blocks = n // HEADS
    rates = proj_ref[:, 4 * width :]
    pre_q, sig_q, full_q = activate(proj_ref[:, 0:width], conv_ref[0])
    pre_k, sig_k, full_k = activate(proj_ref[:, width : 2 * width], conv_ref[1])
    act_q, act_k = split_heads(full_q), split_heads(full_k)
    queries = act_q * (unit(act_q) * HS**-0.5)
    keys = act_k * unit(act_k)
    soft, cum_c, cum_r, upd_c, upd_r = gates(rates, dec_ref[0:1, :], dec_ref[1:2, :])
    row, col, scaled, ratio, kk, qk = parts(queries, keys, cum_c, cum_r, upd_r, P_BGR)
    attend = scaled * qk
    grow = jnp.exp(cum_c)
    last = cum_c[:, BLOCK - 1 :, :]
    fade = jnp.exp(last - cum_c)
    weight = fade * upd_c
    tail = keys * weight
    outputs, errors, states = out_ref[...], err_ref[...], state_ref[...]

    gate = proj_ref[:, 3 * width : 4 * width]
    sig_g = sigmoid(gate)
    scale = lax.rsqrt(jnp.mean(outputs * outputs, -1, keepdims=True) + EPS)
    gain = gain_ref[...]
    normal = outputs * scale
    d_gained = split_heads(d_rows * (gate * sig_g))
    d_gate = d_rows * join_heads(normal * gain) * (sig_g * (1.0 + gate * (1.0 - sig_g)))
    dproj_ref[:, 3 * width : 4 * width] = d_gate.astype(jnp.bfloat16)
    d_gain = jnp.sum((d_gained * normal).reshape(n * BLOCK, HS), 0, keepdims=True)
    d_normal = d_gained * gain
    d_out = scale * d_normal - outputs * (scale * scale * scale) * jnp.mean(d_normal * outputs, -1, keepdims=True)

    d_err_own = bdot(attend, d_out, 0, 0, P_BST)
    to_state = bdot(
        jnp.concatenate([grow * queries, -sk_ref[...]], axis=1),
        jnp.concatenate([d_out, d_err_own], axis=1), 0, 0, P_BST,
    )
    d_ends = [None] * n
    for h in range(HEADS):
        d_end = jnp.zeros((HS, HS), F32)
        for i in range(blocks - 1, -1, -1):
            at = h * blocks + i
            d_ends[at] = d_end
            if i:
                d_end = to_state[at] + (dot2(step_ref[at], d_end, 0, 0, P_BST) if i < blocks - 1 else 0.0)
    d_ends = jnp.stack(d_ends)
    d_err = d_err_own + bdot(tail, d_ends, 1, 0, P_BST)
    d_val = bdot(inv_ref[...], d_err, 0, 0, P_BST)
    pair = jnp.concatenate([d_out, d_val], axis=1)
    by_err = bdot(pair, errors, 1, 1, P_BGR)
    by_state = bdot(pair, states, 1, 1, P_BGR)
    d_tail = bdot(errors, d_ends, 1, 1, P_BGR)
    raw_attend = jnp.where(row >= col, by_err[:, :BLOCK], 0.0)
    raw_system = jnp.where(row > col, -by_err[:, BLOCK:], 0.0)
    d_qk = raw_attend * scaled
    d_kk = raw_system * scaled
    d_seen_q, d_seen_k = by_state[:, :BLOCK], -by_state[:, BLOCK:]
    stacked = jnp.concatenate([d_qk, d_kk], axis=1)
    from_left = bdot(stacked, keys, 1, 0, P_BGR)
    from_right = bdot(stacked, jnp.concatenate([queries, keys], axis=1), 0, 0, P_BGR)
    d_queries = grow * d_seen_q + from_left[:, :BLOCK]
    d_keys = grow * d_seen_k + weight * d_tail + from_left[:, BLOCK:] + from_right

    mixed = ratio * (raw_attend * qk + raw_system * kk)
    moved = mixed * upd_r
    eye = row == col
    over_upd = jnp.sum(mixed, 1, keepdims=True)
    tail_dot = jnp.sum(keys * d_tail, -1, keepdims=True)
    tail_part = weight * tail_dot
    d_upd = jnp.sum(jnp.where(eye, over_upd, 0.0), -1, keepdims=True) + fade * tail_dot
    d_cum = jnp.sum(moved - jnp.where(eye, over_upd * upd_r, 0.0), -1, keepdims=True)
    d_cum = d_cum + grow * jnp.sum(d_seen_q * queries + d_seen_k * keys, -1, keepdims=True) - tail_part
    d_last = jnp.sum(tail_part, 1, keepdims=True) + jnp.exp(last) * jnp.sum(
        jnp.sum(states * d_ends, 1, keepdims=True), 2, keepdims=True
    )
    ones = (lax.broadcasted_iota(jnp.int32, (BLOCK, BLOCK), 0) <= lax.broadcasted_iota(jnp.int32, (BLOCK, BLOCK), 1)).astype(F32)
    lane = lax.broadcasted_iota(jnp.int32, (blocks, BLOCK, 128), 2)
    spread = jnp.where(lane == 0, d_cum[:blocks], jnp.where(lane == 1, d_cum[blocks:], 0.0))
    d_log = jnp.stack([dot2(ones, spread[i], 1, 0, HIGHEST) for i in range(blocks)])
    d_log = d_log + jnp.where(lane == 0, d_last[:blocks], jnp.where(lane == 1, d_last[blocks:], 0.0))
    d_update = jnp.where(lane == 2, d_upd[:blocks], jnp.where(lane == 3, d_upd[blocks:], 0.0))
    d_log = d_log.reshape(blocks * BLOCK, 128)
    d_update = d_update.reshape(blocks * BLOCK, 128)
    update = sigmoid(rates)
    decay_rate, decay_bias = dec_ref[0:1, :], dec_ref[1:2, :]
    d_first = d_log * -decay_rate * sigmoid(rates + decay_bias)
    d_rates = (d_first + d_update * update * (1.0 - update)).astype(jnp.bfloat16)
    dproj_ref[:, 4 * width :] = d_rates
    small = jnp.concatenate(
        [
            jnp.sum(d_log * -soft, 0, keepdims=True),
            jnp.sum(d_first, 0, keepdims=True),
            d_gain,
            jnp.zeros((5, 128), F32),
        ],
        axis=0,
    )
    dsmall_ref[...] = small

    for c, (pre, sig, d_act) in enumerate(
        (
            (pre_q, sig_q, join_heads(unit_back(act_q, d_queries, HS**-0.5))),
            (pre_k, sig_k, join_heads(unit_back(act_k, d_keys, 1.0))),
            (None, None, join_heads(d_val)),
        )
    ):
        rows = proj_ref[:, c * width : (c + 1) * width]
        taps = conv_ref[c]
        if pre is None:
            pre, sig, _ = activate(rows, taps)
        d_pre = d_act * (sig * (1.0 + pre * (1.0 - sig)))
        d_in = d_pre * taps[3:4, :]
        sums = []
        for j in range(3):
            d_in = d_in + shift_up(d_pre, 3 - j) * taps[j : j + 1, :]
            sums.append(jnp.sum(d_pre * shift_down(rows, 3 - j), 0, keepdims=True))
        sums.append(jnp.sum(d_pre * rows, 0, keepdims=True))
        dproj_ref[:, c * width : (c + 1) * width] = d_in.astype(jnp.bfloat16)
        dconv_ref[c] = jnp.concatenate(sums, axis=0)


def whole(shape):
    return pl.BlockSpec(tuple(shape), lambda i, slots: (0,) * len(shape), pipeline_mode=pl.Buffered(1))


def each(shape):
    return pl.BlockSpec((None,) + tuple(shape[1:]), lambda i, slots: (i,) + (0,) * (len(shape) - 1))


def kernel_call(kernel, name, micros, outs, ins, held, time):
    slots, rest = ins[0], ins[1:]
    spec = lambda a: each(a.shape) if len(a.shape) > 2 and a.shape[0] == micros else whole(a.shape)
    return pl.pallas_call(
        kernel,
        grid_spec=pltpu.PrefetchScalarGridSpec(
            num_scalar_prefetch=1,
            grid=(micros,),
            in_specs=[spec(a) for a in rest],
            out_specs=[spec(o) for o in outs],
            scratch_shapes=[pltpu.VMEM(held, jnp.bfloat16)],
        ),
        out_shape=outs,
        compiler_params=pltpu.CompilerParams(vmem_limit_bytes=62 * 2**20),
        cost_estimate=cost(time),
        name=name,
    )(slots, *rest)


def mixer_fwd(slots, pieces, w_in, conv, dec, gain, out_proj, micros):
    rows, features = 8 * pieces[0].shape[0], pieces[0].shape[1]
    own = rows // micros
    n = HEADS * own // BLOCK
    low = lambda *shape: jax.ShapeDtypeStruct(shape, jnp.bfloat16)
    wide = lambda *shape: jax.ShapeDtypeStruct((micros,) + shape, F32)
    outs = [low(rows // 8, features)] * 8
    outs += [low(micros, own, features), wide(own, w_in.shape[1]), low(micros, own, WIDTH)]
    outs += [wide(n, BLOCK, HS), wide(n, BLOCK, HS), wide(n, BLOCK, BLOCK), wide(n, BLOCK, HS)]
    outs += [wide(n, HS, HS), wide(n, HS, HS)]
    ins = (slots, *pieces, w_in, conv, dec, gain, out_proj)
    done = kernel_call(fwd_kernel, "mixer_fwd", micros, outs, ins, (rows, features), 30)
    return done[:8], done[8:11], done[11:]


def mixer_bwd(slots, pieces, mixed, conv, dec, gain, out_proj, saved, micros):
    rows, features = 8 * pieces[0].shape[0], pieces[0].shape[1]
    outs = [
        jax.ShapeDtypeStruct((micros, rows // micros, features), jnp.bfloat16),
        jax.ShapeDtypeStruct(mixed.shape, jnp.bfloat16),
        jax.ShapeDtypeStruct((micros,) + conv.shape, F32),
        jax.ShapeDtypeStruct((micros, 8, 128), F32),
    ]
    ins = (slots, *pieces, mixed, conv, dec, gain, out_proj, *saved)
    return kernel_call(bwd_kernel, "mixer_bwd", micros, outs, ins, (rows, features), 32)


def normed_kernel(slots, d_ref, w_ref, *refs):
    outs, held = refs[:-1], refs[-1]
    micros, blocks, size, _ = d_ref.shape

    @pl.when(pl.program_id(0) == 0)
    def _():
        for n in range(blocks):
            for m in range(micros):
                first = pl.multiple_of((slots[n] * micros + m) * size, size)
                held[pl.ds(first, size), :] = d_ref[m, n]

    product = dot2(held[...], w_ref[...], 1, 1, None).astype(jnp.bfloat16)
    for i, out in enumerate(outs):
        out[...] = product[i * size * micros : (i + 1) * size * micros]


def normed_grad(slots, d_mixed, w_in):
    micros, own, width = d_mixed.shape
    features = w_in.shape[0]
    slot = jax.ShapeDtypeStruct((micros * own // 8, features), jnp.bfloat16)
    shape = (micros, 8, own // 8, width)
    steps = 4
    return pl.pallas_call(
        normed_kernel,
        grid_spec=pltpu.PrefetchScalarGridSpec(
            num_scalar_prefetch=1,
            grid=(steps,),
            in_specs=[
                pl.BlockSpec(shape, lambda i, slots: (0, 0, 0, 0)),
                pl.BlockSpec((features // steps, width), lambda i, slots: (i, 0)),
            ],
            out_specs=[pl.BlockSpec((slot.shape[0], features // steps), lambda i, slots: (0, i))] * 8,
            scratch_shapes=[pltpu.VMEM((micros * own, width), jnp.bfloat16)],
        ),
        out_shape=[slot] * 8,
        compiler_params=pltpu.CompilerParams(vmem_limit_bytes=48 * 2**20),
        cost_estimate=cost(8),
        name="normed_grad",
    )(slots, d_mixed.reshape(shape), w_in)


UP = [(i, (i + 1) % 4) for i in range(4)]
DOWN = [(i, (i - 1) % 4) for i in range(4)]
SWAP = [(0, 1), (1, 0)]
LOWP = jnp.bfloat16


def up(a):
    return lax.ppermute(a, "z", UP)


def down(a):
    return lax.ppermute(a, "z", DOWN)


def across(a):
    return lax.ppermute(a, "yl", SWAP)


def phase(*arrays):
    return lax.optimization_barrier(arrays)


def gather(own, aside=None, needed=None):
    half = own.shape[0] // 2
    b0, am, ap = phase(across(own), up(own), down(own))
    bm, a2, bp, needed = phase(up(b0), down(ap), across(ap), needed(b0) if needed else ())
    other = [] if aside is None else [across(after(aside, bm))]
    low, high, *other = phase(up(bm[:half]), down(bp[half:]), *other)
    return [own, b0, ap, bp, a2, low, high, am, bm], other, needed


def add(*parts):
    total = parts[0].astype(F32)
    for part in parts[1:]:
        total = total + part.astype(F32)
    return total


def scatter(*lists, one=(), two=None, late=None):
    half = lists[0][0].shape[0] // 2
    steps = [(down(b2[:half]), up(b2[half:])) for _, _, _, _, _, b2, _, _ in lists]
    steps, one = phase(steps, one)
    held = []
    for (a0, b0, ap, bp, a2, _, am, bm), (r1, r2) in zip(lists, steps):
        bm = add(bm, jnp.pad(r1, ((0, half), (0, 0)))).astype(LOWP)
        bp = add(bp, jnp.pad(r2, ((half, 0), (0, 0)))).astype(LOWP)
        bm, a2, bp, am = phase(bm, a2, bp, am)
        held.append((a0, b0, ap, am, down(bm), up(a2), across(bp)))
    if two:
        held, one = phase(held, two(one))
    else:
        (held,) = phase(held)
    sent = []
    for a0, b0, ap, am, q1, q2, q3 in held:
        b0, ap, am = phase(add(b0, q1).astype(LOWP), add(ap, q2, q3).astype(LOWP), am)
        sent.append((a0, across(b0), down(am), up(ap)))
    sent, one = phase(sent, late(one) if late else one)
    return [add(*parts) for parts in sent], one


def dot(a, b, ca, cb):
    return lax.dot_general(a, b, (((ca,), (cb,)), ((), ())), preferred_element_type=F32)


def rms(v):
    return lax.rsqrt(jnp.mean(v * v, -1, keepdims=True) + EPS)


def norm_back(values, scale, cube, gain, d_normed):
    weighted = d_normed * gain
    d_gain = jnp.sum(d_normed * values * scale, 0)
    d_values = scale * weighted - values * cube * jnp.mean(weighted * values, -1, keepdims=True)
    return d_values, d_gain


def ffn_kernel(at, *refs):
    pieces, (grad_ref, gate_w, up_w, down_w) = refs[:-16], refs[-16:-12]
    rows_ref, inner_ref, dgu_ref = refs[-12:-9]
    outs, total = refs[-9:-1], refs[-1]
    step = pl.program_id(0)
    quarter = grad_ref.shape[0] // 4

    @pl.when(step == 0)
    def _():
        first = 0
        for piece in pieces:
            rows_ref[first : first + piece.shape[0], :] = piece[...]
            first += piece.shape[0]

    rows = rows_ref[...]
    gate = dot(gate_w[...], rows, 1, 1)
    lift = dot(up_w[...], rows, 1, 1)
    for dz in range(4):
        lanes = slice(dz * quarter, (dz + 1) * quarter)
        place = pl.ds(pl.multiple_of(lax.rem(at[0] + dz, 4) * quarter, quarter), quarter)
        d_inner = dot(down_w[...], grad_ref[place, :], 1, 1)
        g, u = gate[:, lanes], lift[:, lanes]
        sigma = sigmoid(g)
        inner_ref[:, place] = (g * sigma * u).astype(LOWP)
        dgu_ref[0, :, lanes] = (d_inner * u * sigma * (1.0 + g * (1.0 - sigma))).astype(LOWP)
        dgu_ref[1, :, lanes] = (d_inner * g * sigma).astype(LOWP)
    both = dgu_ref[...].reshape(-1, dgu_ref.shape[2])
    weights = jnp.concatenate([gate_w[...], up_w[...]], axis=0)
    part = dot(both, weights, 0, 0)

    @pl.when(step == 0)
    def _():
        total[...] = part

    @pl.when(step == pl.num_programs(0) - 1)
    def _():
        size = outs[0].shape[0]
        done = total[...] + part
        for i, out in enumerate(outs):
            out[...] = done[i * size : (i + 1) * size].astype(LOWP)


def cost(microseconds):
    return pl.CostEstimate(flops=microseconds * 10**9, bytes_accessed=microseconds * 3 * 10**6, transcendentals=0)


def ffn_back(at, pieces, grad_rows, gate_up, down_proj):
    rows, features = grad_rows.shape
    units = down_proj.shape[0]
    tile = units // 2
    full = lambda shape: pl.BlockSpec(tuple(shape), lambda i, at: (0,) * len(shape))
    part = pl.BlockSpec((tile, features), lambda i, at: (i, 0))
    gate, lift = (pl.BlockSpec((None, tile, features), lambda i, at, k=k: (k, i, 0)) for k in range(2))
    lines = pl.BlockSpec((tile, rows), lambda i, at: (i, 0))
    pair = pl.BlockSpec((2, tile, rows), lambda i, at: (0, i, 0))
    slot = (rows // 8, features)
    return pl.pallas_call(
        ffn_kernel,
        grid_spec=pltpu.PrefetchScalarGridSpec(
            num_scalar_prefetch=1,
            grid=(2,),
            in_specs=[full(p.shape) for p in pieces] + [full(grad_rows.shape), gate, lift, part],
            out_specs=[full(grad_rows.shape), lines, pair] + [full(slot)] * 8,
            scratch_shapes=[pltpu.VMEM((rows, features), F32)],
        ),
        out_shape=[jax.ShapeDtypeStruct(grad_rows.shape, LOWP)]
        + [jax.ShapeDtypeStruct((units, rows), LOWP)]
        + [jax.ShapeDtypeStruct((2, units, rows), LOWP)]
        + [jax.ShapeDtypeStruct(slot, LOWP)] * 8,
        compiler_params=pltpu.CompilerParams(vmem_limit_bytes=60 * 2**20),
        cost_estimate=cost(28),
        name="ffn",
    )(at, *pieces, grad_rows, gate_up, gate_up, down_proj)


def ffn_grads_kernel(at, dgu_ref, inner_ref, rows_ref, grad_ref, *refs):
    out_ref = refs[-1]
    width = rows_ref.shape[1]
    for first, value in ((0, dot(dgu_ref[...], rows_ref[...], 1, 0)), (width, dot(inner_ref[...], grad_ref[...], 1, 0))):
        lanes = slice(first, first + value.shape[1])
        for ref in refs[:-1]:
            value = value + ref[:, lanes].astype(F32)
        out_ref[:, lanes] = value.astype(LOWP)


def ffn_grads(half, dgu, inner, rows, grad_rows, *came):
    units, count = inner.shape
    tile = units // 4
    features = rows.shape[1]
    out = pl.BlockSpec((tile, features + features // 2), lambda i, at: (i, 0))
    return pl.pallas_call(
        ffn_grads_kernel,
        grid_spec=pltpu.PrefetchScalarGridSpec(
            num_scalar_prefetch=1,
            grid=(4,),
            in_specs=[
                pl.BlockSpec((None, tile, count), lambda i, at: (at[0], i, 0)),
                pl.BlockSpec((tile, count), lambda i, at: (2 * at[0] + i % 2, 0)),
                pl.BlockSpec(rows.shape, lambda i, at: (0, 0)),
                pl.BlockSpec((count, features // 2), lambda i, at: (0, i // 2)),
            ]
            + [out] * len(came),
            out_specs=out,
        ),
        out_shape=jax.ShapeDtypeStruct((units, features + features // 2), LOWP),
        compiler_params=pltpu.CompilerParams(vmem_limit_bytes=48 * 2**20),
        cost_estimate=cost(9),
        name="ffn_grads",
    )(half, dgu, inner, rows, grad_rows, *came)


def place_ffn_kernel(where, own_ref, other_ref, two_ref, down_ref):
    def write(ref):
        width = two_ref.shape[1]
        two_ref[...] = ref[:, :width].astype(F32)
        down_ref[...] = ref[:, width:].astype(F32)

    pl.when(pl.program_id(0) < 4)(lambda: write(own_ref))
    pl.when(pl.program_id(0) >= 4)(lambda: write(other_ref))


def place_ffn(where, own, other, units, features):
    tile = units // 4
    core = lambda i, at: (at[0] + i // 4) % 2
    part = lambda i, at: i % 4
    return pl.pallas_call(
        place_ffn_kernel,
        grid_spec=pltpu.PrefetchScalarGridSpec(
            num_scalar_prefetch=1,
            grid=(8,),
            in_specs=[
                pl.BlockSpec((tile, own.shape[1]), lambda i, at: (jnp.minimum(i, 3), 0)),
                pl.BlockSpec((tile, own.shape[1]), lambda i, at: (jnp.maximum(i - 4, 0), 0)),
            ],
            out_specs=[
                pl.BlockSpec((None, tile, features), lambda i, at: (core(i, at), part(i, at), 0)),
                pl.BlockSpec((tile, features // 2), lambda i, at: (2 * core(i, at) + part(i, at) % 2, part(i, at) // 2)),
            ],
        ),
        out_shape=[jax.ShapeDtypeStruct((2, units, features), F32), jax.ShapeDtypeStruct((units, features), F32)],
        compiler_params=pltpu.CompilerParams(vmem_limit_bytes=32 * 2**20),
        cost_estimate=cost(9),
        name="place_ffn",
    )(where, own, other)


def grads_kernel(at, rows_ref, proj_ref, mixed_ref, attn_ref, *refs):
    came = refs[: (len(refs) - 1) // 6]
    outs, turn = refs[len(came) : -1], refs[-1]
    step = pl.program_id(0)
    turn[...] = dot(mixed_ref[...], attn_ref[...], 0, 0)
    size = turn.shape[0] // 2
    part = turn[pl.ds(pl.multiple_of(lax.rem(at[1] + step, 2) * size, size), size), :]
    value = jnp.concatenate([dot(rows_ref[...], proj_ref[...], 0, 0), part], axis=0)
    for ref in came:
        value = value + ref[...].astype(F32)
    value = value.astype(LOWP)
    if len(outs) == 1:
        outs[0][...] = value
        return
    half = value.shape[0] // 2

    def write(*pairs):
        for out, part in pairs:
            out[...] = part

    pl.when(step == 0)(lambda: write((outs[0], value)))
    pl.when(step == 1)(lambda: write((outs[1], value)))
    pl.when(step == 2)(lambda: write((outs[2], value[:half]), (outs[3], value[half:])))
    pl.when(step == 3)(lambda: write((outs[4], value)))


def mixer_grads(where, rows, d_mixed, mixer_rows, grad_attn, *came):
    features, width = rows.shape[1], 4 * WIDTH
    tile = features // 8
    heads = mixer_rows.shape[1] // 2
    size = tile + heads // 2
    part = lambda i, at: lax.rem(at[1] + i, 4)
    stacked = pl.BlockSpec((None, size, width), lambda i, at: (i, 0, 0))
    if came:
        sizes = [size, size, size // 2, size // 2, size]
        out_specs = [pl.BlockSpec((n, width), lambda i, at: (0, 0)) for n in sizes]
        out_shape = [jax.ShapeDtypeStruct((n, width), LOWP) for n in sizes]
    else:
        out_specs, out_shape = stacked, jax.ShapeDtypeStruct((4, size, width), LOWP)
    return pl.pallas_call(
        grads_kernel,
        grid_spec=pltpu.PrefetchScalarGridSpec(
            num_scalar_prefetch=1,
            grid=(4,),
            in_specs=[
                pl.BlockSpec((rows.shape[0], tile), lambda i, at: (0, at[0] * 4 + part(i, at))),
                pl.BlockSpec((rows.shape[0], width), lambda i, at: (0, 0)),
                pl.BlockSpec((rows.shape[0], heads), lambda i, at: (0, at[0])),
                pl.BlockSpec((rows.shape[0], width), lambda i, at: (0, part(i, at) // 2)),
            ]
            + [stacked] * len(came),
            out_specs=out_specs,
            scratch_shapes=[pltpu.VMEM((heads, width), F32)],
        ),
        out_shape=out_shape,
        compiler_params=pltpu.CompilerParams(vmem_limit_bytes=48 * 2**20),
        cost_estimate=cost(8),
        name="mixer_grads",
    )(where, rows, d_mixed, mixer_rows, grad_attn, *came)


def place_kernel(order, *refs):
    out_ref, low_ref = refs[-2:]
    parts = refs[:-2]
    width, tile = out_ref.shape[2], out_ref.shape[0]
    step = pl.program_id(0)

    def write(*group):
        value = jnp.concatenate([ref[...] for ref in group], axis=0) if len(group) > 1 else group[0][...]
        for k in range(out_ref.shape[1]):
            out_ref[:, k, :] = value[:tile, k * width : (k + 1) * width].astype(F32)
        low_ref[...] = value[tile:].astype(F32)

    at = 0
    done = 0
    while at < len(parts):
        size = tile + low_ref.shape[0]
        group = parts[at : at + (1 if parts[at].shape[0] == size else 2)]
        pl.when(step == done)(lambda group=group: write(*group))
        at, done = at + len(group), done + 1


def place_rows(where, parts, eighth, shape, low, *rest):
    rows = shape[0] // 8
    size = rows + low[0] // 4
    full = lambda a: pl.BlockSpec(a.shape, lambda i, at: (0, 0))
    steps = sum(p.shape[0] for p in parts) // size
    core = lambda i, at: lax.rem(eighth(i, at)[0], 2)
    x = lambda i, at: lax.rem(eighth(i, at)[1], 4)
    return pl.pallas_call(
        place_kernel if not rest else lambda at, *refs: place_kernel(at, *refs[: len(parts)], *refs[-2:]),
        grid_spec=pltpu.PrefetchScalarGridSpec(
            num_scalar_prefetch=1,
            grid=(steps,),
            in_specs=[full(p) for p in parts] + [pl.BlockSpec(memory_space=pl.ANY)] * len(rest),
            out_specs=[
                pl.BlockSpec((rows,) + shape[1:], lambda i, at: (4 * core(i, at) + x(i, at), 0, 0)),
                pl.BlockSpec((size - rows, low[1] // 2), lambda i, at: (2 * core(i, at) + lax.rem(x(i, at), 2), x(i, at) // 2)),
            ],
        ),
        out_shape=[jax.ShapeDtypeStruct(shape, F32), jax.ShapeDtypeStruct(low, F32)],
        input_output_aliases={1 + len(parts) + i: i for i in range(len(rest))},
        cost_estimate=cost(5),
        name="place_rows",
    )(where, *parts, *rest)


def after(value, *others):
    return lax.optimization_barrier((value, others))[0]


def over_yh(part):
    return add(part, lax.ppermute(part, "yh", SWAP)).astype(LOWP)


def butterfly(value, axis, size):
    step = 1
    while step < size:
        value = value + lax.ppermute(value, axis, [(i, i ^ step) for i in range(size)])
        step *= 2
    return value


def shards(
    tokens, lengths, cotangent, attn_gain, mixer_in, rate_proj, conv_weight, decay_rate, decay_bias,
    out_gain, out_proj, ffn_gain, gate_up, down_proj,
):
    rows = tokens.shape[2]
    micros = tokens.shape[1]
    z, yl = lax.axis_index("z"), lax.axis_index("yl")
    places = (2 * z + yl) * rows + jnp.arange(rows, dtype=jnp.int32)
    block = jnp.arange(8, dtype=jnp.int32)
    slots = 2 * ((block // 2 - z) % 4) + (block % 2 + yl) % 2

    width = mixer_in.shape[1] * mixer_in.shape[2]
    both_in = gate_up.transpose(1, 2, 0)
    dec = jnp.pad(jnp.stack([decay_rate, decay_bias]), ((0, 0), (0, 126)))
    gain_row = out_gain[None]

    source = tokens[0].astype(F32).reshape(-1, tokens.shape[3])
    valid = jnp.concatenate([(places < lengths[0, m]).astype(F32)[:, None] for m in range(micros)], axis=0)
    scale_one = rms(source)
    grad_out = cotangent[0].astype(F32).reshape(source.shape) * valid
    grad_low = grad_out.astype(LOWP)
    swap = lambda a: lax.ppermute(a, "c", SWAP)
    scatter_x = lambda a: lax.psum_scatter(a, "x", scatter_dimension=0, tiled=True)
    core, x = lax.axis_index("c"), lax.axis_index("x")
    where, elsewhere = jnp.stack([core, x]), jnp.stack([1 - core, x])

    normed = (source * scale_one * attn_gain).astype(LOWP)

    def weights(start):
        parts, rates = after((mixer_in, rate_proj), start)
        rates = jnp.pad(rates.reshape(rates.shape[0], 4), ((0, 0), (0, 124)))
        return jnp.concatenate([parts.reshape(parts.shape[0], width), rates], axis=1)

    pieces, (grad_other,), w_in = gather(normed, grad_low, weights)
    pieces = after(pieces, grad_other)
    grad_rows = lax.all_gather(jnp.concatenate([grad_low, grad_other], axis=0), "z", axis=0, tiled=True)

    sums, (rows_one, mixed, mixer_rows), saved = mixer_fwd(
        slots, pieces, w_in, conv_weight, dec, gain_row, out_proj, micros
    )
    (attended,), grad_rows = scatter(sums, two=lambda _: grad_rows)
    hidden = source + attended
    scale_two = rms(hidden)
    pieces, _, _ = gather((hidden * scale_two * ffn_gain).astype(LOWP))

    rows_two, inner, dgu, *parts = ffn_back(z[None], pieces, grad_rows, both_in, down_proj)
    half_of = lambda where, inner, *came: ffn_grads(where, dgu, inner, rows_two, grad_rows, *came)
    (d_normed,), d_ffn = scatter(
        parts,
        one=half_of(elsewhere, inner),
        two=swap,
        late=lambda came: half_of(where, inner, came),
    )
    d_ffn = scatter_x(d_ffn)
    d_from, d_ffn_gain = norm_back(hidden, scale_two, scale_two**3, ffn_gain, d_normed)
    d_hidden = grad_out + d_from
    branch = dot(inner, down_proj, 0, 0).astype(LOWP)
    pieces, _, branch = gather(d_hidden.astype(LOWP), None, lambda _: branch)
    pieces, d_ffn = phase(pieces, d_ffn)
    d_ffn = over_yh(d_ffn)

    grad_attn, d_mixed, d_conv, d_small = mixer_bwd(
        slots, pieces, mixed, conv_weight, dec, gain_row, out_proj, saved, micros
    )
    d_mixed, d_ffn = phase(d_mixed, d_ffn)
    half_of = lambda where, *came: mixer_grads(
        where, *(a.reshape(-1, a.shape[2]) for a in (rows_one, d_mixed, mixer_rows, grad_attn)), *came
    )
    x_up, x_down = (lambda a: lax.ppermute(a, "x", UP)), (lambda a: lax.ppermute(a, "x", DOWN))
    d_ffn = lax.all_gather(d_ffn, "x", axis=0, tiled=True)
    came, parts = phase(swap(half_of(elsewhere)), normed_grad(slots, d_mixed, w_in))

    def far(kept):
        p0, p1, p2, p2_end, p3 = kept
        r1, r3 = x_up(p2), x_down(p2_end)
        return p0, p1, r1, p3, r3

    def near(kept):
        p0, p1, r1, p3, r3 = kept
        half = r1.shape[0]
        p1 = add(p1, jnp.pad(r1, ((0, half), (0, 0)))).astype(LOWP)
        p3 = add(p3, jnp.pad(r3, ((half, 0), (0, 0)))).astype(LOWP)
        d_rate = dot(d_mixed[:, :, width:].reshape(-1, 128), rows_one.reshape(-1, rows_one.shape[2]), 0, 0)[:4]
        return (p0, x_up(p1), x_down(p3)), d_ffn, (d_rate, d_conv.sum(0), d_small.sum(0), scale_one**3)

    (d_normed,), (kept, d_ffn, (d_rate, d_conv, d_small, cube_one)) = scatter(parts, one=half_of(where, came), two=far, late=near)
    own = add(*kept).astype(LOWP)
    branch, own = phase(branch, own)
    branch = lax.psum_scatter(after(branch, d_ffn), "z", scatter_dimension=0, tiled=True)
    d_from, d_attn_gain = norm_back(source, scale_one, cube_one, attn_gain, d_normed)
    d_tokens = (d_hidden + d_from).astype(LOWP)
    flat = [d_rate, d_conv, d_small[:2], d_attn_gain, d_ffn_gain, d_small[2]]
    sizes = [a.size for a in flat]
    small = jnp.concatenate([a.reshape(-1) for a in flat]).reshape(-1, 128)
    came, d_ffn, small = phase(lax.ppermute(own, "yh", SWAP), (d_ffn, swap(d_ffn)), butterfly(butterfly(small, "c", 2), "x", 4))
    own = add(own, came).astype(LOWP)
    d_two, d_down = place_ffn(where, *d_ffn, dgu.shape[1], rows_two.shape[1])
    p3, p1, own_other, small, d_two, d_down, d_tokens = phase(
        x_up(own), x_down(own), swap(own), butterfly(small, "yh", 2), d_two, d_down, d_tokens
    )
    rates_end = sum(sizes[:3])
    half = own.shape[0] // 2
    shape, low = mixer_in.shape, out_proj.shape
    placed = place_rows(
        where, [own, p1, p3, own_other], lambda i, at: (at[0] + i // 3, at[1] + i + i // 2), shape, low
    )
    low_half, high_half, p1_other, p3_other, gains, branch, placed = phase(
        x_down(p1[:half]), x_up(p3[half:]), swap(p1), swap(p3), butterfly(small[rates_end // 128 :], "yl", 2), branch, placed
    )
    half = branch.shape[0] // 2
    gains, small, came, low_other, high_other, placed = phase(
        butterfly(gains, "z", 4),
        small,
        across(branch[half:]),
        swap(low_half),
        swap(high_half),
        place_rows(
            where, [p1_other, p3_other], lambda i, at: (at[0] + 1, at[1] + 1 + 2 * i), shape, low, *placed
        ),
    )
    branch = add(branch[:half], came)
    layer_out = ((hidden + branch) * valid).astype(LOWP)
    last = [low_half, high_half, low_other, high_other]
    d_mixer_in, d_out = place_rows(where, last, lambda i, at: (at[0] + i, at[1] + 2), shape, low, *placed)
    gains = gains.reshape(-1)
    own = small.reshape(-1)[:rates_end]
    d_rate = own[: sizes[0]].reshape(2, 2, -1).transpose(2, 0, 1)
    d_conv = own[sizes[0] : sizes[0] + sizes[1]].reshape(conv_weight.shape)
    d_pair = own[sizes[0] + sizes[1] :].reshape(2, 128)
    return (
        layer_out.reshape(tokens.shape),
        d_tokens.reshape(tokens.shape),
        gains[: sizes[3]],
        d_mixer_in,
        d_rate,
        d_conv,
        d_pair[0, :2],
        d_pair[1, :2],
        gains[sizes[3] + sizes[4] :],
        d_out,
        gains[sizes[3] : sizes[3] + sizes[4]],
        d_two.transpose(2, 0, 1),
        d_down,
    )


def solution(mesh):
    fine = Mesh(mesh.devices.reshape(4, 2, 2, 4, 2), ("x", "yh", "c", "z", "yl"))
    dp, tensor = ("x", "yh", "c"), ("z", "yl")
    in_specs = (
        P(dp, None, tensor, None),
        P(dp, None),
        P(dp, None, tensor, None),
        P(),
        P(None, None, tensor),
        P(None, None, tensor),
        P(None, None, tensor),
        P(tensor),
        P(tensor),
        P(),
        P(tensor, None),
        P(),
        P(None, None, tensor),
        P(tensor, None),
    )
    out_specs = (
        P(dp, None, tensor, None),
        P(dp, None, tensor, None),
        P(),
        P(None, None, tensor),
        P(None, None, tensor),
        P(None, None, tensor),
        P(tensor),
        P(tensor),
        P(),
        P(tensor, None),
        P(),
        P(None, None, tensor),
        P(tensor, None),
    )
    return jax.shard_map(shards, mesh=fine, in_specs=in_specs, out_specs=out_specs, check_vma=False)
```
